32 devices in a mesh: segment: 8 (over z, y), seq: 4 (over x, core).
Axes of the slice: x: 2, y: 2, z: 4, core: 2. Of those that a mesh axis runs over, the one named last changes fastest.
Arguments:
- queue: bfloat16 [8, 512, 3072], P('segment', 'seq'), may hold values from -4 to 4
- fresh_noise: bfloat16 [512, 3072], P('seq'), may hold values from -6 to 6
- w_mod: bfloat16 [8, 3072, 9216], P('segment', None, 'seq'), may hold values from -0.109375 to 0.109375
- w_qkv: bfloat16 [8, 3072, 4, 384], P('segment', None, 'seq'), may hold values from -0.109375 to 0.109375
- w_out: bfloat16 [8, 512, 3072], P('segment', 'seq'), may hold values from -0.25 to 0.25
- q_gain: float32 [8, 128], P('segment'), may hold values from 1.5 to 7, as said below
- k_gain: float32 [8, 128], P('segment'), may hold values from 1.5 to 7, as said below
- levels: int32 [8], P('segment'), may hold values from 0 to 49
- plan: int32 [50], replicated, may hold values from 0 to 999
- positions: int32 [8], P('segment'), may hold values from 0 to 1023
Outputs:
- queue_next: bfloat16 [8, 512, 3072], P('segment', 'seq')
- clean_frame: bfloat16 [512, 3072], P('seq', 'segment')
The draws below stay inside these ranges and needn't reach their ends.
Inputs may be any that keep to these rules, and one draw needn't show every extreme that they name: `q_gain`: query gains are positive. `k_gain`: key gains are positive.
All inputs are finite; a program needn't handle non-finite values.
Results may differ from the reference program's by a relative error of at most 0.035.
Values may be sent and summed in bfloat16 or wider, within the bound.
A program may use at most 128 MiB of HBM per device.

```python
import jax
import jax.numpy as jnp
from jax import lax

D = 3072
HEAD_DIM = 128
HEAD_DEV = 1
GRID_W = 32
LEVELS = 50
HEADS = 4
TOK_F = 512
FRAMES = 8
N_SEQ = 4


def gain_values(key, lowest, highest):
    return jnp.exp(jax.random.uniform(key, (FRAMES, HEAD_DIM), jnp.float32, jnp.log(lowest), jnp.log(highest)))


def draw_q_gain(key, part):
    key = jax.random.fold_in(key, 11)
    return gain_values(key, 1.5, 3.0)


def draw_k_gain(key, part):
    key = jax.random.fold_in(key, 23)
    return gain_values(key, 1.5, 3.0)


def touch_ends(values, rng, least, largest):
    spot = [jax.random.randint(jax.random.fold_in(rng, axis), (), 0, length) for axis, length in enumerate(values.shape)]
    widest = values.shape.index(max(values.shape))
    neighbour = spot[:widest] + [(spot[widest] + 1) % values.shape[widest]] + spot[widest + 1:]
    return values.at[tuple(spot)].set(least).at[tuple(neighbour)].set(largest)


def block_scale(own_key, dims, pieces, least, largest):
    loudness = 1.0
    for dim, blocks in pieces:
        steps = jax.random.uniform(jax.random.fold_in(jax.random.fold_in(own_key, 6), dim), (blocks,), jnp.float32, least / len(pieces), largest / len(pieces))
        loudness = loudness * jnp.repeat(jnp.exp(steps), dims[dim] // blocks).reshape((-1,) + (1,) * (len(dims) - 1 - dim))
    return loudness


def centred(rng, extent, scale, reach, split=(), held_as=jnp.bfloat16):
    values = scale * jax.random.normal(rng, extent, jnp.float32)
    if split:
        values = values * block_scale(rng, extent, split, -0.22, 0.18)
    return jnp.clip(values, -reach, reach).astype(held_as)


def setup_inputs(seed: int = 0) -> dict:
    arg_keys = jax.random.split(jax.random.key(seed), 11)
    queue = centred(arg_keys[0], (FRAMES, TOK_F, D), 0.5, 4.0, ((0, 8), (1, 4)))
    fresh_noise = centred(arg_keys[1], (TOK_F, D), 1.0, 6.0, ((0, 4),))
    w_mod = centred(arg_keys[2], (FRAMES, D, 3 * D), D ** -0.5, 0.109375, ((0, 8), (2, 4)))
    w_qkv = centred(arg_keys[3], (FRAMES, D, HEADS, 3 * HEAD_DIM), D ** -0.5, 0.109375, ((0, 8), (2, 4)))
    w_out = centred(arg_keys[4], (FRAMES, HEADS * HEAD_DIM, D), (HEADS * HEAD_DIM) ** -0.5, 0.25, ((0, 8), (1, 4)))
    q_gain = draw_q_gain(jax.random.fold_in(arg_keys[10], 71), 0)
    k_gain = draw_k_gain(jax.random.fold_in(arg_keys[10], 71), 0)
    levels = touch_ends(jax.random.randint(arg_keys[7], (FRAMES,), 0, LEVELS), jax.random.fold_in(arg_keys[7], 1), 0, LEVELS - 1).astype(jnp.int32)
    plan = touch_ends(jax.random.randint(arg_keys[8], (LEVELS,), 0, 1000), jax.random.fold_in(arg_keys[8], 1), 0, 999).astype(jnp.int32)
    positions = touch_ends(jax.random.randint(arg_keys[9], (FRAMES,), 0, 1024), jax.random.fold_in(arg_keys[9], 1), 0, 1023).astype(jnp.int32)
    return dict(queue=queue, fresh_noise=fresh_noise, w_mod=w_mod, w_qkv=w_qkv, w_out=w_out, q_gain=q_gain, k_gain=k_gain, levels=levels, plan=plan, positions=positions)


EPSILON = 1e-06
ROPE_BASE = 256.0

def time_embedding(step_values, width):
    half_width = width // 2
    counter = jnp.arange(half_width, dtype=jnp.float32)
    frequency = jnp.exp(-jnp.log(10000.0) * counter / half_width)
    angles = step_values.astype(jnp.float32)[:, None] * frequency[None, :]
    return jnp.concatenate([jnp.cos(angles), jnp.sin(angles)], axis=-1)

def rope_angles(frame_position, row_count, head_dim, grid_width):
    time_dim = head_dim // 8
    space_dim = (head_dim - time_dim) // 2
    tokens_at = jnp.arange(row_count, dtype=jnp.int32)
    grid_row = (tokens_at // grid_width).astype(jnp.float32)
    grid_col = (tokens_at % grid_width).astype(jnp.float32)
    moment = jnp.zeros((row_count,), jnp.float32) + frame_position.astype(jnp.float32)
    sections = []
    for coords, section in ((moment, time_dim), (grid_row, space_dim), (grid_col, space_dim)):
        half_size = section // 2
        frequency = ROPE_BASE ** (-2.0 * jnp.arange(half_size, dtype=jnp.float32) / section)
        angles = coords[:, None] * frequency[None, :]
        sections.append(jnp.concatenate([angles, angles], axis=-1))
    return jnp.concatenate(sections, axis=-1)

def rotate_half(values, head_dim):
    time_dim = head_dim // 8
    space_dim = (head_dim - time_dim) // 2
    pieces_out = []
    position = 0
    for section in (time_dim, space_dim, space_dim):
        half_size = section // 2
        leading = values[..., position:position + half_size]
        second = values[..., position + half_size:position + section]
        pieces_out.append(jnp.concatenate([-second, leading], axis=-1))
        position += section
    return jnp.concatenate(pieces_out, axis=-1)

def apply_rope(values, angles, head_dim):
    return values * jnp.cos(angles) + rotate_half(values, head_dim) * jnp.sin(angles)

def rms_gain(values, gains):
    mean_square = lax.optimization_barrier(jnp.mean(values * values, axis=-1, keepdims=True))
    return values * lax.rsqrt(mean_square + EPSILON) * gains

def layer_norm(values):
    centre = lax.optimization_barrier(jnp.mean(values, axis=-1, keepdims=True))
    spread = lax.optimization_barrier(jnp.mean(jnp.square(values - centre), axis=-1, keepdims=True))
    return (values - centre) * lax.rsqrt(spread + EPSILON)

def attend(query_rows, key_rows, value_rows, usable, head_dim):
    scores = jnp.dot(query_rows, key_rows.T, preferred_element_type=jnp.float32) * head_dim ** (-0.5)
    scores = jnp.where(usable[None, :], scores, -jnp.inf)
    row_max = lax.optimization_barrier(jnp.max(scores, axis=-1, keepdims=True))
    raised = jnp.exp(scores - row_max)
    weights = (raised / lax.optimization_barrier(jnp.sum(raised, axis=-1, keepdims=True))).astype(jnp.bfloat16)
    return jnp.dot(weights, value_rows, preferred_element_type=jnp.float32).astype(jnp.bfloat16)

def reference(queue, fresh_noise, w_mod, w_qkv, w_out, q_gain, k_gain, levels, plan, positions):
    picked = levels[:, None] == jnp.arange(LEVELS, dtype=jnp.int32)[None, :]
    step_values = lax.optimization_barrier(jnp.sum(jnp.where(picked, plan[None, :], 0), axis=1)).astype(jnp.int32)
    embedding = jax.nn.silu(time_embedding(step_values, D)).astype(jnp.bfloat16)

    def modulate_one(inputs):
        emb_row, weight = inputs
        return jnp.dot(emb_row[None, :], weight, preferred_element_type=jnp.float32)[0]
    modulation = lax.map(modulate_one, (embedding, w_mod))

    def project_one(inputs):
        frame, mod_row, weight, gain_q, gain_k, frame_position = inputs
        shift_row = mod_row[:D]
        scale_row = mod_row[D:2 * D]
        normed = layer_norm(frame.astype(jnp.float32))
        modulated = (normed * (1.0 + scale_row) + shift_row).astype(jnp.bfloat16)
        projected_qkv = jnp.dot(modulated, weight.reshape(D, HEADS * 3 * HEAD_DIM), preferred_element_type=jnp.float32)
        projected_qkv = projected_qkv.reshape(TOK_F, HEADS, 3 * HEAD_DIM)
        angles = rope_angles(frame_position, TOK_F, HEAD_DIM, GRID_W)[:, None, :]
        queries = apply_rope(rms_gain(projected_qkv[..., :HEAD_DIM], gain_q), angles, HEAD_DIM).astype(jnp.bfloat16)
        key_rows = apply_rope(rms_gain(projected_qkv[..., HEAD_DIM:2 * HEAD_DIM], gain_k), angles, HEAD_DIM).astype(jnp.bfloat16)
        value_rows = projected_qkv[..., 2 * HEAD_DIM:].astype(jnp.bfloat16)
        return (queries, key_rows, value_rows)
    query_all, key_all, value_all = lax.map(project_one, (queue, modulation, w_qkv, q_gain, k_gain, positions))

    def block_one(frame_at):
        before = jnp.maximum(frame_at - 1, 0)
        after = jnp.minimum(frame_at + 1, FRAMES - 1)
        near_keys = jnp.concatenate([key_all[before], key_all[frame_at], key_all[after]], axis=0)
        near_values = jnp.concatenate([value_all[before], value_all[frame_at], value_all[after]], axis=0)
        filled = jnp.ones((TOK_F,), dtype=bool)
        usable = jnp.concatenate([filled & (frame_at > 0), filled, filled & (frame_at < FRAMES - 1)])
        own_queries = query_all[frame_at]

        def head_one(head_at):
            return attend(own_queries[:, head_at], near_keys[:, head_at], near_values[:, head_at], usable, HEAD_DIM)
        attended = lax.map(head_one, jnp.arange(HEADS, dtype=jnp.int32))
        attended = jnp.transpose(attended, (1, 0, 2)).reshape(TOK_F, N_SEQ, HEAD_DEV * HEAD_DIM)
        grouped_rows = w_out[frame_at].reshape(N_SEQ, HEAD_DEV * HEAD_DIM, D)

        def add_group(running, inputs):
            rows_in, weight = inputs
            partial_value = jnp.dot(rows_in, weight, preferred_element_type=jnp.float32).astype(jnp.bfloat16)
            partial_value = lax.optimization_barrier(partial_value)
            return (running + partial_value.astype(jnp.float32), None)
        projected, _ = lax.scan(add_group, jnp.zeros((TOK_F, D), jnp.float32), (jnp.transpose(attended, (1, 0, 2)), grouped_rows))
        gate_row = modulation[frame_at, 2 * D:]
        return (queue[frame_at].astype(jnp.float32) + gate_row * projected).astype(jnp.bfloat16)
    finished = lax.map(block_one, jnp.arange(FRAMES, dtype=jnp.int32))
    queue_next = jnp.concatenate([fresh_noise[None], finished[:-1]], axis=0)
    return (queue_next, finished[FRAMES - 1])
```

```python
import functools
import math

import jax
import jax.numpy as jnp
from jax import lax
import numpy as np
from jax.experimental import pallas as pl
from jax.experimental.pallas import tpu as pltpu
from jax.sharding import PartitionSpec as P

GRID_W = 32


EPSILON = 1e-06
ROPE_BASE = 256.0


def with_halo(cells, sides, width):
    for axis, dim in sides:
        count = lax.axis_size(axis)
        ends = count - 1
        head = lax.slice_in_dim(cells, 0, width, axis=dim)
        tail = lax.slice_in_dim(cells, cells.shape[dim] - width, cells.shape[dim], axis=dim)
        cells = jnp.concatenate(
            [
                lax.ppermute(tail, axis, [(i, (i + 1) % count) for i in range(ends)]),
                cells,
                lax.ppermute(head, axis, [((i + 1) % count, i) for i in range(ends)]),
            ],
            axis=dim,
        )
    return cells


def passed_along(value, axis, by):
    length = lax.axis_size(axis)
    pairs = [(i, i + by) for i in range(length) if 0 <= i + by < length]
    return lax.ppermute(value, axis, pairs)


def broadcast(value, axis, root):
    mine = lax.axis_index(axis) == root
    return lax.psum(jnp.where(mine, value, jnp.zeros_like(value)), axis)


def time_embedding(step_values, width):
    half_width = width // 2
    counter = jnp.arange(half_width, dtype=jnp.float32)
    frequency = jnp.exp(-jnp.log(10000.0) * counter / half_width)
    angles = step_values.astype(jnp.float32)[:, None] * frequency[None, :]
    return jnp.concatenate([jnp.cos(angles), jnp.sin(angles)], axis=-1)


def rope_angles(frame_position, row_count, head_dim, grid_width):
    time_dim = head_dim // 8
    space_dim = (head_dim - time_dim) // 2
    tokens_at = jnp.arange(row_count, dtype=jnp.int32)
    grid_row = (tokens_at // grid_width).astype(jnp.float32)
    grid_col = (tokens_at % grid_width).astype(jnp.float32)
    moment = jnp.zeros((row_count,), jnp.float32) + frame_position.astype(jnp.float32)
    sections = []
    for coords, section in ((moment, time_dim), (grid_row, space_dim), (grid_col, space_dim)):
        half_size = section // 2
        frequency = ROPE_BASE ** (-2.0 * jnp.arange(half_size, dtype=jnp.float32) / section)
        angles = coords[:, None] * frequency[None, :]
        sections.append(jnp.concatenate([angles, angles], axis=-1))
    return jnp.concatenate(sections, axis=-1)


def rotate_half(values, head_dim):
    time_dim = head_dim // 8
    space_dim = (head_dim - time_dim) // 2
    pieces_out = []
    position = 0
    for section in (time_dim, space_dim, space_dim):
        half_size = section // 2
        leading = values[..., position : position + half_size]
        second = values[..., position + half_size : position + section]
        pieces_out.append(jnp.concatenate([-second, leading], axis=-1))
        position += section
    return jnp.concatenate(pieces_out, axis=-1)


def apply_rope(values, angles, head_dim):
    return values * jnp.cos(angles) + rotate_half(values, head_dim) * jnp.sin(angles)


def rms_gain(values, gains):
    mean_square = jnp.mean(values * values, axis=-1, keepdims=True)
    return values * lax.rsqrt(mean_square + EPSILON) * gains


def layer_norm(values):
    centre = jnp.mean(values, axis=-1, keepdims=True)
    spread = jnp.mean(jnp.square(values - centre), axis=-1, keepdims=True)
    return (values - centre) * lax.rsqrt(spread + EPSILON)


def attend(query_rows, key_rows, value_rows, usable, head_dim):
    scores = jnp.dot(query_rows, key_rows.T, preferred_element_type=jnp.float32) * head_dim ** (
        -0.5
    )
    scores = jnp.where(usable[None, :], scores, -jnp.inf)
    row_max = jnp.max(scores, axis=-1, keepdims=True)
    raised = jnp.exp(scores - row_max)
    weights = (raised / jnp.sum(raised, axis=-1, keepdims=True)).astype(jnp.bfloat16)
    return jnp.dot(weights, value_rows, preferred_element_type=jnp.float32).astype(jnp.bfloat16)


def shards(queue, fresh_noise, w_mod, w_qkv, w_out, q_gain, k_gain, levels, plan, positions):
    segments = lax.axis_size("segment")
    seq_count = lax.axis_size("seq")
    segment_at = lax.axis_index("segment")
    tok_dev = queue.shape[1]
    width = queue.shape[2]
    heads_here = w_qkv.shape[2]
    head_dim = w_qkv.shape[3] // 3
    tok_frame = tok_dev * seq_count
    picked = levels[:, None] == jnp.arange(plan.shape[0], dtype=jnp.int32)[None, :]
    step_values = jnp.sum(jnp.where(picked, plan[None, :], 0), axis=1)
    embedding = jax.nn.silu(time_embedding(step_values, width)).astype(jnp.bfloat16)
    mod_part = jnp.dot(embedding, w_mod[0], preferred_element_type=jnp.float32)
    modulation = lax.all_gather(mod_part, "seq", axis=1, tiled=True)[0]
    shift_row = modulation[:width]
    scale_row = modulation[width : 2 * width]
    gate_row = modulation[2 * width :]
    resident = queue[0].astype(jnp.float32)
    modulated = (layer_norm(resident) * (1.0 + scale_row) + shift_row).astype(jnp.bfloat16)
    flat_weight = w_qkv[0].reshape(width, heads_here * 3 * head_dim)
    projected_qkv = jnp.dot(
        lax.all_gather(modulated, "seq", axis=0, tiled=True),
        flat_weight,
        preferred_element_type=jnp.float32,
    )
    projected_qkv = projected_qkv.reshape(tok_frame, heads_here, 3 * head_dim)
    angles = rope_angles(positions[0], tok_frame, head_dim, GRID_W)[:, None, :]
    queries = apply_rope(
        rms_gain(projected_qkv[..., :head_dim], q_gain[0]), angles, head_dim
    ).astype(jnp.bfloat16)
    key_rows = apply_rope(
        rms_gain(projected_qkv[..., head_dim : 2 * head_dim], k_gain[0]), angles, head_dim
    ).astype(jnp.bfloat16)
    value_rows = projected_qkv[..., 2 * head_dim :].astype(jnp.bfloat16)
    stacked = jnp.stack([key_rows, value_rows])[None]
    beside_all = with_halo(stacked, (("segment", 0),), 1)
    earlier = beside_all[0]
    following = beside_all[2]
    near_keys = jnp.concatenate([earlier[0], key_rows, following[0]], axis=0)
    near_values = jnp.concatenate([earlier[1], value_rows, following[1]], axis=0)
    filled = jnp.ones((tok_frame,), dtype=bool)
    usable = jnp.concatenate(
        [filled & (segment_at > 0), filled, filled & (segment_at < segments - 1)]
    )
    block_rows = math.gcd(tok_frame, 512)
    block_count = tok_frame // block_rows
    head_keys = near_keys[:, 0]
    head_values = near_values[:, 0]
    query_blocks = queries[:, 0].reshape(block_count, block_rows, head_dim)

    def one_block(query_rows, head_keys=head_keys, head_values=head_values):
        return attend(query_rows, head_keys, head_values, usable, head_dim)

    outputs = [lax.map(one_block, query_blocks).reshape(tok_frame, head_dim)]
    attended = jnp.stack(outputs, axis=1).reshape(tok_frame, heads_here * head_dim)
    projected = lax.psum_scatter(
        jnp.dot(attended, w_out[0], preferred_element_type=jnp.float32).astype(jnp.bfloat16),
        "seq",
        scatter_dimension=0,
        tiled=True,
    ).astype(jnp.float32)
    finished = (resident + gate_row * projected).astype(jnp.bfloat16)
    arrived = passed_along(finished, "segment", 1)
    queue_next = jnp.where(segment_at == 0, fresh_noise, arrived)[None]
    clean_whole = broadcast(finished, "segment", segments - 1)
    column_count = width // segments
    clean_frame = lax.dynamic_slice_in_dim(clean_whole, segment_at * column_count, column_count, 1)
    return (queue_next, clean_frame)


MESH = pl.DeviceIdType.MESH
PEERS = 4
MOD_CHUNKS = 6
X_CHUNKS = 4
OUT_CHUNKS = 4
LANES = 128


def fits(mesh):
    return mesh.shape["seq"] == PEERS


def rope_rows(head_dim):
    time_dim = head_dim // 8
    space_dim = (head_dim - time_dim) // 2
    rows = np.zeros((8, head_dim), np.float32)
    start = 0
    for at, section in enumerate((time_dim, space_dim, space_dim)):
        half = section // 2
        frequency = ROPE_BASE ** (-2.0 * np.arange(half) / section)
        rows[at, start : start + half] = frequency
        rows[at, start + half : start + section] = frequency
        back, forth = (3, 4) if at == 0 else (5, 6)
        rows[back, start + half : start + section] = 1.0
        rows[forth, start : start + half] = -1.0
        start += section
    return rows, time_dim // 2, space_dim // 2


def time_rates(width):
    half_width = width // 2
    return np.exp(-np.log(10000.0) * np.arange(half_width) / half_width).astype(np.float32)[None]


def block_kernel(
    segments,
    halves,
    queue,
    fresh,
    w_mod,
    w_qkv,
    w_out,
    q_gain,
    k_gain,
    levels,
    plan,
    positions,
    rates,
    rope,
    queue_next,
    clean,
    mod_w,
    qkv_w,
    out_w,
    tokens,
    mod_all,
    mod_rows,
    normed,
    cosines,
    sines,
    queries,
    kv,
    own_att,
    att,
    done,
    local_sem,
    x_send,
    x_recv,
    m_send,
    m_recv,
    h_send,
    h_recv,
    w_send,
    w_recv,
    a_send,
    a_recv,
    s_send,
    s_recv,
    c_send,
    c_recv,
):
    f = lax.axis_index("segment")
    q = lax.axis_index("seq")
    last = segments - 1
    rows, width = queue.shape
    head_dim = q_gain.shape[1]
    mod_cols = w_mod.shape[1]
    peers = (q, q + 1 - 2 * lax.rem(q, 2), lax.rem(q + 2, 4), 3 - q)

    def remote(source, target, send, recv, device):
        return pltpu.make_async_remote_copy(
            src_ref=source,
            dst_ref=target,
            send_sem=send,
            recv_sem=recv,
            device_id=device,
            device_id_type=MESH,
        )

    own_tokens = pltpu.make_async_copy(queue, tokens.at[0], local_sem.at[0])
    own_tokens.start()
    mod_depth = width // MOD_CHUNKS
    mod_loads = []
    for i in range(MOD_CHUNKS):
        part = pl.ds(i * mod_depth, mod_depth)
        load = pltpu.make_async_copy(w_mod.at[part], mod_w.at[part], local_sem.at[1 + i])
        load.start()
        mod_loads.append(load)
    qkv_load = pltpu.make_async_copy(w_qkv, qkv_w, local_sem.at[1 + MOD_CHUNKS])
    qkv_load.start()
    out_load = pltpu.make_async_copy(w_out, out_w.at[0], local_sem.at[2 + MOD_CHUNKS])
    out_load.start()

    barrier = pltpu.get_barrier_semaphore()
    for rel in range(1, PEERS):
        pl.semaphore_signal(barrier, inc=1, device_id=(f, peers[rel]), device_id_type=MESH)
    for step in range(1, segments):
        pl.semaphore_signal(
            barrier, inc=1, device_id=(lax.rem(f + step, segments), q), device_id_type=MESH
        )
    pl.semaphore_wait(barrier, PEERS - 1 + segments - 1)

    piece = rows // X_CHUNKS
    mirror_x = []
    for i in range(X_CHUNKS):
        part = pl.ds(i * piece, piece)
        copy = remote(
            queue.at[part], tokens.at[2, part], x_send.at[i], x_recv.at[i], (f, peers[2])
        )
        copy.start()
        mirror_x.append(copy)
    sibling_x = remote(
        queue, tokens.at[1], x_send.at[X_CHUNKS], x_recv.at[X_CHUNKS], (f, peers[1])
    )
    sibling_x.start()
    fresh_copy = pltpu.make_async_copy(fresh, queue_next, local_sem.at[3 + MOD_CHUNKS])

    @pl.when(f == 0)
    def _():
        fresh_copy.start()

    step_value = plan[levels[0]].astype(jnp.float32)
    angles = rates[...] * step_value
    embedding = jnp.concatenate([jnp.cos(angles), jnp.sin(angles)], axis=1)
    embedding = embedding / (1.0 + jnp.exp(-embedding))
    embedding = jnp.broadcast_to(embedding, (16, width)).astype(jnp.bfloat16)
    total = jnp.zeros((16, mod_cols), jnp.float32)
    for i in range(MOD_CHUNKS):
        mod_loads[i].wait()
        total = total + jnp.dot(
            embedding[:, i * mod_depth : (i + 1) * mod_depth],
            mod_w[i * mod_depth : (i + 1) * mod_depth, :],
            preferred_element_type=jnp.float32,
        )
    mod_all[q] = total[:1]
    mod_copies = []
    for rel in range(1, PEERS):
        copy = remote(
            mod_all.at[q], mod_all.at[q], m_send.at[rel], m_recv.at[rel], (f, peers[rel])
        )
        copy.start()
        mod_copies.append(copy)

    position = positions[0].astype(jnp.float32)
    for rel in range(PEERS):
        spot = lax.broadcasted_iota(jnp.int32, (rows, head_dim), 0) + peers[rel] * rows
        grid_row = (spot // GRID_W).astype(jnp.float32)
        grid_col = (spot % GRID_W).astype(jnp.float32)
        turn = position * rope[0:1] + grid_row * rope[1:2] + grid_col * rope[2:3]
        cosines[rel] = jnp.cos(turn)
        sines[rel] = jnp.sin(turn)

    @pl.when(f == 0)
    def _():
        kv[0] = jnp.zeros_like(kv[0])

    @pl.when(f == last)
    def _():
        kv[2] = jnp.zeros_like(kv[2])

    own_tokens.wait()
    qkv_load.wait()
    out_load.wait()
    for copy in mod_copies:
        copy.wait()
    for peer in range(PEERS):
        mod_rows[:, peer * mod_cols : (peer + 1) * mod_cols] = mod_all[peer]

    halo = []

    def project(pieces, task):
        count = len(pieces)
        at = 0
        for rel, start, size in pieces:

            def norm_rows(i, carry, rel=rel, start=start, at=at):
                offset = pl.multiple_of(i * 16, 16)
                x = tokens[rel, pl.ds(start + offset, 16), :].astype(jnp.float32)
                x = x - jnp.mean(x, axis=1, keepdims=True)
                spread = jnp.mean(x * x, axis=1, keepdims=True)
                x = x * lax.rsqrt(spread + EPSILON)
                x = x * (1.0 + mod_rows[:, width : 2 * width]) + mod_rows[:, :width]
                normed[pl.ds(at + offset, 16), :] = x.astype(jnp.bfloat16)
                return carry

            lax.fori_loop(0, size // 16, norm_rows, 0)
            at += size
        joined = jnp.dot(normed[:at, :], qkv_w[...], preferred_element_type=jnp.float32)
        at = 0
        for rel, start, size in pieces:
            cos = cosines[rel, start : start + size, :]
            sin = sines[rel, start : start + size, :]

            def turned(x, gain):
                x = x * lax.rsqrt(jnp.mean(x * x, axis=1, keepdims=True) + EPSILON) * gain
                swapped = (
                    pltpu.roll(x, halves[0], 1) * rope[3:4]
                    + pltpu.roll(x, head_dim - halves[0], 1) * rope[4:5]
                    + pltpu.roll(x, halves[1], 1) * rope[5:6]
                    + pltpu.roll(x, head_dim - halves[1], 1) * rope[6:7]
                )
                return (x * cos + swapped * sin).astype(jnp.bfloat16)

            own = joined[at : at + size]
            queries[rel, start : start + size, :] = turned(own[:, :head_dim], q_gain[...])
            kv[1, 0, rel, start : start + size, :] = turned(
                own[:, head_dim : 2 * head_dim], k_gain[...]
            )
            kv[1, 1, rel, start : start + size, :] = own[:, 2 * head_dim :].astype(jnp.bfloat16)
            at += size
        rels = pl.ds(pieces[0][0], count)
        part = pl.ds(pieces[0][1], pieces[0][2])
        forth = remote(
            kv.at[1, :, rels, part],
            kv.at[0, :, rels, part],
            h_send.at[0, task],
            h_recv.at[0, task],
            (lax.rem(f + 1, segments), q),
        )
        back = remote(
            kv.at[1, :, rels, part],
            kv.at[2, :, rels, part],
            h_send.at[1, task],
            h_recv.at[1, task],
            (lax.rem(f + segments - 1, segments), q),
        )

        @pl.when(f < last)
        def _():
            forth.start()

        @pl.when(f > 0)
        def _():
            back.start()

        halo.append((forth, back))

    forwards = []

    def forward_tokens(i):
        mirror_x[i].wait_recv()
        part = pl.ds(i * piece, piece)
        copy = remote(
            tokens.at[2, part],
            tokens.at[3, part],
            x_send.at[X_CHUNKS + 1 + i],
            x_recv.at[X_CHUNKS + 1 + i],
            (f, peers[1]),
        )
        copy.start()
        forwards.append(copy)

    sibling_x.wait_recv()
    project([(0, 0, rows), (1, 0, rows)], 0)
    half = rows // 2
    for i in range(X_CHUNKS // 2):
        forward_tokens(i)
    for i in range(X_CHUNKS // 2):
        forwards[i].wait_recv()
    project([(2, 0, half), (3, 0, half)], 1)
    for i in range(X_CHUNKS // 2, X_CHUNKS):
        forward_tokens(i)

    cols = width // OUT_CHUNKS
    mirror_w = []
    for i in range(OUT_CHUNKS):
        part = pl.ds(i * cols, cols)
        copy = remote(
            out_w.at[0, :, part],
            out_w.at[2, :, part],
            w_send.at[i],
            w_recv.at[i],
            (f, peers[2]),
        )
        copy.start()
        mirror_w.append(copy)
    sibling_w = remote(
        out_w.at[0], out_w.at[1], w_send.at[OUT_CHUNKS], w_recv.at[OUT_CHUNKS], (f, peers[1])
    )
    for i in range(X_CHUNKS // 2, X_CHUNKS):
        forwards[i].wait_recv()
    project([(2, half, half), (3, half, half)], 2)
    sibling_w.start()

    for forth, back in halo:

        @pl.when(f > 0)
        def _(forth=forth):
            forth.wait_recv()

        @pl.when(f < last)
        def _(back=back):
            back.wait_recv()

    scale = head_dim ** (-0.5)
    tokens_all = PEERS * rows
    att_copies = []
    for rel in (3, 2, 1, 0):
        query_rows = queries[rel]
        scores = []
        for side in range(3):
            key_rows = kv[side, 0].reshape(tokens_all, head_dim)
            part = (
                lax.dot_general(
                    query_rows,
                    key_rows,
                    (((1,), (1,)), ((), ())),
                    preferred_element_type=jnp.float32,
                )
                * scale
            )
            if side == 0:
                part = jnp.where(f > 0, part, -jnp.inf)
            if side == 2:
                part = jnp.where(f < last, part, -jnp.inf)
            scores.append(part)
        top = jnp.maximum(
            jnp.max(jnp.maximum(scores[0], scores[2]), axis=1, keepdims=True),
            jnp.max(scores[1], axis=1, keepdims=True),
        )
        weight = jnp.zeros((rows, 1), jnp.float32)
        mixed = jnp.zeros((rows, head_dim), jnp.float32)
        for side in range(3):
            raised = jnp.exp(scores[side] - top)
            weight = weight + jnp.sum(raised, axis=1, keepdims=True)
            mixed = mixed + jnp.dot(
                raised.astype(jnp.bfloat16),
                kv[side, 1].reshape(tokens_all, head_dim),
                preferred_element_type=jnp.float32,
            )
        mixed = (mixed / weight).astype(jnp.bfloat16)
        if rel == 0:
            att[0] = mixed
        else:
            own_att[rel] = mixed
            copy = remote(
                own_att.at[rel], att.at[rel], a_send.at[rel], a_recv.at[rel], (f, peers[rel])
            )
            copy.start()
            att_copies.append(copy)

    forward_w = []

    def forward_weights(i):
        mirror_w[i].wait_recv()
        part = pl.ds(i * cols, cols)
        copy = remote(
            out_w.at[2, :, part],
            out_w.at[3, :, part],
            w_send.at[OUT_CHUNKS + 1 + i],
            w_recv.at[OUT_CHUNKS + 1 + i],
            (f, peers[1]),
        )
        copy.start()
        forward_w.append(copy)

    forward_weights(0)
    sibling_w.wait_recv()
    for copy in att_copies:
        copy.wait_recv()
    mixed = jnp.concatenate([att[rel] for rel in range(PEERS)], axis=1)

    clean_cols = width // segments
    shifts = []
    cleans = []
    for i in range(OUT_CHUNKS):
        if i + 1 < OUT_CHUNKS:
            forward_weights(i + 1)
        forward_w[i].wait_recv()
        begin = i * cols
        part = pl.ds(begin, cols)
        projected = jnp.dot(
            mixed,
            out_w[:, :, begin : begin + cols].reshape(PEERS * rows, cols),
            preferred_element_type=jnp.float32,
        )
        gate = mod_rows[:, 2 * width + begin : 2 * width + begin + cols]
        kept = tokens[0, :, begin : begin + cols].astype(jnp.float32)
        done[:, begin : begin + cols] = (kept + gate * projected).astype(jnp.bfloat16)
        shift = remote(
            done.at[:, part],
            queue_next.at[:, part],
            s_send.at[i],
            s_recv.at[i],
            (lax.rem(f + 1, segments), q),
        )
        shifts.append(shift)

        @pl.when(f < last)
        def _(shift=shift):
            shift.start()

        for to in range(begin // clean_cols, (begin + cols) // clean_cols):
            from_cols = done.at[:, pl.ds(to * clean_cols, clean_cols)]
            if to < last:
                clean_copy = remote(from_cols, clean, c_send.at[to], c_recv, (to, q))
            else:
                clean_copy = pltpu.make_async_copy(from_cols, clean, c_send.at[to])
            cleans.append(clean_copy)

            @pl.when(f == last)
            def _(clean_copy=clean_copy):
                clean_copy.start()

    for copy in mirror_x + [sibling_x] + forwards + mirror_w + [sibling_w] + forward_w + att_copies:
        copy.wait_send()
    for forth, back in halo:

        @pl.when(f < last)
        def _(forth=forth):
            forth.wait_send()

        @pl.when(f > 0)
        def _(back=back):
            back.wait_send()

    @pl.when(f == 0)
    def _():
        fresh_copy.wait()

    for shift in shifts:

        @pl.when(f < last)
        def _(shift=shift):
            shift.wait_send()

        @pl.when(f > 0)
        def _(shift=shift):
            shift.wait_recv()

    @pl.when(f == last)
    def _():
        for clean_copy in cleans[:-1]:
            clean_copy.wait_send()
        cleans[-1].wait()

    @pl.when(f < last)
    def _():
        cleans[0].wait_recv()


def fused(
    mesh, queue, fresh_noise, w_mod, w_qkv, w_out, q_gain, k_gain, levels, plan, positions
):
    segments = mesh.shape["segment"]
    rows, width = queue.shape[1:]
    mod_cols = w_mod.shape[2]
    head_dim = q_gain.shape[1]
    rope, *halves = rope_rows(head_dim)
    whole = pl.BlockSpec(memory_space=pltpu.VMEM)
    scalars = pl.BlockSpec(memory_space=pltpu.SMEM)
    outside = pl.BlockSpec(memory_space=pl.ANY)
    bf16, f32 = jnp.bfloat16, jnp.float32
    dma = pltpu.SemaphoreType.DMA
    queue_next, clean_frame = pl.pallas_call(
        functools.partial(block_kernel, segments, tuple(halves)),
        out_shape=(
            jax.ShapeDtypeStruct((rows, width), bf16),
            jax.ShapeDtypeStruct((rows, width // segments), bf16),
        ),
        in_specs=[outside] * 5 + [whole] * 2 + [scalars] * 3 + [whole] * 2,
        out_specs=(outside, outside),
        scratch_shapes=[
            pltpu.VMEM((width, mod_cols), bf16),
            pltpu.VMEM((width, 3 * head_dim), bf16),
            pltpu.VMEM((PEERS, rows, width), bf16),
            pltpu.VMEM((PEERS, rows, width), bf16),
            pltpu.VMEM((PEERS, 1, mod_cols), f32),
            pltpu.VMEM((1, 3 * width), f32),
            pltpu.VMEM((2 * rows, width), bf16),
            pltpu.VMEM((PEERS, rows, head_dim), f32),
            pltpu.VMEM((PEERS, rows, head_dim), f32),
            pltpu.VMEM((PEERS, rows, head_dim), bf16),
            pltpu.VMEM((3, 2, PEERS, rows, head_dim), bf16),
            pltpu.VMEM((PEERS, rows, head_dim), bf16),
            pltpu.VMEM((PEERS, rows, head_dim), bf16),
            pltpu.VMEM((rows, width), bf16),
            dma((4 + MOD_CHUNKS,)),
            dma((2 * X_CHUNKS + 1,)),
            dma((2 * X_CHUNKS + 1,)),
            dma((PEERS,)),
            dma((PEERS,)),
            dma((2, 3)),
            dma((2, 3)),
            dma((2 * OUT_CHUNKS + 1,)),
            dma((2 * OUT_CHUNKS + 1,)),
            dma((PEERS,)),
            dma((PEERS,)),
            dma((OUT_CHUNKS,)),
            dma((OUT_CHUNKS,)),
            dma((segments,)),
            dma(()),
        ],
        compiler_params=pltpu.CompilerParams(
            collective_id=0, has_side_effects=True, vmem_limit_bytes=56 * 1024 * 1024
        ),
        cost_estimate=pl.CostEstimate(
            flops=2 * 10**9, bytes_accessed=22 * 10**6, transcendentals=10**6
        ),
        name="relayed_block",
    )(
        queue[0],
        fresh_noise,
        w_mod[0],
        w_qkv.reshape(width, 3 * head_dim),
        w_out[0],
        q_gain,
        k_gain,
        levels,
        plan,
        positions,
        jnp.asarray(time_rates(width)),
        jnp.asarray(rope),
    )
    return queue_next[None], clean_frame


def solution(mesh):
    placed = (
        P("segment", "seq", None),
        P("seq", None),
        P("segment", None, "seq"),
        P("segment", None, "seq", None),
        P("segment", "seq", None),
        P("segment", None),
        P("segment", None),
        P("segment"),
        P(),
        P("segment"),
    )
    return jax.shard_map(
        functools.partial(fused, mesh) if fits(mesh) else shards,
        mesh=mesh,
        in_specs=placed,
        out_specs=(P("segment", "seq", None), P("seq", "segment")),
        check_vma=False,
    )
```

```python
import functools
import math

import jax
import jax.numpy as jnp
from jax import lax
import numpy as np
from jax.experimental import pallas as pl
from jax.experimental.pallas import tpu as pltpu
from jax.sharding import PartitionSpec as P

GRID_W = 32


EPSILON = 1e-06
ROPE_BASE = 256.0


def with_halo(cells, sides, width):
    for axis, dim in sides:
        count = lax.axis_size(axis)
        ends = count - 1
        head = lax.slice_in_dim(cells, 0, width, axis=dim)
        tail = lax.slice_in_dim(cells, cells.shape[dim] - width, cells.shape[dim], axis=dim)
        cells = jnp.concatenate(
            [
                lax.ppermute(tail, axis, [(i, (i + 1) % count) for i in range(ends)]),
                cells,
                lax.ppermute(head, axis, [((i + 1) % count, i) for i in range(ends)]),
            ],
            axis=dim,
        )
    return cells


def passed_along(value, axis, by):
    length = lax.axis_size(axis)
    pairs = [(i, i + by) for i in range(length) if 0 <= i + by < length]
    return lax.ppermute(value, axis, pairs)


def broadcast(value, axis, root):
    mine = lax.axis_index(axis) == root
    return lax.psum(jnp.where(mine, value, jnp.zeros_like(value)), axis)


def time_embedding(step_values, width):
    half_width = width // 2
    counter = jnp.arange(half_width, dtype=jnp.float32)
    frequency = jnp.exp(-jnp.log(10000.0) * counter / half_width)
    angles = step_values.astype(jnp.float32)[:, None] * frequency[None, :]
    return jnp.concatenate([jnp.cos(angles), jnp.sin(angles)], axis=-1)


def rope_angles(frame_position, row_count, head_dim, grid_width):
    time_dim = head_dim // 8
    space_dim = (head_dim - time_dim) // 2
    tokens_at = jnp.arange(row_count, dtype=jnp.int32)
    grid_row = (tokens_at // grid_width).astype(jnp.float32)
    grid_col = (tokens_at % grid_width).astype(jnp.float32)
    moment = jnp.zeros((row_count,), jnp.float32) + frame_position.astype(jnp.float32)
    sections = []
    for coords, section in ((moment, time_dim), (grid_row, space_dim), (grid_col, space_dim)):
        half_size = section // 2
        frequency = ROPE_BASE ** (-2.0 * jnp.arange(half_size, dtype=jnp.float32) / section)
        angles = coords[:, None] * frequency[None, :]
        sections.append(jnp.concatenate([angles, angles], axis=-1))
    return jnp.concatenate(sections, axis=-1)


def rotate_half(values, head_dim):
    time_dim = head_dim // 8
    space_dim = (head_dim - time_dim) // 2
    pieces_out = []
    position = 0
    for section in (time_dim, space_dim, space_dim):
        half_size = section // 2
        leading = values[..., position : position + half_size]
        second = values[..., position + half_size : position + section]
        pieces_out.append(jnp.concatenate([-second, leading], axis=-1))
        position += section
    return jnp.concatenate(pieces_out, axis=-1)


def apply_rope(values, angles, head_dim):
    return values * jnp.cos(angles) + rotate_half(values, head_dim) * jnp.sin(angles)


def rms_gain(values, gains):
    mean_square = jnp.mean(values * values, axis=-1, keepdims=True)
    return values * lax.rsqrt(mean_square + EPSILON) * gains


def layer_norm(values):
    centre = jnp.mean(values, axis=-1, keepdims=True)
    spread = jnp.mean(jnp.square(values - centre), axis=-1, keepdims=True)
    return (values - centre) * lax.rsqrt(spread + EPSILON)


def attend(query_rows, key_rows, value_rows, usable, head_dim):
    scores = jnp.dot(query_rows, key_rows.T, preferred_element_type=jnp.float32) * head_dim ** (
        -0.5
    )
    scores = jnp.where(usable[None, :], scores, -jnp.inf)
    row_max = jnp.max(scores, axis=-1, keepdims=True)
    raised = jnp.exp(scores - row_max)
    weights = (raised / jnp.sum(raised, axis=-1, keepdims=True)).astype(jnp.bfloat16)
    return jnp.dot(weights, value_rows, preferred_element_type=jnp.float32).astype(jnp.bfloat16)


def shards(queue, fresh_noise, w_mod, w_qkv, w_out, q_gain, k_gain, levels, plan, positions):
    segments = lax.axis_size("segment")
    seq_count = lax.axis_size("seq")
    segment_at = lax.axis_index("segment")
    tok_dev = queue.shape[1]
    width = queue.shape[2]
    heads_here = w_qkv.shape[2]
    head_dim = w_qkv.shape[3] // 3
    tok_frame = tok_dev * seq_count
    picked = levels[:, None] == jnp.arange(plan.shape[0], dtype=jnp.int32)[None, :]
    step_values = jnp.sum(jnp.where(picked, plan[None, :], 0), axis=1)
    embedding = jax.nn.silu(time_embedding(step_values, width)).astype(jnp.bfloat16)
    mod_part = jnp.dot(embedding, w_mod[0], preferred_element_type=jnp.float32)
    modulation = lax.all_gather(mod_part, "seq", axis=1, tiled=True)[0]
    shift_row = modulation[:width]
    scale_row = modulation[width : 2 * width]
    gate_row = modulation[2 * width :]
    resident = queue[0].astype(jnp.float32)
    modulated = (layer_norm(resident) * (1.0 + scale_row) + shift_row).astype(jnp.bfloat16)
    flat_weight = w_qkv[0].reshape(width, heads_here * 3 * head_dim)
    projected_qkv = jnp.dot(
        lax.all_gather(modulated, "seq", axis=0, tiled=True),
        flat_weight,
        preferred_element_type=jnp.float32,
    )
    projected_qkv = projected_qkv.reshape(tok_frame, heads_here, 3 * head_dim)
    angles = rope_angles(positions[0], tok_frame, head_dim, GRID_W)[:, None, :]
    queries = apply_rope(
        rms_gain(projected_qkv[..., :head_dim], q_gain[0]), angles, head_dim
    ).astype(jnp.bfloat16)
    key_rows = apply_rope(
        rms_gain(projected_qkv[..., head_dim : 2 * head_dim], k_gain[0]), angles, head_dim
    ).astype(jnp.bfloat16)
    value_rows = projected_qkv[..., 2 * head_dim :].astype(jnp.bfloat16)
    stacked = jnp.stack([key_rows, value_rows])[None]
    beside_all = with_halo(stacked, (("segment", 0),), 1)
    earlier = beside_all[0]
    following = beside_all[2]
    near_keys = jnp.concatenate([earlier[0], key_rows, following[0]], axis=0)
    near_values = jnp.concatenate([earlier[1], value_rows, following[1]], axis=0)
    filled = jnp.ones((tok_frame,), dtype=bool)
    usable = jnp.concatenate(
        [filled & (segment_at > 0), filled, filled & (segment_at < segments - 1)]
    )
    block_rows = math.gcd(tok_frame, 512)
    block_count = tok_frame // block_rows
    head_keys = near_keys[:, 0]
    head_values = near_values[:, 0]
    query_blocks = queries[:, 0].reshape(block_count, block_rows, head_dim)

    def one_block(query_rows, head_keys=head_keys, head_values=head_values):
        return attend(query_rows, head_keys, head_values, usable, head_dim)

    outputs = [lax.map(one_block, query_blocks).reshape(tok_frame, head_dim)]
    attended = jnp.stack(outputs, axis=1).reshape(tok_frame, heads_here * head_dim)
    projected = lax.psum_scatter(
        jnp.dot(attended, w_out[0], preferred_element_type=jnp.float32).astype(jnp.bfloat16),
        "seq",
        scatter_dimension=0,
        tiled=True,
    ).astype(jnp.float32)
    finished = (resident + gate_row * projected).astype(jnp.bfloat16)
    arrived = passed_along(finished, "segment", 1)
    queue_next = jnp.where(segment_at == 0, fresh_noise, arrived)[None]
    clean_whole = broadcast(finished, "segment", segments - 1)
    column_count = width // segments
    clean_frame = lax.dynamic_slice_in_dim(clean_whole, segment_at * column_count, column_count, 1)
    return (queue_next, clean_frame)


MESH = pl.DeviceIdType.MESH
PEERS = 4
MOD_CHUNKS = 6
X_CHUNKS = 4
OUT_CHUNKS = 4
LANES = 128


def fits(mesh):
    return mesh.shape["seq"] == PEERS


def rope_rows(head_dim):
    time_dim = head_dim // 8
    space_dim = (head_dim - time_dim) // 2
    rows = np.zeros((8, head_dim), np.float32)
    start = 0
    for at, section in enumerate((time_dim, space_dim, space_dim)):
        half = section // 2
        frequency = ROPE_BASE ** (-2.0 * np.arange(half) / section)
        rows[at, start : start + half] = frequency
        rows[at, start + half : start + section] = frequency
        back, forth = (3, 4) if at == 0 else (5, 6)
        rows[back, start + half : start + section] = 1.0
        rows[forth, start : start + half] = -1.0
        start += section
    return rows, time_dim // 2, space_dim // 2


def time_rates(width):
    half_width = width // 2
    return np.exp(-np.log(10000.0) * np.arange(half_width) / half_width).astype(np.float32)[None]


def block_kernel(
    segments,
    halves,
    queue,
    fresh,
    w_mod,
    w_qkv,
    w_out,
    q_gain_in,
    k_gain_in,
    levels,
    plan,
    positions,
    rates_in,
    rope_in,
    queue_next,
    clean,
    mod_w,
    qkv_w,
    out_w,
    tokens,
    mod_all,
    mod_rows,
    rates,
    rope,
    q_gain,
    k_gain,
    embedded,
    settled,
    normed,
    cosines,
    sines,
    queries,
    kv,
    own_att,
    att,
    done,
    small_sem,
    local_sem,
    x_send,
    x_recv,
    m_send,
    m_recv,
    h_send,
    h_recv,
    w_send,
    w_recv,
    a_send,
    a_recv,
    s_send,
    s_recv,
    c_send,
    c_recv,
):
    f = lax.axis_index("segment")
    q = lax.axis_index("seq")
    last = segments - 1
    rows, width = queue.shape
    head_dim = q_gain_in.shape[1]
    mod_cols = w_mod.shape[1]
    peers = (q, q + 1 - 2 * lax.rem(q, 2), lax.rem(q + 2, 4), 3 - q)

    def remote(source, target, send, recv, device):
        return pltpu.make_async_remote_copy(
            src_ref=source,
            dst_ref=target,
            send_sem=send,
            recv_sem=recv,
            device_id=device,
            device_id_type=MESH,
        )

    barrier = pltpu.get_barrier_semaphore()
    for rel in range(1, PEERS):
        pl.semaphore_signal(barrier, inc=1, device_id=(f, peers[rel]), device_id_type=MESH)
    for step in range(1, segments):
        pl.semaphore_signal(
            barrier, inc=1, device_id=(lax.rem(f + step, segments), q), device_id_type=MESH
        )

    small_loads = []
    for i, (source, target) in enumerate(
        ((rates_in, rates), (rope_in, rope), (q_gain_in, q_gain), (k_gain_in, k_gain))
    ):
        load = pltpu.make_async_copy(source, target, small_sem.at[i])
        load.start()
        small_loads.append(load)
    own_tokens = pltpu.make_async_copy(queue, tokens.at[0], local_sem.at[0])
    own_tokens.start()
    mod_depth = width // MOD_CHUNKS
    mod_loads = []
    for i in range(MOD_CHUNKS):
        part = pl.ds(i * mod_depth, mod_depth)
        load = pltpu.make_async_copy(w_mod.at[part], mod_w.at[part], local_sem.at[1 + i])
        load.start()
        mod_loads.append(load)
    qkv_load = pltpu.make_async_copy(w_qkv, qkv_w, local_sem.at[1 + MOD_CHUNKS])
    qkv_load.start()
    out_load = pltpu.make_async_copy(w_out, out_w.at[0], local_sem.at[2 + MOD_CHUNKS])
    out_load.start()

    pl.semaphore_wait(barrier, PEERS - 1 + segments - 1)

    piece = rows // X_CHUNKS
    mirror_x = []
    for i in range(X_CHUNKS):
        part = pl.ds(i * piece, piece)
        copy = remote(
            queue.at[part], tokens.at[2, part], x_send.at[i], x_recv.at[i], (f, peers[2])
        )
        copy.start()
        mirror_x.append(copy)
    sibling_x = remote(
        queue, tokens.at[1], x_send.at[X_CHUNKS], x_recv.at[X_CHUNKS], (f, peers[1])
    )
    sibling_x.start()
    fresh_copy = pltpu.make_async_copy(fresh, queue_next, local_sem.at[3 + MOD_CHUNKS])

    @pl.when(f == 0)
    def _():
        fresh_copy.start()

    for load in small_loads:
        load.wait()
    step_value = plan[levels[0]].astype(jnp.float32)
    angles = rates[...] * step_value
    embedding = jnp.concatenate([jnp.cos(angles), jnp.sin(angles)], axis=1)
    embedding = embedding / (1.0 + jnp.exp(-embedding))
    embedding = embedding.astype(jnp.bfloat16).astype(jnp.float32)
    for start in range(0, width, LANES):
        entries = jnp.broadcast_to(embedding[:, start : start + LANES], (LANES, LANES))
        embedded[start : start + LANES, :] = entries.T
    tiles = mod_cols // LANES

    def add_rows(i, totals):
        offset = pl.multiple_of(i * 16, 16)
        entries = embedded[pl.ds(offset, 16), :]
        sums = []
        for tile in range(tiles):
            lanes = slice(tile * LANES, (tile + 1) * LANES)
            product = mod_w[pl.ds(offset, 16), lanes].astype(jnp.float32) * entries
            sums.append(totals[tile] + (product[:8] + product[8:]))
        return tuple(sums)

    totals = tuple(jnp.zeros((8, LANES), jnp.float32) for _ in range(tiles))
    steps = mod_depth // 16
    for i in range(MOD_CHUNKS):
        mod_loads[i].wait()
        totals = lax.fori_loop(i * steps, (i + 1) * steps, add_rows, totals, unroll=4)
    mod_all[q] = jnp.concatenate(
        [jnp.sum(total, axis=0, keepdims=True) for total in totals], axis=1
    )
    mod_copies = []
    for rel in range(1, PEERS):
        copy = remote(
            mod_all.at[q], mod_all.at[q], m_send.at[rel], m_recv.at[rel], (f, peers[rel])
        )
        copy.start()
        mod_copies.append(copy)

    position = positions[0].astype(jnp.float32)
    grid_col = lax.broadcasted_iota(jnp.int32, (GRID_W, head_dim), 0).astype(jnp.float32)
    col_turn = grid_col * rope[2:3]
    col_cos = jnp.cos(col_turn)
    col_sin = jnp.sin(col_turn)
    by_col = lax.broadcasted_iota(jnp.int32, (GRID_W, head_dim), 1) >= head_dim - 2 * halves[1]
    rows_here = rows // GRID_W
    for rel in range(PEERS):
        grid_row = lax.broadcasted_iota(jnp.int32, (8, head_dim), 0) + peers[rel] * rows_here
        row_turn = position * rope[0:1] + grid_row.astype(jnp.float32) * rope[1:2]
        row_cos = jnp.cos(row_turn)
        row_sin = jnp.sin(row_turn)
        for r in range(rows_here):
            part = slice(r * GRID_W, (r + 1) * GRID_W)
            cosines[rel, part, :] = jnp.where(by_col, col_cos, row_cos[r : r + 1])
            sines[rel, part, :] = jnp.where(by_col, col_sin, row_sin[r : r + 1])

    forwards = []

    def forward_tokens(i):
        mirror_x[i].wait_recv()
        part = pl.ds(i * piece, piece)
        copy = remote(
            tokens.at[2, part],
            tokens.at[3, part],
            x_send.at[X_CHUNKS + 1 + i],
            x_recv.at[X_CHUNKS + 1 + i],
            (f, peers[1]),
        )
        copy.start()
        forwards.append(copy)

    def settle(x):
        x = x.astype(jnp.float32)
        x = x - jnp.mean(x, axis=1, keepdims=True)
        return x * lax.rsqrt(jnp.mean(x * x, axis=1, keepdims=True) + EPSILON)

    def modulate(x):
        return (x * mod_rows[:, width : 2 * width] + mod_rows[:, :width]).astype(jnp.bfloat16)

    own_tokens.wait()
    forward_tokens(0)
    sibling_x.wait_recv()
    for rel in range(2):

        def settle_rows(i, carry, rel=rel):
            offset = pl.multiple_of(i * 16, 16)
            settled[pl.ds(rel * rows + offset, 16), :] = settle(tokens[rel, pl.ds(offset, 16), :])
            return carry

        lax.fori_loop(0, rows // 16, settle_rows, 0, unroll=4)
    forward_tokens(1)
    qkv_load.wait()
    out_load.wait()
    for copy in mod_copies:
        copy.wait()
    for peer in range(PEERS):
        mod_rows[:, peer * mod_cols : (peer + 1) * mod_cols] = mod_all[peer]
    mod_rows[:, width : 2 * width] = 1.0 + mod_rows[:, width : 2 * width]

    def modulate_rows(i, carry):
        offset = pl.multiple_of(i * 16, 16)
        normed[pl.ds(offset, 16), :] = modulate(settled[pl.ds(offset, 16), :])
        return carry

    lax.fori_loop(0, 2 * rows // 16, modulate_rows, 0, unroll=4)

    def norm_piece(rel, start, size, at):
        def norm_rows(i, carry):
            offset = pl.multiple_of(i * 16, 16)
            x = settle(tokens[rel, pl.ds(start + offset, 16), :])
            normed[pl.ds(at + offset, 16), :] = modulate(x)
            return carry

        lax.fori_loop(0, size // 16, norm_rows, 0, unroll=True)

    score_scale = head_dim ** (-0.5) * math.log2(math.e)
    halo = []

    def project(pieces, task):
        count = len(pieces)
        at = sum(size for _, _, size in pieces)
        joined = jnp.dot(normed[:at, :], qkv_w[...], preferred_element_type=jnp.float32)
        at = 0
        for rel, start, size in pieces:
            cos = cosines[rel, start : start + size, :]
            sin = sines[rel, start : start + size, :]

            def turned(x, gain):
                x = x * lax.rsqrt(jnp.mean(x * x, axis=1, keepdims=True) + EPSILON) * gain
                swapped = (
                    pltpu.roll(x, halves[0], 1) * rope[3:4]
                    + pltpu.roll(x, head_dim - halves[0], 1) * rope[4:5]
                    + pltpu.roll(x, halves[1], 1) * rope[5:6]
                    + pltpu.roll(x, head_dim - halves[1], 1) * rope[6:7]
                )
                return (x * cos + swapped * sin).astype(jnp.bfloat16)

            own = joined[at : at + size]
            queries[rel, start : start + size, :] = turned(
                own[:, :head_dim], q_gain[...] * score_scale
            )
            kv[1, 0, rel, start : start + size, :] = turned(
                own[:, head_dim : 2 * head_dim], k_gain[...]
            )
            kv[1, 1, rel, start : start + size, :] = own[:, 2 * head_dim :].astype(jnp.bfloat16)
            at += size
        rels = pl.ds(pieces[0][0], count)
        part = pl.ds(pieces[0][1], pieces[0][2])
        forth = remote(
            kv.at[1, :, rels, part],
            kv.at[0, :, rels, part],
            h_send.at[0, task],
            h_recv.at[0, task],
            (lax.rem(f + 1, segments), q),
        )
        back = remote(
            kv.at[1, :, rels, part],
            kv.at[2, :, rels, part],
            h_send.at[1, task],
            h_recv.at[1, task],
            (lax.rem(f + segments - 1, segments), q),
        )

        @pl.when(f < last)
        def _():
            forth.start()

        @pl.when(f > 0)
        def _():
            back.start()

        halo.append((forth, back))

    cols = width // OUT_CHUNKS
    mirror_w = []

    def send_weights(i):
        part = pl.ds(i * cols, cols)
        copy = remote(
            out_w.at[0, :, part],
            out_w.at[2, :, part],
            w_send.at[i],
            w_recv.at[i],
            (f, peers[2]),
        )
        copy.start()
        mirror_w.append(copy)

    sibling_w = remote(
        out_w.at[0], out_w.at[1], w_send.at[OUT_CHUNKS], w_recv.at[OUT_CHUNKS], (f, peers[1])
    )
    project([(0, 0, rows), (1, 0, rows)], 0)
    half = rows // 2
    forward_tokens(2)
    send_weights(0)
    for i in range(2):
        forwards[i].wait_recv()
        norm_piece(2, i * piece, piece, i * piece)
        norm_piece(3, i * piece, piece, half + i * piece)
    project([(2, 0, half), (3, 0, half)], 1)
    send_weights(1)
    norm_piece(2, half, piece, 0)
    forwards[2].wait_recv()
    norm_piece(3, half, piece, half)
    forward_tokens(3)
    send_weights(2)
    send_weights(3)
    norm_piece(2, half + piece, piece, piece)
    forwards[3].wait_recv()
    norm_piece(3, half + piece, piece, half + piece)
    project([(2, half, half), (3, half, half)], 2)
    sibling_w.start()

    @pl.when(f == 0)
    def _():
        kv[0, 0] = kv[1, 0]
        kv[0, 1] = jnp.zeros_like(kv[0, 1])

    @pl.when(f == last)
    def _():
        kv[2, 0] = kv[1, 0]
        kv[2, 1] = jnp.zeros_like(kv[2, 1])

    for forth, back in halo:

        @pl.when(f > 0)
        def _(forth=forth):
            forth.wait_recv()

        @pl.when(f < last)
        def _(back=back):
            back.wait_recv()

    counted = (
        jnp.where(f > 0, 1.0, 0.0).astype(jnp.float32),
        jnp.float32(1.0),
        jnp.where(f < last, 1.0, 0.0).astype(jnp.float32),
    )
    tokens_all = PEERS * rows
    att_copies = []
    for rel in (3, 2, 1, 0):
        query_rows = queries[rel]
        scores = []
        for side in range(3):
            key_rows = kv[side, 0].reshape(tokens_all, head_dim)
            scores.append(
                lax.dot_general(
                    query_rows,
                    key_rows,
                    (((1,), (1,)), ((), ())),
                    preferred_element_type=jnp.float32,
                )
            )
        top = jnp.maximum(
            jnp.max(jnp.maximum(scores[0], scores[2]), axis=1, keepdims=True),
            jnp.max(scores[1], axis=1, keepdims=True),
        )
        weight = jnp.zeros((rows, 1), jnp.float32)
        mixed = jnp.zeros((rows, head_dim), jnp.float32)
        for side in range(3):
            raised = jnp.exp2(scores[side] - top)
            weight = weight + counted[side] * jnp.sum(raised, axis=1, keepdims=True)
            mixed = mixed + jnp.dot(
                raised.astype(jnp.bfloat16),
                kv[side, 1].reshape(tokens_all, head_dim),
                preferred_element_type=jnp.float32,
            )
        mixed = (mixed / weight).astype(jnp.bfloat16)
        if rel == 0:
            att[0] = mixed
        else:
            own_att[rel] = mixed
            copy = remote(
                own_att.at[rel], att.at[rel], a_send.at[rel], a_recv.at[rel], (f, peers[rel])
            )
            copy.start()
            att_copies.append(copy)

    forward_w = []

    def forward_weights(i):
        mirror_w[i].wait_recv()
        part = pl.ds(i * cols, cols)
        copy = remote(
            out_w.at[2, :, part],
            out_w.at[3, :, part],
            w_send.at[OUT_CHUNKS + 1 + i],
            w_recv.at[OUT_CHUNKS + 1 + i],
            (f, peers[1]),
        )
        copy.start()
        forward_w.append(copy)

    forward_weights(0)
    sibling_w.wait_recv()
    for copy in att_copies:
        copy.wait_recv()
    mixed = jnp.concatenate([att[rel] for rel in range(PEERS)], axis=1)

    clean_cols = width // segments
    shifts = []
    cleans = []
    for i in range(OUT_CHUNKS):
        if i + 1 < OUT_CHUNKS:
            forward_weights(i + 1)
        forward_w[i].wait_recv()
        begin = i * cols
        part = pl.ds(begin, cols)
        projected = jnp.dot(
            mixed,
            out_w[:, :, begin : begin + cols].reshape(PEERS * rows, cols),
            preferred_element_type=jnp.float32,
        )
        gate = mod_rows[:, 2 * width + begin : 2 * width + begin + cols]
        kept = tokens[0, :, begin : begin + cols].astype(jnp.float32)
        done[:, begin : begin + cols] = (kept + gate * projected).astype(jnp.bfloat16)
        shift = remote(
            done.at[:, part],
            queue_next.at[:, part],
            s_send.at[i],
            s_recv.at[i],
            (lax.rem(f + 1, segments), q),
        )
        shifts.append(shift)

        @pl.when(f < last)
        def _(shift=shift):
            shift.start()

        for to in range(begin // clean_cols, (begin + cols) // clean_cols):
            from_cols = done.at[:, pl.ds(to * clean_cols, clean_cols)]
            if to < last:
                clean_copy = remote(from_cols, clean, c_send.at[to], c_recv, (to, q))
            else:
                clean_copy = pltpu.make_async_copy(from_cols, clean, c_send.at[to])
            cleans.append(clean_copy)

            @pl.when(f == last)
            def _(clean_copy=clean_copy):
                clean_copy.start()

    for copy in mirror_x + [sibling_x] + forwards + mirror_w + [sibling_w] + forward_w + att_copies:
        copy.wait_send()
    for forth, back in halo:

        @pl.when(f < last)
        def _(forth=forth):
            forth.wait_send()

        @pl.when(f > 0)
        def _(back=back):
            back.wait_send()

    @pl.when(f == 0)
    def _():
        fresh_copy.wait()

    for shift in shifts:

        @pl.when(f < last)
        def _(shift=shift):
            shift.wait_send()

        @pl.when(f > 0)
        def _(shift=shift):
            shift.wait_recv()

    @pl.when(f == last)
    def _():
        for clean_copy in cleans[:-1]:
            clean_copy.wait_send()
        cleans[-1].wait()

    @pl.when(f < last)
    def _():
        cleans[0].wait_recv()


def hand_over(queue_in, clean_in, queue_next, clean, sem):
    copies = [
        pltpu.make_async_copy(queue_in, queue_next, sem.at[0]),
        pltpu.make_async_copy(clean_in, clean, sem.at[1]),
    ]
    for copy in copies:
        copy.start()
    for copy in copies:
        copy.wait()


def fused(
    mesh, queue, fresh_noise, w_mod, w_qkv, w_out, q_gain, k_gain, levels, plan, positions
):
    segments = mesh.shape["segment"]
    rows, width = queue.shape[1:]
    mod_cols = w_mod.shape[2]
    head_dim = q_gain.shape[1]
    rope, *halves = rope_rows(head_dim)
    scalars = pl.BlockSpec(memory_space=pltpu.SMEM)
    outside = pl.BlockSpec(memory_space=pl.ANY)
    bf16, f32 = jnp.bfloat16, jnp.float32
    dma = pltpu.SemaphoreType.DMA
    queue_next, clean_frame = pl.pallas_call(
        functools.partial(block_kernel, segments, tuple(halves)),
        out_shape=(
            jax.ShapeDtypeStruct((rows, width), bf16),
            jax.ShapeDtypeStruct((rows, width // segments), bf16),
        ),
        in_specs=[outside] * 7 + [scalars] * 3 + [outside] * 2,
        out_specs=(outside, outside),
        scratch_shapes=[
            pltpu.VMEM((width, mod_cols), bf16),
            pltpu.VMEM((width, 3 * head_dim), bf16),
            pltpu.VMEM((PEERS, rows, width), bf16),
            pltpu.VMEM((PEERS, rows, width), bf16),
            pltpu.VMEM((PEERS, 1, mod_cols), f32),
            pltpu.VMEM((1, 3 * width), f32),
            pltpu.VMEM((1, width // 2), f32),
            pltpu.VMEM((8, head_dim), f32),
            pltpu.VMEM((1, head_dim), f32),
            pltpu.VMEM((1, head_dim), f32),
            pltpu.VMEM((width, LANES), f32),
            pltpu.VMEM((2 * rows, width), f32),
            pltpu.VMEM((2 * rows, width), bf16),
            pltpu.VMEM((PEERS, rows, head_dim), f32),
            pltpu.VMEM((PEERS, rows, head_dim), f32),
            pltpu.VMEM((PEERS, rows, head_dim), bf16),
            pltpu.VMEM((3, 2, PEERS, rows, head_dim), bf16),
            pltpu.VMEM((PEERS, rows, head_dim), bf16),
            pltpu.VMEM((PEERS, rows, head_dim), bf16),
            pltpu.VMEM((rows, width), bf16),
            dma((4,)),
            dma((4 + MOD_CHUNKS,)),
            dma((2 * X_CHUNKS + 1,)),
            dma((2 * X_CHUNKS + 1,)),
            dma((PEERS,)),
            dma((PEERS,)),
            dma((2, 3)),
            dma((2, 3)),
            dma((2 * OUT_CHUNKS + 1,)),
            dma((2 * OUT_CHUNKS + 1,)),
            dma((PEERS,)),
            dma((PEERS,)),
            dma((OUT_CHUNKS,)),
            dma((OUT_CHUNKS,)),
            dma((segments,)),
            dma(()),
        ],
        compiler_params=pltpu.CompilerParams(
            collective_id=0, has_side_effects=True, vmem_limit_bytes=56 * 1024 * 1024
        ),
        cost_estimate=pl.CostEstimate(
            flops=2 * 10**9, bytes_accessed=22 * 10**6, transcendentals=10**6
        ),
        name="relayed_block",
    )(
        queue[0],
        fresh_noise,
        w_mod[0],
        w_qkv.reshape(width, 3 * head_dim),
        w_out[0],
        q_gain,
        k_gain,
        levels,
        plan,
        positions,
        jnp.asarray(time_rates(width)),
        jnp.asarray(rope),
    )
    queue_next, clean_frame = pl.pallas_call(
        hand_over,
        out_shape=(
            jax.ShapeDtypeStruct(queue_next.shape, bf16),
            jax.ShapeDtypeStruct(clean_frame.shape, bf16),
        ),
        in_specs=[outside] * 2,
        out_specs=(outside, outside),
        scratch_shapes=[dma((2,))],
        compiler_params=pltpu.CompilerParams(vmem_limit_bytes=56 * 1024 * 1024),
        name="hand_over",
    )(queue_next, clean_frame)
    return queue_next[None], clean_frame


def solution(mesh):
    placed = (
        P("segment", "seq", None),
        P("seq", None),
        P("segment", None, "seq"),
        P("segment", None, "seq", None),
        P("segment", "seq", None),
        P("segment", None),
        P("segment", None),
        P("segment"),
        P(),
        P("segment"),
    )
    return jax.shard_map(
        functools.partial(fused, mesh) if fits(mesh) else shards,
        mesh=mesh,
        in_specs=placed,
        out_specs=(P("segment", "seq", None), P("seq", "segment")),
        check_vma=False,
    )
```

```python
import functools
import math

import jax
import jax.numpy as jnp
from jax import lax
import numpy as np
from jax.experimental import pallas as pl
from jax.experimental.pallas import tpu as pltpu
from jax.sharding import PartitionSpec as P

GRID_W = 32


EPSILON = 1e-06
ROPE_BASE = 256.0


def with_halo(cells, sides, width):
    for axis, dim in sides:
        count = lax.axis_size(axis)
        ends = count - 1
        head = lax.slice_in_dim(cells, 0, width, axis=dim)
        tail = lax.slice_in_dim(cells, cells.shape[dim] - width, cells.shape[dim], axis=dim)
        cells = jnp.concatenate(
            [
                lax.ppermute(tail, axis, [(i, (i + 1) % count) for i in range(ends)]),
                cells,
                lax.ppermute(head, axis, [((i + 1) % count, i) for i in range(ends)]),
            ],
            axis=dim,
        )
    return cells


def passed_along(value, axis, by):
    length = lax.axis_size(axis)
    pairs = [(i, i + by) for i in range(length) if 0 <= i + by < length]
    return lax.ppermute(value, axis, pairs)


def broadcast(value, axis, root):
    mine = lax.axis_index(axis) == root
    return lax.psum(jnp.where(mine, value, jnp.zeros_like(value)), axis)


def time_embedding(step_values, width):
    half_width = width // 2
    counter = jnp.arange(half_width, dtype=jnp.float32)
    frequency = jnp.exp(-jnp.log(10000.0) * counter / half_width)
    angles = step_values.astype(jnp.float32)[:, None] * frequency[None, :]
    return jnp.concatenate([jnp.cos(angles), jnp.sin(angles)], axis=-1)


def rope_angles(frame_position, row_count, head_dim, grid_width):
    time_dim = head_dim // 8
    space_dim = (head_dim - time_dim) // 2
    tokens_at = jnp.arange(row_count, dtype=jnp.int32)
    grid_row = (tokens_at // grid_width).astype(jnp.float32)
    grid_col = (tokens_at % grid_width).astype(jnp.float32)
    moment = jnp.zeros((row_count,), jnp.float32) + frame_position.astype(jnp.float32)
    sections = []
    for coords, section in ((moment, time_dim), (grid_row, space_dim), (grid_col, space_dim)):
        half_size = section // 2
        frequency = ROPE_BASE ** (-2.0 * jnp.arange(half_size, dtype=jnp.float32) / section)
        angles = coords[:, None] * frequency[None, :]
        sections.append(jnp.concatenate([angles, angles], axis=-1))
    return jnp.concatenate(sections, axis=-1)


def rotate_half(values, head_dim):
    time_dim = head_dim // 8
    space_dim = (head_dim - time_dim) // 2
    pieces_out = []
    position = 0
    for section in (time_dim, space_dim, space_dim):
        half_size = section // 2
        leading = values[..., position : position + half_size]
        second = values[..., position + half_size : position + section]
        pieces_out.append(jnp.concatenate([-second, leading], axis=-1))
        position += section
    return jnp.concatenate(pieces_out, axis=-1)


def apply_rope(values, angles, head_dim):
    return values * jnp.cos(angles) + rotate_half(values, head_dim) * jnp.sin(angles)


def rms_gain(values, gains):
    mean_square = jnp.mean(values * values, axis=-1, keepdims=True)
    return values * lax.rsqrt(mean_square + EPSILON) * gains


def layer_norm(values):
    centre = jnp.mean(values, axis=-1, keepdims=True)
    spread = jnp.mean(jnp.square(values - centre), axis=-1, keepdims=True)
    return (values - centre) * lax.rsqrt(spread + EPSILON)


def attend(query_rows, key_rows, value_rows, usable, head_dim):
    scores = jnp.dot(query_rows, key_rows.T, preferred_element_type=jnp.float32) * head_dim ** (
        -0.5
    )
    scores = jnp.where(usable[None, :], scores, -jnp.inf)
    row_max = jnp.max(scores, axis=-1, keepdims=True)
    raised = jnp.exp(scores - row_max)
    weights = (raised / jnp.sum(raised, axis=-1, keepdims=True)).astype(jnp.bfloat16)
    return jnp.dot(weights, value_rows, preferred_element_type=jnp.float32).astype(jnp.bfloat16)


def shards(queue, fresh_noise, w_mod, w_qkv, w_out, q_gain, k_gain, levels, plan, positions):
    segments = lax.axis_size("segment")
    seq_count = lax.axis_size("seq")
    segment_at = lax.axis_index("segment")
    tok_dev = queue.shape[1]
    width = queue.shape[2]
    heads_here = w_qkv.shape[2]
    head_dim = w_qkv.shape[3] // 3
    tok_frame = tok_dev * seq_count
    picked = levels[:, None] == jnp.arange(plan.shape[0], dtype=jnp.int32)[None, :]
    step_values = jnp.sum(jnp.where(picked, plan[None, :], 0), axis=1)
    embedding = jax.nn.silu(time_embedding(step_values, width)).astype(jnp.bfloat16)
    mod_part = jnp.dot(embedding, w_mod[0], preferred_element_type=jnp.float32)
    modulation = lax.all_gather(mod_part, "seq", axis=1, tiled=True)[0]
    shift_row = modulation[:width]
    scale_row = modulation[width : 2 * width]
    gate_row = modulation[2 * width :]
    resident = queue[0].astype(jnp.float32)
    modulated = (layer_norm(resident) * (1.0 + scale_row) + shift_row).astype(jnp.bfloat16)
    flat_weight = w_qkv[0].reshape(width, heads_here * 3 * head_dim)
    projected_qkv = jnp.dot(
        lax.all_gather(modulated, "seq", axis=0, tiled=True),
        flat_weight,
        preferred_element_type=jnp.float32,
    )
    projected_qkv = projected_qkv.reshape(tok_frame, heads_here, 3 * head_dim)
    angles = rope_angles(positions[0], tok_frame, head_dim, GRID_W)[:, None, :]
    queries = apply_rope(
        rms_gain(projected_qkv[..., :head_dim], q_gain[0]), angles, head_dim
    ).astype(jnp.bfloat16)
    key_rows = apply_rope(
        rms_gain(projected_qkv[..., head_dim : 2 * head_dim], k_gain[0]), angles, head_dim
    ).astype(jnp.bfloat16)
    value_rows = projected_qkv[..., 2 * head_dim :].astype(jnp.bfloat16)
    stacked = jnp.stack([key_rows, value_rows])[None]
    beside_all = with_halo(stacked, (("segment", 0),), 1)
    earlier = beside_all[0]
    following = beside_all[2]
    near_keys = jnp.concatenate([earlier[0], key_rows, following[0]], axis=0)
    near_values = jnp.concatenate([earlier[1], value_rows, following[1]], axis=0)
    filled = jnp.ones((tok_frame,), dtype=bool)
    usable = jnp.concatenate(
        [filled & (segment_at > 0), filled, filled & (segment_at < segments - 1)]
    )
    block_rows = math.gcd(tok_frame, 512)
    block_count = tok_frame // block_rows
    head_keys = near_keys[:, 0]
    head_values = near_values[:, 0]
    query_blocks = queries[:, 0].reshape(block_count, block_rows, head_dim)

    def one_block(query_rows, head_keys=head_keys, head_values=head_values):
        return attend(query_rows, head_keys, head_values, usable, head_dim)

    outputs = [lax.map(one_block, query_blocks).reshape(tok_frame, head_dim)]
    attended = jnp.stack(outputs, axis=1).reshape(tok_frame, heads_here * head_dim)
    projected = lax.psum_scatter(
        jnp.dot(attended, w_out[0], preferred_element_type=jnp.float32).astype(jnp.bfloat16),
        "seq",
        scatter_dimension=0,
        tiled=True,
    ).astype(jnp.float32)
    finished = (resident + gate_row * projected).astype(jnp.bfloat16)
    arrived = passed_along(finished, "segment", 1)
    queue_next = jnp.where(segment_at == 0, fresh_noise, arrived)[None]
    clean_whole = broadcast(finished, "segment", segments - 1)
    column_count = width // segments
    clean_frame = lax.dynamic_slice_in_dim(clean_whole, segment_at * column_count, column_count, 1)
    return (queue_next, clean_frame)


MESH = pl.DeviceIdType.MESH
PEERS = 4
MOD_CHUNKS = 6
X_CHUNKS = 4
OUT_CHUNKS = 4
LANES = 128


def fits(mesh):
    return mesh.shape["seq"] == PEERS


def rope_rows(head_dim):
    time_dim = head_dim // 8
    space_dim = (head_dim - time_dim) // 2
    rows = np.zeros((8, head_dim), np.float32)
    start = 0
    for at, section in enumerate((time_dim, space_dim, space_dim)):
        half = section // 2
        frequency = ROPE_BASE ** (-2.0 * np.arange(half) / section)
        rows[at, start : start + half] = frequency
        rows[at, start + half : start + section] = frequency
        back, forth = (3, 4) if at == 0 else (5, 6)
        rows[back, start + half : start + section] = 1.0
        rows[forth, start : start + half] = -1.0
        start += section
    return rows, time_dim // 2, space_dim // 2


def time_rates(width):
    half_width = width // 2
    return np.exp(-np.log(10000.0) * np.arange(half_width) / half_width).astype(np.float32)[None]


def block_kernel(
    segments,
    halves,
    queue,
    fresh,
    w_mod,
    w_qkv,
    w_out,
    q_gain_in,
    k_gain_in,
    levels,
    plan,
    positions,
    rates_in,
    rope_in,
    queue_next,
    clean,
    mod_w,
    qkv_w,
    out_w,
    tokens,
    mod_all,
    mod_rows,
    rates,
    rope,
    q_gain,
    k_gain,
    embedded,
    settled,
    normed,
    cosines,
    sines,
    queries,
    kv,
    own_att,
    att,
    done,
    arrived,
    small_sem,
    local_sem,
    x_send,
    x_recv,
    m_send,
    m_recv,
    h_send,
    h_recv,
    w_send,
    w_recv,
    a_send,
    a_recv,
    s_send,
    s_recv,
    c_send,
    c_recv,
    out_sem,
):
    f = lax.axis_index("segment")
    q = lax.axis_index("seq")
    last = segments - 1
    rows, width = queue.shape
    head_dim = q_gain_in.shape[1]
    mod_cols = w_mod.shape[1]
    peers = (q, q + 1 - 2 * lax.rem(q, 2), lax.rem(q + 2, 4), 3 - q)

    def remote(source, target, send, recv, device):
        return pltpu.make_async_remote_copy(
            src_ref=source,
            dst_ref=target,
            send_sem=send,
            recv_sem=recv,
            device_id=device,
            device_id_type=MESH,
        )

    barrier = pltpu.get_barrier_semaphore()
    for rel in range(1, PEERS):
        pl.semaphore_signal(barrier, inc=1, device_id=(f, peers[rel]), device_id_type=MESH)
    for step in range(1, segments):
        pl.semaphore_signal(
            barrier, inc=1, device_id=(lax.rem(f + step, segments), q), device_id_type=MESH
        )

    own_tokens = pltpu.make_async_copy(queue, tokens.at[0], local_sem.at[0])
    own_tokens.start()
    small_loads = []
    for i, (source, target) in enumerate(
        ((rates_in, rates), (rope_in, rope), (q_gain_in, q_gain), (k_gain_in, k_gain))
    ):
        load = pltpu.make_async_copy(source, target, small_sem.at[i])
        load.start()
        small_loads.append(load)
    mod_depth = width // MOD_CHUNKS
    mod_loads = []
    for i in range(MOD_CHUNKS):
        part = pl.ds(i * mod_depth, mod_depth)
        load = pltpu.make_async_copy(w_mod.at[part], mod_w.at[part], local_sem.at[1 + i])
        load.start()
        mod_loads.append(load)
    qkv_load = pltpu.make_async_copy(w_qkv, qkv_w, local_sem.at[1 + MOD_CHUNKS])
    qkv_load.start()
    out_load = pltpu.make_async_copy(w_out, out_w.at[0], local_sem.at[2 + MOD_CHUNKS])
    out_load.start()

    pl.semaphore_wait(barrier, PEERS - 1 + segments - 1)

    own_tokens.wait()

    piece = rows // X_CHUNKS
    mirror_x = []
    for i in range(X_CHUNKS):
        part = pl.ds(i * piece, piece)
        copy = remote(
            tokens.at[0, part], tokens.at[2, part], x_send.at[i], x_recv.at[i], (f, peers[2])
        )
        copy.start()
        mirror_x.append(copy)
    sibling_x = remote(
        tokens.at[0], tokens.at[1], x_send.at[X_CHUNKS], x_recv.at[X_CHUNKS], (f, peers[1])
    )
    sibling_x.start()
    fresh_copy = pltpu.make_async_copy(fresh, arrived, local_sem.at[3 + MOD_CHUNKS])

    @pl.when(f == 0)
    def _():
        fresh_copy.start()

    for load in small_loads:
        load.wait()
    step_value = plan[levels[0]].astype(jnp.float32)
    angles = rates[...] * step_value
    embedding = jnp.concatenate([jnp.cos(angles), jnp.sin(angles)], axis=1)
    embedding = embedding / (1.0 + jnp.exp(-embedding))
    embedding = embedding.astype(jnp.bfloat16).astype(jnp.float32)
    for start in range(0, width, LANES):
        entries = jnp.broadcast_to(embedding[:, start : start + LANES], (LANES, LANES))
        embedded[start : start + LANES, :] = entries.T
    tiles = mod_cols // LANES

    def add_rows(i, totals):
        offset = pl.multiple_of(i * 16, 16)
        entries = embedded[pl.ds(offset, 16), :]
        sums = []
        for tile in range(tiles):
            lanes = slice(tile * LANES, (tile + 1) * LANES)
            product = mod_w[pl.ds(offset, 16), lanes].astype(jnp.float32) * entries
            sums.append(totals[tile] + (product[:8] + product[8:]))
        return tuple(sums)

    totals = tuple(jnp.zeros((8, LANES), jnp.float32) for _ in range(tiles))
    steps = mod_depth // 16
    for i in range(MOD_CHUNKS):
        mod_loads[i].wait()
        totals = lax.fori_loop(i * steps, (i + 1) * steps, add_rows, totals, unroll=4)
    mod_all[q] = jnp.concatenate(
        [jnp.sum(total, axis=0, keepdims=True) for total in totals], axis=1
    )
    mod_copies = []
    for rel in range(1, PEERS):
        copy = remote(
            mod_all.at[q], mod_all.at[q], m_send.at[rel], m_recv.at[rel], (f, peers[rel])
        )
        copy.start()
        mod_copies.append(copy)

    position = positions[0].astype(jnp.float32)
    grid_col = lax.broadcasted_iota(jnp.int32, (GRID_W, head_dim), 0).astype(jnp.float32)
    col_turn = grid_col * rope[2:3]
    col_cos = jnp.cos(col_turn)
    col_sin = jnp.sin(col_turn)
    by_col = lax.broadcasted_iota(jnp.int32, (GRID_W, head_dim), 1) >= head_dim - 2 * halves[1]
    rows_here = rows // GRID_W
    for rel in range(PEERS):
        grid_row = lax.broadcasted_iota(jnp.int32, (8, head_dim), 0) + peers[rel] * rows_here
        row_turn = position * rope[0:1] + grid_row.astype(jnp.float32) * rope[1:2]
        row_cos = jnp.cos(row_turn)
        row_sin = jnp.sin(row_turn)
        for r in range(rows_here):
            part = slice(r * GRID_W, (r + 1) * GRID_W)
            cosines[rel, part, :] = jnp.where(by_col, col_cos, row_cos[r : r + 1])
            sines[rel, part, :] = jnp.where(by_col, col_sin, row_sin[r : r + 1])

    forwards = []

    def forward_tokens(i):
        mirror_x[i].wait_recv()
        part = pl.ds(i * piece, piece)
        copy = remote(
            tokens.at[2, part],
            tokens.at[3, part],
            x_send.at[X_CHUNKS + 1 + i],
            x_recv.at[X_CHUNKS + 1 + i],
            (f, peers[1]),
        )
        copy.start()
        forwards.append(copy)

    def settle(x):
        x = x.astype(jnp.float32)
        x = x - jnp.mean(x, axis=1, keepdims=True)
        return x * lax.rsqrt(jnp.mean(x * x, axis=1, keepdims=True) + EPSILON)

    def modulate(x):
        return (x * mod_rows[:, width : 2 * width] + mod_rows[:, :width]).astype(jnp.bfloat16)

    forward_tokens(0)
    sibling_x.wait_recv()
    for rel in range(2):

        def settle_rows(i, carry, rel=rel):
            offset = pl.multiple_of(i * 16, 16)
            settled[pl.ds(rel * rows + offset, 16), :] = settle(tokens[rel, pl.ds(offset, 16), :])
            return carry

        lax.fori_loop(0, rows // 16, settle_rows, 0, unroll=4)
    forward_tokens(1)
    qkv_load.wait()
    out_load.wait()
    for copy in mod_copies:
        copy.wait()
    for peer in range(PEERS):
        mod_rows[:, peer * mod_cols : (peer + 1) * mod_cols] = mod_all[peer]
    mod_rows[:, width : 2 * width] = 1.0 + mod_rows[:, width : 2 * width]

    def modulate_rows(i, carry):
        offset = pl.multiple_of(i * 16, 16)
        normed[pl.ds(offset, 16), :] = modulate(settled[pl.ds(offset, 16), :])
        return carry

    lax.fori_loop(0, 2 * rows // 16, modulate_rows, 0, unroll=4)

    def norm_piece(rel, start, size, at):
        def norm_rows(i, carry):
            offset = pl.multiple_of(i * 16, 16)
            x = settle(tokens[rel, pl.ds(start + offset, 16), :])
            normed[pl.ds(at + offset, 16), :] = modulate(x)
            return carry

        lax.fori_loop(0, size // 16, norm_rows, 0, unroll=True)

    score_scale = head_dim ** (-0.5) * math.log2(math.e)
    halo = []

    def project(pieces, task):
        count = len(pieces)
        at = sum(size for _, _, size in pieces)
        joined = jnp.dot(normed[:at, :], qkv_w[...], preferred_element_type=jnp.float32)
        at = 0
        for rel, start, size in pieces:
            cos = cosines[rel, start : start + size, :]
            sin = sines[rel, start : start + size, :]

            def turned(x, gain):
                x = x * lax.rsqrt(jnp.mean(x * x, axis=1, keepdims=True) + EPSILON) * gain
                swapped = (
                    pltpu.roll(x, halves[0], 1) * rope[3:4]
                    + pltpu.roll(x, head_dim - halves[0], 1) * rope[4:5]
                    + pltpu.roll(x, halves[1], 1) * rope[5:6]
                    + pltpu.roll(x, head_dim - halves[1], 1) * rope[6:7]
                )
                return (x * cos + swapped * sin).astype(jnp.bfloat16)

            own = joined[at : at + size]
            queries[rel, start : start + size, :] = turned(
                own[:, :head_dim], q_gain[...] * score_scale
            )
            kv[1, 0, rel, start : start + size, :] = turned(
                own[:, head_dim : 2 * head_dim], k_gain[...]
            )
            kv[1, 1, rel, start : start + size, :] = own[:, 2 * head_dim :].astype(jnp.bfloat16)
            at += size
        rels = pl.ds(pieces[0][0], count)
        part = pl.ds(pieces[0][1], pieces[0][2])
        forth = remote(
            kv.at[1, :, rels, part],
            kv.at[0, :, rels, part],
            h_send.at[0, task],
            h_recv.at[0, task],
            (lax.rem(f + 1, segments), q),
        )
        back = remote(
            kv.at[1, :, rels, part],
            kv.at[2, :, rels, part],
            h_send.at[1, task],
            h_recv.at[1, task],
            (lax.rem(f + segments - 1, segments), q),
        )

        @pl.when(f < last)
        def _():
            forth.start()

        @pl.when(f > 0)
        def _():
            back.start()

        halo.append((forth, back))

    cols = width // OUT_CHUNKS
    mirror_w = []

    def send_weights(i):
        part = pl.ds(i * cols, cols)
        copy = remote(
            out_w.at[0, :, part],
            out_w.at[2, :, part],
            w_send.at[i],
            w_recv.at[i],
            (f, peers[2]),
        )
        copy.start()
        mirror_w.append(copy)

    sibling_w = remote(
        out_w.at[0], out_w.at[1], w_send.at[OUT_CHUNKS], w_recv.at[OUT_CHUNKS], (f, peers[1])
    )
    project([(0, 0, rows), (1, 0, rows)], 0)
    half = rows // 2
    forward_tokens(2)
    send_weights(0)
    for i in range(2):
        forwards[i].wait_recv()
        norm_piece(2, i * piece, piece, i * piece)
        norm_piece(3, i * piece, piece, half + i * piece)
    project([(2, 0, half), (3, 0, half)], 1)
    send_weights(1)
    norm_piece(2, half, piece, 0)
    forwards[2].wait_recv()
    norm_piece(3, half, piece, half)
    forward_tokens(3)
    send_weights(2)
    send_weights(3)
    norm_piece(2, half + piece, piece, piece)
    forwards[3].wait_recv()
    norm_piece(3, half + piece, piece, half + piece)
    project([(2, half, half), (3, half, half)], 2)
    sibling_w.start()

    @pl.when(f == 0)
    def _():
        kv[0, 0] = kv[1, 0]
        kv[0, 1] = jnp.zeros_like(kv[0, 1])

    @pl.when(f == last)
    def _():
        kv[2, 0] = kv[1, 0]
        kv[2, 1] = jnp.zeros_like(kv[2, 1])

    for forth, back in halo:

        @pl.when(f > 0)
        def _(forth=forth):
            forth.wait_recv()

        @pl.when(f < last)
        def _(back=back):
            back.wait_recv()

    counted = (
        jnp.where(f > 0, 1.0, 0.0).astype(jnp.float32),
        jnp.float32(1.0),
        jnp.where(f < last, 1.0, 0.0).astype(jnp.float32),
    )
    tokens_all = PEERS * rows
    att_copies = []
    for rel in (3, 2, 1, 0):
        query_rows = queries[rel]
        scores = []
        for side in range(3):
            key_rows = kv[side, 0].reshape(tokens_all, head_dim)
            scores.append(
                lax.dot_general(
                    query_rows,
                    key_rows,
                    (((1,), (1,)), ((), ())),
                    preferred_element_type=jnp.float32,
                )
            )
        top = jnp.maximum(
            jnp.max(jnp.maximum(scores[0], scores[2]), axis=1, keepdims=True),
            jnp.max(scores[1], axis=1, keepdims=True),
        )
        weight = jnp.zeros((rows, 1), jnp.float32)
        mixed = jnp.zeros((rows, head_dim), jnp.float32)
        for side in range(3):
            raised = jnp.exp2(scores[side] - top)
            weight = weight + counted[side] * jnp.sum(raised, axis=1, keepdims=True)
            mixed = mixed + jnp.dot(
                raised.astype(jnp.bfloat16),
                kv[side, 1].reshape(tokens_all, head_dim),
                preferred_element_type=jnp.float32,
            )
        mixed = (mixed / weight).astype(jnp.bfloat16)
        if rel == 0:
            att[0] = mixed
        else:
            own_att[rel] = mixed
            copy = remote(
                own_att.at[rel], att.at[rel], a_send.at[rel], a_recv.at[rel], (f, peers[rel])
            )
            copy.start()
            att_copies.append(copy)

    forward_w = []

    def forward_weights(i):
        mirror_w[i].wait_recv()
        part = pl.ds(i * cols, cols)
        copy = remote(
            out_w.at[2, :, part],
            out_w.at[3, :, part],
            w_send.at[OUT_CHUNKS + 1 + i],
            w_recv.at[OUT_CHUNKS + 1 + i],
            (f, peers[1]),
        )
        copy.start()
        forward_w.append(copy)

    forward_weights(0)
    sibling_w.wait_recv()
    for copy in att_copies:
        copy.wait_recv()
    mixed = jnp.concatenate([att[rel] for rel in range(PEERS)], axis=1)

    clean_cols = width // segments
    shifts = []
    cleans = []
    for i in range(OUT_CHUNKS):
        if i + 1 < OUT_CHUNKS:
            forward_weights(i + 1)
        forward_w[i].wait_recv()
        begin = i * cols
        part = pl.ds(begin, cols)
        projected = jnp.dot(
            mixed,
            out_w[:, :, begin : begin + cols].reshape(PEERS * rows, cols),
            preferred_element_type=jnp.float32,
        )
        gate = mod_rows[:, 2 * width + begin : 2 * width + begin + cols]
        kept = tokens[0, :, begin : begin + cols].astype(jnp.float32)
        done[:, begin : begin + cols] = (kept + gate * projected).astype(jnp.bfloat16)
        shift = remote(
            done.at[:, part],
            arrived.at[:, part],
            s_send.at[i],
            s_recv.at[i],
            (lax.rem(f + 1, segments), q),
        )
        shifts.append(shift)

        @pl.when(f < last)
        def _(shift=shift):
            shift.start()

        for to in range(begin // clean_cols, (begin + cols) // clean_cols):
            from_cols = done.at[:, pl.ds(to * clean_cols, clean_cols)]
            if to < last:
                clean_copy = remote(from_cols, clean, c_send.at[to], c_recv, (to, q))
            else:
                clean_copy = pltpu.make_async_copy(from_cols, clean, c_send.at[to])
            cleans.append(clean_copy)

            @pl.when(f == last)
            def _(clean_copy=clean_copy):
                clean_copy.start()

    for copy in mirror_x + [sibling_x] + forwards + mirror_w + [sibling_w] + forward_w + att_copies:
        copy.wait_send()
    for forth, back in halo:

        @pl.when(f < last)
        def _(forth=forth):
            forth.wait_send()

        @pl.when(f > 0)
        def _(back=back):
            back.wait_send()

    @pl.when(f == 0)
    def _():
        fresh_copy.wait()

    written = []
    for i, shift in enumerate(shifts):

        @pl.when(f > 0)
        def _(shift=shift):
            shift.wait_recv()

        part = pl.ds(i * cols, cols)
        copy = pltpu.make_async_copy(
            arrived.at[:, part], queue_next.at[:, part], out_sem.at[i]
        )
        copy.start()
        written.append(copy)
    for copy in written:
        copy.wait()
    for shift in shifts:

        @pl.when(f < last)
        def _(shift=shift):
            shift.wait_send()

    @pl.when(f == last)
    def _():
        for clean_copy in cleans[:-1]:
            clean_copy.wait_send()
        cleans[-1].wait()

    @pl.when(f < last)
    def _():
        cleans[0].wait_recv()


def hand_over(queue_in, clean_in, queue_next, clean, queue_held, clean_held, sem_in, sem_out):
    piece = queue_in.shape[0] // X_CHUNKS
    steps = []
    for i in range(X_CHUNKS):
        part = pl.ds(i * piece, piece)
        steps.append((queue_in.at[part], queue_held.at[part], queue_next.at[part]))
    steps.append((clean_in, clean_held, clean))
    reads = []
    for i, (source, held, _) in enumerate(steps):
        copy = pltpu.make_async_copy(source, held, sem_in.at[i])
        copy.start()
        reads.append(copy)
    writes = []
    for i, (_, held, target) in enumerate(steps):
        reads[i].wait()
        copy = pltpu.make_async_copy(held, target, sem_out.at[i])
        copy.start()
        writes.append(copy)
    for copy in writes:
        copy.wait()


def fused(
    mesh, queue, fresh_noise, w_mod, w_qkv, w_out, q_gain, k_gain, levels, plan, positions
):
    segments = mesh.shape["segment"]
    rows, width = queue.shape[1:]
    mod_cols = w_mod.shape[2]
    head_dim = q_gain.shape[1]
    rope, *halves = rope_rows(head_dim)
    scalars = pl.BlockSpec(memory_space=pltpu.SMEM)
    outside = pl.BlockSpec(memory_space=pl.ANY)
    bf16, f32 = jnp.bfloat16, jnp.float32
    dma = pltpu.SemaphoreType.DMA
    queue_next, clean_frame = pl.pallas_call(
        functools.partial(block_kernel, segments, tuple(halves)),
        out_shape=(
            jax.ShapeDtypeStruct((rows, width), bf16),
            jax.ShapeDtypeStruct((rows, width // segments), bf16),
        ),
        in_specs=[outside] * 7 + [scalars] * 3 + [outside] * 2,
        out_specs=(outside, outside),
        scratch_shapes=[
            pltpu.VMEM((width, mod_cols), bf16),
            pltpu.VMEM((width, 3 * head_dim), bf16),
            pltpu.VMEM((PEERS, rows, width), bf16),
            pltpu.VMEM((PEERS, rows, width), bf16),
            pltpu.VMEM((PEERS, 1, mod_cols), f32),
            pltpu.VMEM((1, 3 * width), f32),
            pltpu.VMEM((1, width // 2), f32),
            pltpu.VMEM((8, head_dim), f32),
            pltpu.VMEM((1, head_dim), f32),
            pltpu.VMEM((1, head_dim), f32),
            pltpu.VMEM((width, LANES), f32),
            pltpu.VMEM((2 * rows, width), f32),
            pltpu.VMEM((2 * rows, width), bf16),
            pltpu.VMEM((PEERS, rows, head_dim), f32),
            pltpu.VMEM((PEERS, rows, head_dim), f32),
            pltpu.VMEM((PEERS, rows, head_dim), bf16),
            pltpu.VMEM((3, 2, PEERS, rows, head_dim), bf16),
            pltpu.VMEM((PEERS, rows, head_dim), bf16),
            pltpu.VMEM((PEERS, rows, head_dim), bf16),
            pltpu.VMEM((rows, width), bf16),
            pltpu.VMEM((rows, width), bf16),
            dma((4,)),
            dma((4 + MOD_CHUNKS,)),
            dma((2 * X_CHUNKS + 1,)),
            dma((2 * X_CHUNKS + 1,)),
            dma((PEERS,)),
            dma((PEERS,)),
            dma((2, 3)),
            dma((2, 3)),
            dma((2 * OUT_CHUNKS + 1,)),
            dma((2 * OUT_CHUNKS + 1,)),
            dma((PEERS,)),
            dma((PEERS,)),
            dma((OUT_CHUNKS,)),
            dma((OUT_CHUNKS,)),
            dma((segments,)),
            dma(()),
            dma((OUT_CHUNKS,)),
        ],
        compiler_params=pltpu.CompilerParams(
            collective_id=0, has_side_effects=True, vmem_limit_bytes=56 * 1024 * 1024
        ),
        cost_estimate=pl.CostEstimate(
            flops=2 * 10**9, bytes_accessed=22 * 10**6, transcendentals=10**6
        ),
        name="relayed_block",
    )(
        queue[0],
        fresh_noise,
        w_mod[0],
        w_qkv.reshape(width, 3 * head_dim),
        w_out[0],
        q_gain,
        k_gain,
        levels,
        plan,
        positions,
        jnp.asarray(time_rates(width)),
        jnp.asarray(rope),
    )
    queue_next, clean_frame = pl.pallas_call(
        hand_over,
        out_shape=(
            jax.ShapeDtypeStruct(queue_next.shape, bf16),
            jax.ShapeDtypeStruct(clean_frame.shape, bf16),
        ),
        in_specs=[outside] * 2,
        out_specs=(outside, outside),
        scratch_shapes=[
            pltpu.VMEM(queue_next.shape, bf16),
            pltpu.VMEM(clean_frame.shape, bf16),
            dma((X_CHUNKS + 1,)),
            dma((X_CHUNKS + 1,)),
        ],
        compiler_params=pltpu.CompilerParams(vmem_limit_bytes=56 * 1024 * 1024),
        name="hand_over",
    )(queue_next, clean_frame)
    return queue_next[None], clean_frame


def solution(mesh):
    placed = (
        P("segment", "seq", None),
        P("seq", None),
        P("segment", None, "seq"),
        P("segment", None, "seq", None),
        P("segment", "seq", None),
        P("segment", None),
        P("segment", None),
        P("segment"),
        P(),
        P("segment"),
    )
    return jax.shard_map(
        functools.partial(fused, mesh) if fits(mesh) else shards,
        mesh=mesh,
        in_specs=placed,
        out_specs=(P("segment", "seq", None), P("seq", "segment")),
        check_vma=False,
    )
```

```python
import functools
import math

import jax
import jax.numpy as jnp
from jax import lax
import numpy as np
from jax.experimental import pallas as pl
from jax.experimental.pallas import tpu as pltpu
from jax.sharding import PartitionSpec as P

GRID_W = 32


EPSILON = 1e-06
ROPE_BASE = 256.0


def with_halo(cells, sides, width):
    for axis, dim in sides:
        count = lax.axis_size(axis)
        ends = count - 1
        head = lax.slice_in_dim(cells, 0, width, axis=dim)
        tail = lax.slice_in_dim(cells, cells.shape[dim] - width, cells.shape[dim], axis=dim)
        cells = jnp.concatenate(
            [
                lax.ppermute(tail, axis, [(i, (i + 1) % count) for i in range(ends)]),
                cells,
                lax.ppermute(head, axis, [((i + 1) % count, i) for i in range(ends)]),
            ],
            axis=dim,
        )
    return cells


def passed_along(value, axis, by):
    length = lax.axis_size(axis)
    pairs = [(i, i + by) for i in range(length) if 0 <= i + by < length]
    return lax.ppermute(value, axis, pairs)


def broadcast(value, axis, root):
    mine = lax.axis_index(axis) == root
    return lax.psum(jnp.where(mine, value, jnp.zeros_like(value)), axis)


def time_embedding(step_values, width):
    half_width = width // 2
    counter = jnp.arange(half_width, dtype=jnp.float32)
    frequency = jnp.exp(-jnp.log(10000.0) * counter / half_width)
    angles = step_values.astype(jnp.float32)[:, None] * frequency[None, :]
    return jnp.concatenate([jnp.cos(angles), jnp.sin(angles)], axis=-1)


def rope_angles(frame_position, row_count, head_dim, grid_width):
    time_dim = head_dim // 8
    space_dim = (head_dim - time_dim) // 2
    tokens_at = jnp.arange(row_count, dtype=jnp.int32)
    grid_row = (tokens_at // grid_width).astype(jnp.float32)
    grid_col = (tokens_at % grid_width).astype(jnp.float32)
    moment = jnp.zeros((row_count,), jnp.float32) + frame_position.astype(jnp.float32)
    sections = []
    for coords, section in ((moment, time_dim), (grid_row, space_dim), (grid_col, space_dim)):
        half_size = section // 2
        frequency = ROPE_BASE ** (-2.0 * jnp.arange(half_size, dtype=jnp.float32) / section)
        angles = coords[:, None] * frequency[None, :]
        sections.append(jnp.concatenate([angles, angles], axis=-1))
    return jnp.concatenate(sections, axis=-1)


def rotate_half(values, head_dim):
    time_dim = head_dim // 8
    space_dim = (head_dim - time_dim) // 2
    pieces_out = []
    position = 0
    for section in (time_dim, space_dim, space_dim):
        half_size = section // 2
        leading = values[..., position : position + half_size]
        second = values[..., position + half_size : position + section]
        pieces_out.append(jnp.concatenate([-second, leading], axis=-1))
        position += section
    return jnp.concatenate(pieces_out, axis=-1)


def apply_rope(values, angles, head_dim):
    return values * jnp.cos(angles) + rotate_half(values, head_dim) * jnp.sin(angles)


def rms_gain(values, gains):
    mean_square = jnp.mean(values * values, axis=-1, keepdims=True)
    return values * lax.rsqrt(mean_square + EPSILON) * gains


def layer_norm(values):
    centre = jnp.mean(values, axis=-1, keepdims=True)
    spread = jnp.mean(jnp.square(values - centre), axis=-1, keepdims=True)
    return (values - centre) * lax.rsqrt(spread + EPSILON)


def attend(query_rows, key_rows, value_rows, usable, head_dim):
    scores = jnp.dot(query_rows, key_rows.T, preferred_element_type=jnp.float32) * head_dim ** (
        -0.5
    )
    scores = jnp.where(usable[None, :], scores, -jnp.inf)
    row_max = jnp.max(scores, axis=-1, keepdims=True)
    raised = jnp.exp(scores - row_max)
    weights = (raised / jnp.sum(raised, axis=-1, keepdims=True)).astype(jnp.bfloat16)
    return jnp.dot(weights, value_rows, preferred_element_type=jnp.float32).astype(jnp.bfloat16)


def shards(queue, fresh_noise, w_mod, w_qkv, w_out, q_gain, k_gain, levels, plan, positions):
    segments = lax.axis_size("segment")
    seq_count = lax.axis_size("seq")
    segment_at = lax.axis_index("segment")
    tok_dev = queue.shape[1]
    width = queue.shape[2]
    heads_here = w_qkv.shape[2]
    head_dim = w_qkv.shape[3] // 3
    tok_frame = tok_dev * seq_count
    picked = levels[:, None] == jnp.arange(plan.shape[0], dtype=jnp.int32)[None, :]
    step_values = jnp.sum(jnp.where(picked, plan[None, :], 0), axis=1)
    embedding = jax.nn.silu(time_embedding(step_values, width)).astype(jnp.bfloat16)
    mod_part = jnp.dot(embedding, w_mod[0], preferred_element_type=jnp.float32)
    modulation = lax.all_gather(mod_part, "seq", axis=1, tiled=True)[0]
    shift_row = modulation[:width]
    scale_row = modulation[width : 2 * width]
    gate_row = modulation[2 * width :]
    resident = queue[0].astype(jnp.float32)
    modulated = (layer_norm(resident) * (1.0 + scale_row) + shift_row).astype(jnp.bfloat16)
    flat_weight = w_qkv[0].reshape(width, heads_here * 3 * head_dim)
    projected_qkv = jnp.dot(
        lax.all_gather(modulated, "seq", axis=0, tiled=True),
        flat_weight,
        preferred_element_type=jnp.float32,
    )
    projected_qkv = projected_qkv.reshape(tok_frame, heads_here, 3 * head_dim)
    angles = rope_angles(positions[0], tok_frame, head_dim, GRID_W)[:, None, :]
    queries = apply_rope(
        rms_gain(projected_qkv[..., :head_dim], q_gain[0]), angles, head_dim
    ).astype(jnp.bfloat16)
    key_rows = apply_rope(
        rms_gain(projected_qkv[..., head_dim : 2 * head_dim], k_gain[0]), angles, head_dim
    ).astype(jnp.bfloat16)
    value_rows = projected_qkv[..., 2 * head_dim :].astype(jnp.bfloat16)
    stacked = jnp.stack([key_rows, value_rows])[None]
    beside_all = with_halo(stacked, (("segment", 0),), 1)
    earlier = beside_all[0]
    following = beside_all[2]
    near_keys = jnp.concatenate([earlier[0], key_rows, following[0]], axis=0)
    near_values = jnp.concatenate([earlier[1], value_rows, following[1]], axis=0)
    filled = jnp.ones((tok_frame,), dtype=bool)
    usable = jnp.concatenate(
        [filled & (segment_at > 0), filled, filled & (segment_at < segments - 1)]
    )
    block_rows = math.gcd(tok_frame, 512)
    block_count = tok_frame // block_rows
    head_keys = near_keys[:, 0]
    head_values = near_values[:, 0]
    query_blocks = queries[:, 0].reshape(block_count, block_rows, head_dim)

    def one_block(query_rows, head_keys=head_keys, head_values=head_values):
        return attend(query_rows, head_keys, head_values, usable, head_dim)

    outputs = [lax.map(one_block, query_blocks).reshape(tok_frame, head_dim)]
    attended = jnp.stack(outputs, axis=1).reshape(tok_frame, heads_here * head_dim)
    projected = lax.psum_scatter(
        jnp.dot(attended, w_out[0], preferred_element_type=jnp.float32).astype(jnp.bfloat16),
        "seq",
        scatter_dimension=0,
        tiled=True,
    ).astype(jnp.float32)
    finished = (resident + gate_row * projected).astype(jnp.bfloat16)
    arrived = passed_along(finished, "segment", 1)
    queue_next = jnp.where(segment_at == 0, fresh_noise, arrived)[None]
    clean_whole = broadcast(finished, "segment", segments - 1)
    column_count = width // segments
    clean_frame = lax.dynamic_slice_in_dim(clean_whole, segment_at * column_count, column_count, 1)
    return (queue_next, clean_frame)


MESH = pl.DeviceIdType.MESH
PEERS = 4
MOD_CHUNKS = 6
X_CHUNKS = 4
OUT_CHUNKS = 4
LANES = 128


def fits(mesh):
    return mesh.shape["seq"] == PEERS


def rope_rows(head_dim):
    time_dim = head_dim // 8
    space_dim = (head_dim - time_dim) // 2
    rows = np.zeros((8, head_dim), np.float32)
    start = 0
    for at, section in enumerate((time_dim, space_dim, space_dim)):
        half = section // 2
        frequency = ROPE_BASE ** (-2.0 * np.arange(half) / section)
        rows[at, start : start + half] = frequency
        rows[at, start + half : start + section] = frequency
        back, forth = (3, 4) if at == 0 else (5, 6)
        rows[back, start + half : start + section] = 1.0
        rows[forth, start : start + half] = -1.0
        start += section
    return rows, time_dim // 2, space_dim // 2


def time_rates(width):
    half_width = width // 2
    return np.exp(-np.log(10000.0) * np.arange(half_width) / half_width).astype(np.float32)[None]


def block_kernel(
    segments,
    halves,
    queue,
    fresh,
    w_mod,
    w_qkv,
    w_out,
    q_gain_in,
    k_gain_in,
    levels,
    plan,
    positions,
    rates_in,
    rope_in,
    queue_next,
    clean,
    mod_w,
    qkv_w,
    out_w,
    tokens,
    mod_all,
    mod_rows,
    rates,
    rope,
    q_gain,
    k_gain,
    embedded,
    settled,
    normed,
    cosines,
    sines,
    queries,
    kv,
    ranges,
    mixes,
    own_att,
    att,
    done,
    arrived,
    small_sem,
    local_sem,
    x_send,
    x_recv,
    m_send,
    m_recv,
    h_send,
    h_recv,
    w_send,
    w_recv,
    a_send,
    a_recv,
    s_send,
    s_recv,
    c_send,
    c_recv,
    out_sem,
):
    f = lax.axis_index("segment")
    q = lax.axis_index("seq")
    last = segments - 1
    rows, width = queue.shape
    head_dim = q_gain_in.shape[1]
    mod_cols = w_mod.shape[1]
    peers = (q, q + 1 - 2 * lax.rem(q, 2), lax.rem(q + 2, 4), 3 - q)

    def remote(source, target, send, recv, device):
        return pltpu.make_async_remote_copy(
            src_ref=source,
            dst_ref=target,
            send_sem=send,
            recv_sem=recv,
            device_id=device,
            device_id_type=MESH,
        )

    barrier = pltpu.get_barrier_semaphore()
    for rel in range(1, PEERS):
        pl.semaphore_signal(barrier, inc=1, device_id=(f, peers[rel]), device_id_type=MESH)
    for step in range(1, segments):
        pl.semaphore_signal(
            barrier, inc=1, device_id=(lax.rem(f + step, segments), q), device_id_type=MESH
        )

    own_tokens = pltpu.make_async_copy(queue, tokens.at[0], local_sem.at[0])
    own_tokens.start()
    small_loads = []
    for i, (source, target) in enumerate(
        ((rates_in, rates), (rope_in, rope), (q_gain_in, q_gain), (k_gain_in, k_gain))
    ):
        load = pltpu.make_async_copy(source, target, small_sem.at[i])
        load.start()
        small_loads.append(load)
    mod_depth = width // MOD_CHUNKS
    mod_loads = []
    for i in range(MOD_CHUNKS):
        part = pl.ds(i * mod_depth, mod_depth)
        load = pltpu.make_async_copy(w_mod.at[part], mod_w.at[part], local_sem.at[1 + i])
        load.start()
        mod_loads.append(load)
    qkv_load = pltpu.make_async_copy(w_qkv, qkv_w, local_sem.at[1 + MOD_CHUNKS])
    qkv_load.start()
    out_load = pltpu.make_async_copy(w_out, out_w.at[0], local_sem.at[2 + MOD_CHUNKS])
    out_load.start()

    pl.semaphore_wait(barrier, PEERS - 1 + segments - 1)

    own_tokens.wait()

    piece = rows // X_CHUNKS
    mirror_x = []
    for i in range(X_CHUNKS):
        part = pl.ds(i * piece, piece)
        copy = remote(
            tokens.at[0, part], tokens.at[2, part], x_send.at[i], x_recv.at[i], (f, peers[2])
        )
        copy.start()
        mirror_x.append(copy)
    sibling_x = remote(
        tokens.at[0], tokens.at[1], x_send.at[X_CHUNKS], x_recv.at[X_CHUNKS], (f, peers[1])
    )
    sibling_x.start()
    fresh_copy = pltpu.make_async_copy(fresh, arrived, local_sem.at[3 + MOD_CHUNKS])

    @pl.when(f == 0)
    def _():
        fresh_copy.start()

    for load in small_loads:
        load.wait()
    step_value = plan[levels[0]].astype(jnp.float32)
    angles = rates[...] * step_value
    embedding = jnp.concatenate([jnp.cos(angles), jnp.sin(angles)], axis=1)
    embedding = embedding / (1.0 + jnp.exp(-embedding))
    embedding = embedding.astype(jnp.bfloat16).astype(jnp.float32)
    for start in range(0, width, LANES):
        entries = jnp.broadcast_to(embedding[:, start : start + LANES], (LANES, LANES))
        embedded[start : start + LANES, :] = entries.T
    tiles = mod_cols // LANES

    def add_rows(i, totals):
        offset = pl.multiple_of(i * 16, 16)
        entries = embedded[pl.ds(offset, 16), :]
        sums = []
        for tile in range(tiles):
            lanes = slice(tile * LANES, (tile + 1) * LANES)
            product = mod_w[pl.ds(offset, 16), lanes].astype(jnp.float32) * entries
            sums.append(totals[tile] + (product[:8] + product[8:]))
        return tuple(sums)

    totals = tuple(jnp.zeros((8, LANES), jnp.float32) for _ in range(tiles))
    steps = mod_depth // 16
    for i in range(MOD_CHUNKS):
        mod_loads[i].wait()
        totals = lax.fori_loop(i * steps, (i + 1) * steps, add_rows, totals, unroll=4)
    mod_all[q] = jnp.concatenate(
        [jnp.sum(total, axis=0, keepdims=True) for total in totals], axis=1
    )
    mod_copies = []
    for rel in range(1, PEERS):
        copy = remote(
            mod_all.at[q], mod_all.at[q], m_send.at[rel], m_recv.at[rel], (f, peers[rel])
        )
        copy.start()
        mod_copies.append(copy)

    position = positions[0].astype(jnp.float32)
    grid_col = lax.broadcasted_iota(jnp.int32, (GRID_W, head_dim), 0).astype(jnp.float32)
    col_turn = grid_col * rope[2:3]
    col_cos = jnp.cos(col_turn)
    col_sin = jnp.sin(col_turn)
    by_col = lax.broadcasted_iota(jnp.int32, (GRID_W, head_dim), 1) >= head_dim - 2 * halves[1]
    rows_here = rows // GRID_W
    for rel in range(PEERS):
        grid_row = lax.broadcasted_iota(jnp.int32, (8, head_dim), 0) + peers[rel] * rows_here
        row_turn = position * rope[0:1] + grid_row.astype(jnp.float32) * rope[1:2]
        row_cos = jnp.cos(row_turn)
        row_sin = jnp.sin(row_turn)
        for r in range(rows_here):
            part = slice(r * GRID_W, (r + 1) * GRID_W)
            cosines[rel, part, :] = jnp.where(by_col, col_cos, row_cos[r : r + 1])
            sines[rel, part, :] = jnp.where(by_col, col_sin, row_sin[r : r + 1])

    forwards = []

    def forward_tokens(i):
        mirror_x[i].wait_recv()
        part = pl.ds(i * piece, piece)
        copy = remote(
            tokens.at[2, part],
            tokens.at[3, part],
            x_send.at[X_CHUNKS + 1 + i],
            x_recv.at[X_CHUNKS + 1 + i],
            (f, peers[1]),
        )
        copy.start()
        forwards.append(copy)

    def settle(x):
        x = x.astype(jnp.float32)
        x = x - jnp.mean(x, axis=1, keepdims=True)
        return x * lax.rsqrt(jnp.mean(x * x, axis=1, keepdims=True) + EPSILON)

    def modulate(x):
        return (x * mod_rows[:, width : 2 * width] + mod_rows[:, :width]).astype(jnp.bfloat16)

    forward_tokens(0)
    sibling_x.wait_recv()
    for rel in range(2):

        def settle_rows(i, carry, rel=rel):
            offset = pl.multiple_of(i * 16, 16)
            settled[pl.ds(rel * rows + offset, 16), :] = settle(tokens[rel, pl.ds(offset, 16), :])
            return carry

        lax.fori_loop(0, rows // 16, settle_rows, 0, unroll=4)
    forward_tokens(1)
    qkv_load.wait()
    out_load.wait()
    for copy in mod_copies:
        copy.wait()
    for peer in range(PEERS):
        mod_rows[:, peer * mod_cols : (peer + 1) * mod_cols] = mod_all[peer]
    mod_rows[:, width : 2 * width] = 1.0 + mod_rows[:, width : 2 * width]

    def modulate_rows(i, carry):
        offset = pl.multiple_of(i * 16, 16)
        normed[pl.ds(offset, 16), :] = modulate(settled[pl.ds(offset, 16), :])
        return carry

    lax.fori_loop(0, 2 * rows // 16, modulate_rows, 0, unroll=4)

    def norm_piece(rel, start, size, at):
        def norm_rows(i, carry):
            offset = pl.multiple_of(i * 16, 16)
            x = settle(tokens[rel, pl.ds(start + offset, 16), :])
            normed[pl.ds(at + offset, 16), :] = modulate(x)
            return carry

        lax.fori_loop(0, size // 16, norm_rows, 0, unroll=True)

    score_scale = head_dim ** (-0.5) * math.log2(math.e)
    halo = []

    def project(pieces, task):
        at = sum(size for _, _, size in pieces)
        base = (0, 2 * rows, 3 * rows)[task]
        joined = jnp.dot(normed[:at, :], qkv_w[...], preferred_element_type=jnp.float32)
        at = 0
        for rel, start, size in pieces:
            cos = cosines[rel, start : start + size, :]
            sin = sines[rel, start : start + size, :]

            def turned(x, gain):
                x = x * lax.rsqrt(jnp.mean(x * x, axis=1, keepdims=True) + EPSILON) * gain
                swapped = (
                    pltpu.roll(x, halves[0], 1) * rope[3:4]
                    + pltpu.roll(x, head_dim - halves[0], 1) * rope[4:5]
                    + pltpu.roll(x, halves[1], 1) * rope[5:6]
                    + pltpu.roll(x, head_dim - halves[1], 1) * rope[6:7]
                )
                return (x * cos + swapped * sin).astype(jnp.bfloat16)

            own = joined[at : at + size]
            queries[base + at : base + at + size, :] = turned(
                own[:, :head_dim], q_gain[...] * score_scale
            )
            kv[1, 0, base + at : base + at + size, :] = turned(
                own[:, head_dim : 2 * head_dim], k_gain[...]
            )
            kv[1, 1, base + at : base + at + size, :] = own[:, 2 * head_dim :].astype(
                jnp.bfloat16
            )
            at += size
        part = pl.ds(base, at)
        forth = remote(
            kv.at[1, :, part],
            kv.at[0, :, part],
            h_send.at[0, task],
            h_recv.at[0, task],
            (lax.rem(f + 1, segments), q),
        )
        back = remote(
            kv.at[1, :, part],
            kv.at[2, :, part],
            h_send.at[1, task],
            h_recv.at[1, task],
            (lax.rem(f + segments - 1, segments), q),
        )

        @pl.when(f < last)
        def _():
            forth.start()

        @pl.when(f > 0)
        def _():
            back.start()

        halo.append((forth, back))

    cols = width // OUT_CHUNKS
    mirror_w = []

    def send_weights(i):
        part = pl.ds(i * cols, cols)
        copy = remote(
            out_w.at[0, :, part],
            out_w.at[2, :, part],
            w_send.at[i],
            w_recv.at[i],
            (f, peers[2]),
        )
        copy.start()
        mirror_w.append(copy)

    sibling_w = remote(
        out_w.at[0], out_w.at[1], w_send.at[OUT_CHUNKS], w_recv.at[OUT_CHUNKS], (f, peers[1])
    )
    counted = (
        jnp.where(f > 0, 1.0, 0.0).astype(jnp.float32),
        jnp.float32(1.0),
        jnp.where(f < last, 1.0, 0.0).astype(jnp.float32),
    )

    def wait_halo(task):
        forth, back = halo[task]
        begin = (0, 2 * rows, 3 * rows)[task]
        size = (2 * rows, rows, rows)[task]
        part = slice(begin, begin + size)

        @pl.when(f > 0)
        def _():
            forth.wait_recv()

        @pl.when(f < last)
        def _():
            back.wait_recv()

        for edge, side in ((0, 0), (last, 2)):

            @pl.when(f == edge)
            def _(side=side):
                kv[side, 0, part, :] = kv[1, 0, part, :]
                kv[side, 1, part, :] = jnp.zeros((size, head_dim), jnp.bfloat16)

    def attend_to(block, begin, size):
        own = queries[block * rows : (block + 1) * rows, :]
        scores = [
            lax.dot_general(
                own,
                kv[side, 0, begin : begin + size, :],
                (((1,), (1,)), ((), ())),
                preferred_element_type=jnp.float32,
            )
            for side in range(3)
        ]
        top = jnp.max(
            jnp.maximum(jnp.maximum(scores[0], scores[2]), scores[1]), axis=1, keepdims=True
        )
        return scores, top

    def mix(scores, top, begin, size):
        weight = jnp.zeros((rows, 1), jnp.float32)
        mixed = jnp.zeros((rows, head_dim), jnp.float32)
        for side in range(3):
            raised = jnp.exp2(scores[side] - top)
            weight = weight + counted[side] * jnp.sum(raised, axis=1, keepdims=True)
            mixed = mixed + jnp.dot(
                raised.astype(jnp.bfloat16),
                kv[side, 1, begin : begin + size, :],
                preferred_element_type=jnp.float32,
            )
        return weight, mixed

    early = 3 * rows

    def attend_early(block):
        part = slice(block * rows, (block + 1) * rows)
        scores, top = attend_to(block, 0, early)
        weight, mixed = mix(scores, top, 0, early)
        ranges[0, part, :] = jnp.broadcast_to(top, (rows, head_dim))
        ranges[1, part, :] = jnp.broadcast_to(weight, (rows, head_dim))
        mixes[part, :] = mixed

    def attend_late(block):
        part = slice(block * rows, (block + 1) * rows)
        scores, late_top = attend_to(block, early, rows)
        early_top = ranges[0, part, :]
        top = jnp.maximum(early_top, late_top)
        weight, mixed = mix(scores, top[:, :1], early, rows)
        keep = jnp.exp2(early_top - top)
        weight = weight + ranges[1, part, :] * keep
        return ((mixed + mixes[part, :] * keep) / weight).astype(jnp.bfloat16)

    project([(0, 0, rows), (1, 0, rows)], 0)
    half = rows // 2
    forward_tokens(2)
    send_weights(0)
    for i in range(2):
        forwards[i].wait_recv()
        norm_piece(2, i * piece, piece, i * piece)
        norm_piece(3, i * piece, piece, half + i * piece)
    project([(2, 0, half), (3, 0, half)], 1)
    send_weights(1)
    norm_piece(2, half, piece, 0)
    forwards[2].wait_recv()
    norm_piece(3, half, piece, half)
    wait_halo(0)
    wait_halo(1)
    attend_early(0)
    forward_tokens(3)
    send_weights(2)
    send_weights(3)
    norm_piece(2, half + piece, piece, piece)
    forwards[3].wait_recv()
    norm_piece(3, half + piece, piece, half + piece)
    project([(2, half, half), (3, half, half)], 2)
    sibling_w.start()
    attend_early(1)
    attend_early(2)
    attend_early(3)
    wait_halo(2)
    att_copies = []
    both = [attend_late(2), attend_late(3)]
    for rel in (3, 2, 1):
        if rel == 1:
            own_att[1] = attend_late(1)
        else:
            part = slice((rel - 2) * half, (rel - 1) * half)
            own_att[rel, :half, :] = both[0][part]
            own_att[rel, half:, :] = both[1][part]
        copy = remote(own_att.at[rel], att.at[rel], a_send.at[rel], a_recv.at[rel], (f, peers[rel]))
        copy.start()
        att_copies.append(copy)
    att[0] = attend_late(0)

    forward_w = []

    def forward_weights(i):
        mirror_w[i].wait_recv()
        part = pl.ds(i * cols, cols)
        copy = remote(
            out_w.at[2, :, part],
            out_w.at[3, :, part],
            w_send.at[OUT_CHUNKS + 1 + i],
            w_recv.at[OUT_CHUNKS + 1 + i],
            (f, peers[1]),
        )
        copy.start()
        forward_w.append(copy)

    forward_weights(0)
    sibling_w.wait_recv()
    for copy in att_copies:
        copy.wait_recv()
    mixed = jnp.concatenate([att[rel] for rel in range(PEERS)], axis=1)

    clean_cols = width // segments
    shifts = []
    cleans = []
    for i in range(OUT_CHUNKS):
        if i + 1 < OUT_CHUNKS:
            forward_weights(i + 1)
        forward_w[i].wait_recv()
        begin = i * cols
        part = pl.ds(begin, cols)
        projected = jnp.dot(
            mixed,
            out_w[:, :, begin : begin + cols].reshape(PEERS * rows, cols),
            preferred_element_type=jnp.float32,
        )
        gate = mod_rows[:, 2 * width + begin : 2 * width + begin + cols]
        kept = tokens[0, :, begin : begin + cols].astype(jnp.float32)
        done[:, begin : begin + cols] = (kept + gate * projected).astype(jnp.bfloat16)
        shift = remote(
            done.at[:, part],
            arrived.at[:, part],
            s_send.at[i],
            s_recv.at[i],
            (lax.rem(f + 1, segments), q),
        )
        shifts.append(shift)

        @pl.when(f < last)
        def _(shift=shift):
            shift.start()

        for to in range(begin // clean_cols, (begin + cols) // clean_cols):
            from_cols = done.at[:, pl.ds(to * clean_cols, clean_cols)]
            if to < last:
                clean_copy = remote(from_cols, clean, c_send.at[to], c_recv, (to, q))
            else:
                clean_copy = pltpu.make_async_copy(from_cols, clean, c_send.at[to])
            cleans.append(clean_copy)

            @pl.when(f == last)
            def _(clean_copy=clean_copy):
                clean_copy.start()

    for copy in mirror_x + [sibling_x] + forwards + mirror_w + [sibling_w] + forward_w + att_copies:
        copy.wait_send()
    for forth, back in halo:

        @pl.when(f < last)
        def _(forth=forth):
            forth.wait_send()

        @pl.when(f > 0)
        def _(back=back):
            back.wait_send()

    @pl.when(f == 0)
    def _():
        fresh_copy.wait()

    written = []
    for i, shift in enumerate(shifts):

        @pl.when(f > 0)
        def _(shift=shift):
            shift.wait_recv()

        part = pl.ds(i * cols, cols)
        copy = pltpu.make_async_copy(
            arrived.at[:, part], queue_next.at[:, part], out_sem.at[i]
        )
        copy.start()
        written.append(copy)
    for copy in written:
        copy.wait()
    for shift in shifts:

        @pl.when(f < last)
        def _(shift=shift):
            shift.wait_send()

    @pl.when(f == last)
    def _():
        for clean_copy in cleans[:-1]:
            clean_copy.wait_send()
        cleans[-1].wait()

    @pl.when(f < last)
    def _():
        cleans[0].wait_recv()


def hand_over(queue_in, clean_in, queue_next, clean, queue_held, clean_held, sem_in, sem_out):
    piece = queue_in.shape[0] // X_CHUNKS
    steps = []
    for i in range(X_CHUNKS):
        part = pl.ds(i * piece, piece)
        steps.append((queue_in.at[part], queue_held.at[part], queue_next.at[part]))
    steps.append((clean_in, clean_held, clean))
    reads = []
    for i, (source, held, _) in enumerate(steps):
        copy = pltpu.make_async_copy(source, held, sem_in.at[i])
        copy.start()
        reads.append(copy)
    writes = []
    for i, (_, held, target) in enumerate(steps):
        reads[i].wait()
        copy = pltpu.make_async_copy(held, target, sem_out.at[i])
        copy.start()
        writes.append(copy)
    for copy in writes:
        copy.wait()


def fused(
    mesh, queue, fresh_noise, w_mod, w_qkv, w_out, q_gain, k_gain, levels, plan, positions
):
    segments = mesh.shape["segment"]
    rows, width = queue.shape[1:]
    mod_cols = w_mod.shape[2]
    head_dim = q_gain.shape[1]
    rope, *halves = rope_rows(head_dim)
    scalars = pl.BlockSpec(memory_space=pltpu.SMEM)
    outside = pl.BlockSpec(memory_space=pl.ANY)
    bf16, f32 = jnp.bfloat16, jnp.float32
    dma = pltpu.SemaphoreType.DMA
    queue_next, clean_frame = pl.pallas_call(
        functools.partial(block_kernel, segments, tuple(halves)),
        out_shape=(
            jax.ShapeDtypeStruct((rows, width), bf16),
            jax.ShapeDtypeStruct((rows, width // segments), bf16),
        ),
        in_specs=[outside] * 7 + [scalars] * 3 + [outside] * 2,
        out_specs=(outside, outside),
        scratch_shapes=[
            pltpu.VMEM((width, mod_cols), bf16),
            pltpu.VMEM((width, 3 * head_dim), bf16),
            pltpu.VMEM((PEERS, rows, width), bf16),
            pltpu.VMEM((PEERS, rows, width), bf16),
            pltpu.VMEM((PEERS, 1, mod_cols), f32),
            pltpu.VMEM((1, 3 * width), f32),
            pltpu.VMEM((1, width // 2), f32),
            pltpu.VMEM((8, head_dim), f32),
            pltpu.VMEM((1, head_dim), f32),
            pltpu.VMEM((1, head_dim), f32),
            pltpu.VMEM((width, LANES), f32),
            pltpu.VMEM((2 * rows, width), f32),
            pltpu.VMEM((2 * rows, width), bf16),
            pltpu.VMEM((PEERS, rows, head_dim), f32),
            pltpu.VMEM((PEERS, rows, head_dim), f32),
            pltpu.VMEM((PEERS * rows, head_dim), bf16),
            pltpu.VMEM((3, 2, PEERS * rows, head_dim), bf16),
            pltpu.VMEM((2, PEERS * rows, head_dim), f32),
            pltpu.VMEM((PEERS * rows, head_dim), f32),
            pltpu.VMEM((PEERS, rows, head_dim), bf16),
            pltpu.VMEM((PEERS, rows, head_dim), bf16),
            pltpu.VMEM((rows, width), bf16),
            pltpu.VMEM((rows, width), bf16),
            dma((4,)),
            dma((4 + MOD_CHUNKS,)),
            dma((2 * X_CHUNKS + 1,)),
            dma((2 * X_CHUNKS + 1,)),
            dma((PEERS,)),
            dma((PEERS,)),
            dma((2, 3)),
            dma((2, 3)),
            dma((2 * OUT_CHUNKS + 1,)),
            dma((2 * OUT_CHUNKS + 1,)),
            dma((PEERS,)),
            dma((PEERS,)),
            dma((OUT_CHUNKS,)),
            dma((OUT_CHUNKS,)),
            dma((segments,)),
            dma(()),
            dma((OUT_CHUNKS,)),
        ],
        compiler_params=pltpu.CompilerParams(
            collective_id=0, has_side_effects=True, vmem_limit_bytes=56 * 1024 * 1024
        ),
        cost_estimate=pl.CostEstimate(
            flops=2 * 10**9, bytes_accessed=22 * 10**6, transcendentals=10**6
        ),
        name="relayed_block",
    )(
        queue[0],
        fresh_noise,
        w_mod[0],
        w_qkv.reshape(width, 3 * head_dim),
        w_out[0],
        q_gain,
        k_gain,
        levels,
        plan,
        positions,
        jnp.asarray(time_rates(width)),
        jnp.asarray(rope),
    )
    queue_next, clean_frame = pl.pallas_call(
        hand_over,
        out_shape=(
            jax.ShapeDtypeStruct(queue_next.shape, bf16),
            jax.ShapeDtypeStruct(clean_frame.shape, bf16),
        ),
        in_specs=[outside] * 2,
        out_specs=(outside, outside),
        scratch_shapes=[
            pltpu.VMEM(queue_next.shape, bf16),
            pltpu.VMEM(clean_frame.shape, bf16),
            dma((X_CHUNKS + 1,)),
            dma((X_CHUNKS + 1,)),
        ],
        compiler_params=pltpu.CompilerParams(vmem_limit_bytes=56 * 1024 * 1024),
        name="hand_over",
    )(queue_next, clean_frame)
    return queue_next[None], clean_frame


def solution(mesh):
    placed = (
        P("segment", "seq", None),
        P("seq", None),
        P("segment", None, "seq"),
        P("segment", None, "seq", None),
        P("segment", "seq", None),
        P("segment", None),
        P("segment", None),
        P("segment"),
        P(),
        P("segment"),
    )
    return jax.shard_map(
        functools.partial(fused, mesh) if fits(mesh) else shards,
        mesh=mesh,
        in_specs=placed,
        out_specs=(P("segment", "seq", None), P("seq", "segment")),
        check_vma=False,
    )
```

```python
import functools
import math

import jax
import jax.numpy as jnp
from jax import lax
import numpy as np
from jax.experimental import pallas as pl
from jax.experimental.pallas import tpu as pltpu
from jax.sharding import PartitionSpec as P

GRID_W = 32


EPSILON = 1e-06
ROPE_BASE = 256.0


def with_halo(cells, sides, width):
    for axis, dim in sides:
        count = lax.axis_size(axis)
        ends = count - 1
        head = lax.slice_in_dim(cells, 0, width, axis=dim)
        tail = lax.slice_in_dim(cells, cells.shape[dim] - width, cells.shape[dim], axis=dim)
        cells = jnp.concatenate(
            [
                lax.ppermute(tail, axis, [(i, (i + 1) % count) for i in range(ends)]),
                cells,
                lax.ppermute(head, axis, [((i + 1) % count, i) for i in range(ends)]),
            ],
            axis=dim,
        )
    return cells


def passed_along(value, axis, by):
    length = lax.axis_size(axis)
    pairs = [(i, i + by) for i in range(length) if 0 <= i + by < length]
    return lax.ppermute(value, axis, pairs)


def broadcast(value, axis, root):
    mine = lax.axis_index(axis) == root
    return lax.psum(jnp.where(mine, value, jnp.zeros_like(value)), axis)


def time_embedding(step_values, width):
    half_width = width // 2
    counter = jnp.arange(half_width, dtype=jnp.float32)
    frequency = jnp.exp(-jnp.log(10000.0) * counter / half_width)
    angles = step_values.astype(jnp.float32)[:, None] * frequency[None, :]
    return jnp.concatenate([jnp.cos(angles), jnp.sin(angles)], axis=-1)


def rope_angles(frame_position, row_count, head_dim, grid_width):
    time_dim = head_dim // 8
    space_dim = (head_dim - time_dim) // 2
    tokens_at = jnp.arange(row_count, dtype=jnp.int32)
    grid_row = (tokens_at // grid_width).astype(jnp.float32)
    grid_col = (tokens_at % grid_width).astype(jnp.float32)
    moment = jnp.zeros((row_count,), jnp.float32) + frame_position.astype(jnp.float32)
    sections = []
    for coords, section in ((moment, time_dim), (grid_row, space_dim), (grid_col, space_dim)):
        half_size = section // 2
        frequency = ROPE_BASE ** (-2.0 * jnp.arange(half_size, dtype=jnp.float32) / section)
        angles = coords[:, None] * frequency[None, :]
        sections.append(jnp.concatenate([angles, angles], axis=-1))
    return jnp.concatenate(sections, axis=-1)


def rotate_half(values, head_dim):
    time_dim = head_dim // 8
    space_dim = (head_dim - time_dim) // 2
    pieces_out = []
    position = 0
    for section in (time_dim, space_dim, space_dim):
        half_size = section // 2
        leading = values[..., position : position + half_size]
        second = values[..., position + half_size : position + section]
        pieces_out.append(jnp.concatenate([-second, leading], axis=-1))
        position += section
    return jnp.concatenate(pieces_out, axis=-1)


def apply_rope(values, angles, head_dim):
    return values * jnp.cos(angles) + rotate_half(values, head_dim) * jnp.sin(angles)


def rms_gain(values, gains):
    mean_square = jnp.mean(values * values, axis=-1, keepdims=True)
    return values * lax.rsqrt(mean_square + EPSILON) * gains


def layer_norm(values):
    centre = jnp.mean(values, axis=-1, keepdims=True)
    spread = jnp.mean(jnp.square(values - centre), axis=-1, keepdims=True)
    return (values - centre) * lax.rsqrt(spread + EPSILON)


def attend(query_rows, key_rows, value_rows, usable, head_dim):
    scores = jnp.dot(query_rows, key_rows.T, preferred_element_type=jnp.float32) * head_dim ** (
        -0.5
    )
    scores = jnp.where(usable[None, :], scores, -jnp.inf)
    row_max = jnp.max(scores, axis=-1, keepdims=True)
    raised = jnp.exp(scores - row_max)
    weights = (raised / jnp.sum(raised, axis=-1, keepdims=True)).astype(jnp.bfloat16)
    return jnp.dot(weights, value_rows, preferred_element_type=jnp.float32).astype(jnp.bfloat16)


def shards(queue, fresh_noise, w_mod, w_qkv, w_out, q_gain, k_gain, levels, plan, positions):
    segments = lax.axis_size("segment")
    seq_count = lax.axis_size("seq")
    segment_at = lax.axis_index("segment")
    tok_dev = queue.shape[1]
    width = queue.shape[2]
    heads_here = w_qkv.shape[2]
    head_dim = w_qkv.shape[3] // 3
    tok_frame = tok_dev * seq_count
    picked = levels[:, None] == jnp.arange(plan.shape[0], dtype=jnp.int32)[None, :]
    step_values = jnp.sum(jnp.where(picked, plan[None, :], 0), axis=1)
    embedding = jax.nn.silu(time_embedding(step_values, width)).astype(jnp.bfloat16)
    mod_part = jnp.dot(embedding, w_mod[0], preferred_element_type=jnp.float32)
    modulation = lax.all_gather(mod_part, "seq", axis=1, tiled=True)[0]
    shift_row = modulation[:width]
    scale_row = modulation[width : 2 * width]
    gate_row = modulation[2 * width :]
    resident = queue[0].astype(jnp.float32)
    modulated = (layer_norm(resident) * (1.0 + scale_row) + shift_row).astype(jnp.bfloat16)
    flat_weight = w_qkv[0].reshape(width, heads_here * 3 * head_dim)
    projected_qkv = jnp.dot(
        lax.all_gather(modulated, "seq", axis=0, tiled=True),
        flat_weight,
        preferred_element_type=jnp.float32,
    )
    projected_qkv = projected_qkv.reshape(tok_frame, heads_here, 3 * head_dim)
    angles = rope_angles(positions[0], tok_frame, head_dim, GRID_W)[:, None, :]
    queries = apply_rope(
        rms_gain(projected_qkv[..., :head_dim], q_gain[0]), angles, head_dim
    ).astype(jnp.bfloat16)
    key_rows = apply_rope(
        rms_gain(projected_qkv[..., head_dim : 2 * head_dim], k_gain[0]), angles, head_dim
    ).astype(jnp.bfloat16)
    value_rows = projected_qkv[..., 2 * head_dim :].astype(jnp.bfloat16)
    stacked = jnp.stack([key_rows, value_rows])[None]
    beside_all = with_halo(stacked, (("segment", 0),), 1)
    earlier = beside_all[0]
    following = beside_all[2]
    near_keys = jnp.concatenate([earlier[0], key_rows, following[0]], axis=0)
    near_values = jnp.concatenate([earlier[1], value_rows, following[1]], axis=0)
    filled = jnp.ones((tok_frame,), dtype=bool)
    usable = jnp.concatenate(
        [filled & (segment_at > 0), filled, filled & (segment_at < segments - 1)]
    )
    block_rows = math.gcd(tok_frame, 512)
    block_count = tok_frame // block_rows
    head_keys = near_keys[:, 0]
    head_values = near_values[:, 0]
    query_blocks = queries[:, 0].reshape(block_count, block_rows, head_dim)

    def one_block(query_rows, head_keys=head_keys, head_values=head_values):
        return attend(query_rows, head_keys, head_values, usable, head_dim)

    outputs = [lax.map(one_block, query_blocks).reshape(tok_frame, head_dim)]
    attended = jnp.stack(outputs, axis=1).reshape(tok_frame, heads_here * head_dim)
    projected = lax.psum_scatter(
        jnp.dot(attended, w_out[0], preferred_element_type=jnp.float32).astype(jnp.bfloat16),
        "seq",
        scatter_dimension=0,
        tiled=True,
    ).astype(jnp.float32)
    finished = (resident + gate_row * projected).astype(jnp.bfloat16)
    arrived = passed_along(finished, "segment", 1)
    queue_next = jnp.where(segment_at == 0, fresh_noise, arrived)[None]
    clean_whole = broadcast(finished, "segment", segments - 1)
    column_count = width // segments
    clean_frame = lax.dynamic_slice_in_dim(clean_whole, segment_at * column_count, column_count, 1)
    return (queue_next, clean_frame)


MESH = pl.DeviceIdType.MESH
PEERS = 4
MOD_CHUNKS = 6
X_CHUNKS = 4
OUT_CHUNKS = 4
LANES = 128


def fits(mesh):
    return mesh.shape["seq"] == PEERS


def rope_rows(head_dim):
    time_dim = head_dim // 8
    space_dim = (head_dim - time_dim) // 2
    rows = np.zeros((8, head_dim), np.float32)
    start = 0
    for at, section in enumerate((time_dim, space_dim, space_dim)):
        half = section // 2
        frequency = ROPE_BASE ** (-2.0 * np.arange(half) / section)
        rows[at, start : start + half] = frequency
        rows[at, start + half : start + section] = frequency
        back, forth = (3, 4) if at == 0 else (5, 6)
        rows[back, start + half : start + section] = 1.0
        rows[forth, start : start + half] = -1.0
        start += section
    return rows, time_dim // 2, space_dim // 2


def time_rates(width):
    half_width = width // 2
    return np.exp(-np.log(10000.0) * np.arange(half_width) / half_width).astype(np.float32)[None]


def block_kernel(
    segments,
    halves,
    queue,
    fresh,
    w_mod,
    w_qkv,
    w_out,
    q_gain_in,
    k_gain_in,
    levels,
    plan,
    positions,
    rates_in,
    rope_in,
    queue_next,
    clean,
    mod_w,
    qkv_w,
    out_w,
    tokens,
    mod_all,
    mod_rows,
    rates,
    rope,
    q_gain,
    k_gain,
    embedded,
    kept,
    normed,
    cosines,
    sines,
    queries,
    kv,
    ranges,
    mixes,
    own_att,
    att,
    done,
    arrived,
    small_sem,
    local_sem,
    x_send,
    x_recv,
    m_send,
    m_recv,
    h_send,
    h_recv,
    w_send,
    w_recv,
    a_send,
    a_recv,
    s_send,
    s_recv,
    c_send,
    c_recv,
    out_sem,
):
    f = lax.axis_index("segment")
    q = lax.axis_index("seq")
    last = segments - 1
    rows, width = queue.shape
    head_dim = q_gain_in.shape[1]
    mod_cols = w_mod.shape[1]
    peers = (q, q + 1 - 2 * lax.rem(q, 2), lax.rem(q + 2, 4), 3 - q)

    def remote(source, target, send, recv, device):
        return pltpu.make_async_remote_copy(
            src_ref=source,
            dst_ref=target,
            send_sem=send,
            recv_sem=recv,
            device_id=device,
            device_id_type=MESH,
        )

    barrier = pltpu.get_barrier_semaphore()
    for rel in range(1, PEERS):
        pl.semaphore_signal(barrier, inc=1, device_id=(f, peers[rel]), device_id_type=MESH)
    for step in range(1, segments):
        pl.semaphore_signal(
            barrier, inc=1, device_id=(lax.rem(f + step, segments), q), device_id_type=MESH
        )

    own_tokens = pltpu.make_async_copy(queue, kept, local_sem.at[0])
    own_tokens.start()
    small_loads = []
    for i, (source, target) in enumerate(
        ((rates_in, rates), (rope_in, rope), (q_gain_in, q_gain), (k_gain_in, k_gain))
    ):
        load = pltpu.make_async_copy(source, target, small_sem.at[i])
        load.start()
        small_loads.append(load)
    mod_depth = width // MOD_CHUNKS
    mod_loads = []
    for i in range(MOD_CHUNKS):
        part = pl.ds(i * mod_depth, mod_depth)
        load = pltpu.make_async_copy(w_mod.at[part], mod_w.at[part], local_sem.at[1 + i])
        load.start()
        mod_loads.append(load)
    qkv_load = pltpu.make_async_copy(w_qkv, qkv_w, local_sem.at[1 + MOD_CHUNKS])
    qkv_load.start()
    out_load = pltpu.make_async_copy(w_out, out_w.at[0], local_sem.at[2 + MOD_CHUNKS])
    out_load.start()

    pl.semaphore_wait(barrier, PEERS - 1 + segments - 1)

    own_tokens.wait()

    def settle_rows(i, carry):
        offset = pl.multiple_of(i * 16, 16)
        x = kept[pl.ds(offset, 16), :].astype(jnp.float32)
        x = x - jnp.mean(x, axis=1, keepdims=True)
        x = x * lax.rsqrt(jnp.mean(x * x, axis=1, keepdims=True) + EPSILON)
        tokens[0, pl.ds(offset, 16), :] = x.astype(jnp.bfloat16)
        return carry

    piece = rows // X_CHUNKS
    mirror_x = []
    for i in range(X_CHUNKS):
        lax.fori_loop(i * piece // 16, (i + 1) * piece // 16, settle_rows, 0, unroll=True)
        part = pl.ds(i * piece, piece)
        copy = remote(
            tokens.at[0, part], tokens.at[2, part], x_send.at[i], x_recv.at[i], (f, peers[2])
        )
        copy.start()
        mirror_x.append(copy)
    sibling_x = remote(
        tokens.at[0], tokens.at[1], x_send.at[X_CHUNKS], x_recv.at[X_CHUNKS], (f, peers[1])
    )
    sibling_x.start()
    fresh_copy = pltpu.make_async_copy(fresh, arrived, local_sem.at[3 + MOD_CHUNKS])

    @pl.when(f == 0)
    def _():
        fresh_copy.start()

    for load in small_loads:
        load.wait()
    step_value = plan[levels[0]].astype(jnp.float32)
    angles = rates[...] * step_value
    embedding = jnp.concatenate([jnp.cos(angles), jnp.sin(angles)], axis=1)
    embedding = embedding / (1.0 + jnp.exp(-embedding))
    embedding = embedding.astype(jnp.bfloat16).astype(jnp.float32)
    for start in range(0, width, LANES):
        entries = jnp.broadcast_to(embedding[:, start : start + LANES], (LANES, LANES))
        embedded[start : start + LANES, :] = entries.T
    tiles = mod_cols // LANES

    def add_rows(i, totals):
        offset = pl.multiple_of(i * 16, 16)
        entries = embedded[pl.ds(offset, 16), :]
        sums = []
        for tile in range(tiles):
            lanes = slice(tile * LANES, (tile + 1) * LANES)
            product = mod_w[pl.ds(offset, 16), lanes].astype(jnp.float32) * entries
            sums.append(totals[tile] + (product[:8] + product[8:]))
        return tuple(sums)

    totals = tuple(jnp.zeros((8, LANES), jnp.float32) for _ in range(tiles))
    steps = mod_depth // 16
    for i in range(MOD_CHUNKS):
        mod_loads[i].wait()
        totals = lax.fori_loop(i * steps, (i + 1) * steps, add_rows, totals, unroll=4)
    mod_all[q] = jnp.concatenate(
        [jnp.sum(total, axis=0, keepdims=True) for total in totals], axis=1
    )
    mod_copies = []
    for rel in range(1, PEERS):
        copy = remote(
            mod_all.at[q], mod_all.at[q], m_send.at[rel], m_recv.at[rel], (f, peers[rel])
        )
        copy.start()
        mod_copies.append(copy)

    position = positions[0].astype(jnp.float32)
    grid_col = lax.broadcasted_iota(jnp.int32, (GRID_W, head_dim), 0).astype(jnp.float32)
    col_turn = grid_col * rope[2:3]
    col_cos = jnp.cos(col_turn)
    col_sin = jnp.sin(col_turn)
    by_col = lax.broadcasted_iota(jnp.int32, (GRID_W, head_dim), 1) >= head_dim - 2 * halves[1]
    rows_here = rows // GRID_W
    for rel in range(PEERS):
        grid_row = lax.broadcasted_iota(jnp.int32, (8, head_dim), 0) + peers[rel] * rows_here
        row_turn = position * rope[0:1] + grid_row.astype(jnp.float32) * rope[1:2]
        row_cos = jnp.cos(row_turn)
        row_sin = jnp.sin(row_turn)
        for r in range(rows_here):
            part = slice(r * GRID_W, (r + 1) * GRID_W)
            cosines[rel, part, :] = jnp.where(by_col, col_cos, row_cos[r : r + 1])
            sines[rel, part, :] = jnp.where(by_col, col_sin, row_sin[r : r + 1])

    forwards = []

    def forward_tokens(i):
        mirror_x[i].wait_recv()
        part = pl.ds(i * piece, piece)
        copy = remote(
            tokens.at[2, part],
            tokens.at[3, part],
            x_send.at[X_CHUNKS + 1 + i],
            x_recv.at[X_CHUNKS + 1 + i],
            (f, peers[1]),
        )
        copy.start()
        forwards.append(copy)

    forward_tokens(0)
    sibling_x.wait_recv()
    forward_tokens(1)
    qkv_load.wait()
    out_load.wait()
    for copy in mod_copies:
        copy.wait()
    for peer in range(PEERS):
        mod_rows[:, peer * mod_cols : (peer + 1) * mod_cols] = jnp.broadcast_to(
            mod_all[peer], (8, mod_cols)
        )
    mod_rows[:, width : 2 * width] = 1.0 + mod_rows[:, width : 2 * width]

    def norm_piece(rel, start, size, at):
        def norm_rows(i, carry):
            offset = pl.multiple_of(i * 16, 16)
            x = tokens[rel, pl.ds(start + offset, 16), :].astype(jnp.float32)
            x = x.reshape(2, 8, width) * mod_rows[:, width : 2 * width] + mod_rows[:, :width]
            normed[pl.ds(at + offset, 16), :] = x.reshape(16, width).astype(jnp.bfloat16)
            return carry

        lax.fori_loop(0, size // 16, norm_rows, 0, unroll=2)

    norm_piece(0, 0, rows, 0)
    norm_piece(1, 0, rows, rows)
    score_scale = head_dim ** (-0.5) * math.log2(math.e)
    halo = []

    def project(pieces, task):
        at = sum(size for _, _, size in pieces)
        base = (0, 2 * rows, 3 * rows)[task]
        joined = jnp.dot(normed[:at, :], qkv_w[...], preferred_element_type=jnp.float32)
        at = 0
        for rel, start, size in pieces:
            cos = cosines[rel, start : start + size, :]
            sin = sines[rel, start : start + size, :]

            def turned(x, gain):
                x = x * lax.rsqrt(jnp.mean(x * x, axis=1, keepdims=True) + EPSILON) * gain
                swapped = (
                    pltpu.roll(x, halves[0], 1) * rope[3:4]
                    + pltpu.roll(x, head_dim - halves[0], 1) * rope[4:5]
                    + pltpu.roll(x, halves[1], 1) * rope[5:6]
                    + pltpu.roll(x, head_dim - halves[1], 1) * rope[6:7]
                )
                return (x * cos + swapped * sin).astype(jnp.bfloat16)

            own = joined[at : at + size]
            queries[base + at : base + at + size, :] = turned(
                own[:, :head_dim], q_gain[...] * score_scale
            )
            kv[1, 0, base + at : base + at + size, :] = turned(
                own[:, head_dim : 2 * head_dim], k_gain[...]
            )
            kv[1, 1, base + at : base + at + size, :] = own[:, 2 * head_dim :].astype(
                jnp.bfloat16
            )
            at += size
        part = pl.ds(base, at)
        forth = remote(
            kv.at[1, :, part],
            kv.at[0, :, part],
            h_send.at[0, task],
            h_recv.at[0, task],
            (lax.rem(f + 1, segments), q),
        )
        back = remote(
            kv.at[1, :, part],
            kv.at[2, :, part],
            h_send.at[1, task],
            h_recv.at[1, task],
            (lax.rem(f + segments - 1, segments), q),
        )

        @pl.when(f < last)
        def _():
            forth.start()

        @pl.when(f > 0)
        def _():
            back.start()

        halo.append((forth, back))

    cols = width // OUT_CHUNKS
    mirror_w = []

    def send_weights(i):
        part = pl.ds(i * cols, cols)
        copy = remote(
            out_w.at[0, :, part],
            out_w.at[2, :, part],
            w_send.at[i],
            w_recv.at[i],
            (f, peers[2]),
        )
        copy.start()
        mirror_w.append(copy)

    sibling_w = remote(
        out_w.at[0], out_w.at[1], w_send.at[OUT_CHUNKS], w_recv.at[OUT_CHUNKS], (f, peers[1])
    )
    counted = (
        jnp.where(f > 0, 1.0, 0.0).astype(jnp.float32),
        jnp.float32(1.0),
        jnp.where(f < last, 1.0, 0.0).astype(jnp.float32),
    )

    def wait_halo(task):
        forth, back = halo[task]
        begin = (0, 2 * rows, 3 * rows)[task]
        size = (2 * rows, rows, rows)[task]
        part = slice(begin, begin + size)

        @pl.when(f > 0)
        def _():
            forth.wait_recv()

        @pl.when(f < last)
        def _():
            back.wait_recv()

        for edge, side in ((0, 0), (last, 2)):

            @pl.when(f == edge)
            def _(side=side):
                kv[side, 0, part, :] = kv[1, 0, part, :]
                kv[side, 1, part, :] = jnp.zeros((size, head_dim), jnp.bfloat16)

    def attend_to(block, begin, size):
        own = queries[block * rows : (block + 1) * rows, :]
        scores = [
            lax.dot_general(
                own,
                kv[side, 0, begin : begin + size, :],
                (((1,), (1,)), ((), ())),
                preferred_element_type=jnp.float32,
            )
            for side in range(3)
        ]
        top = jnp.max(
            jnp.maximum(jnp.maximum(scores[0], scores[2]), scores[1]), axis=1, keepdims=True
        )
        return scores, top

    def mix(scores, top, begin, size):
        weight = jnp.zeros((rows, 1), jnp.float32)
        mixed = jnp.zeros((rows, head_dim), jnp.float32)
        for side in range(3):
            raised = jnp.exp2(scores[side] - top)
            weight = weight + counted[side] * jnp.sum(raised, axis=1, keepdims=True)
            mixed = mixed + jnp.dot(
                raised.astype(jnp.bfloat16),
                kv[side, 1, begin : begin + size, :],
                preferred_element_type=jnp.float32,
            )
        return weight, mixed

    early = 3 * rows

    def attend_early(block):
        part = slice(block * rows, (block + 1) * rows)
        scores, top = attend_to(block, 0, early)
        weight, mixed = mix(scores, top, 0, early)
        ranges[0, part, :] = jnp.broadcast_to(top, (rows, head_dim))
        ranges[1, part, :] = jnp.broadcast_to(weight, (rows, head_dim))
        mixes[part, :] = mixed

    def attend_late(block):
        part = slice(block * rows, (block + 1) * rows)
        scores, late_top = attend_to(block, early, rows)
        early_top = ranges[0, part, :]
        top = jnp.maximum(early_top, late_top)
        weight, mixed = mix(scores, top[:, :1], early, rows)
        keep = jnp.exp2(early_top - top)
        weight = weight + ranges[1, part, :] * keep
        return ((mixed + mixes[part, :] * keep) / weight).astype(jnp.bfloat16)

    project([(0, 0, rows), (1, 0, rows)], 0)
    half = rows // 2
    forward_tokens(2)
    send_weights(0)
    for i in range(2):
        forwards[i].wait_recv()
        norm_piece(2, i * piece, piece, i * piece)
        norm_piece(3, i * piece, piece, half + i * piece)
    project([(2, 0, half), (3, 0, half)], 1)
    send_weights(1)
    norm_piece(2, half, piece, 0)
    forwards[2].wait_recv()
    norm_piece(3, half, piece, half)
    forward_tokens(3)
    send_weights(2)
    send_weights(3)
    norm_piece(2, half + piece, piece, piece)
    forwards[3].wait_recv()
    norm_piece(3, half + piece, piece, half + piece)
    project([(2, half, half), (3, half, half)], 2)
    sibling_w.start()
    wait_halo(0)
    wait_halo(1)
    for block in range(PEERS):
        attend_early(block)
    wait_halo(2)
    att_copies = []
    both = [attend_late(2), attend_late(3)]
    for rel in (3, 2, 1):
        if rel == 1:
            own_att[1] = attend_late(1)
        else:
            part = slice((rel - 2) * half, (rel - 1) * half)
            own_att[rel, :half, :] = both[0][part]
            own_att[rel, half:, :] = both[1][part]
        copy = remote(own_att.at[rel], att.at[rel], a_send.at[rel], a_recv.at[rel], (f, peers[rel]))
        copy.start()
        att_copies.append(copy)
    att[0] = attend_late(0)

    forward_w = []

    def forward_weights(i):
        mirror_w[i].wait_recv()
        part = pl.ds(i * cols, cols)
        copy = remote(
            out_w.at[2, :, part],
            out_w.at[3, :, part],
            w_send.at[OUT_CHUNKS + 1 + i],
            w_recv.at[OUT_CHUNKS + 1 + i],
            (f, peers[1]),
        )
        copy.start()
        forward_w.append(copy)

    forward_weights(0)
    sibling_w.wait_recv()
    for copy in att_copies:
        copy.wait_recv()
    mixed = jnp.concatenate([att[rel] for rel in range(PEERS)], axis=1)

    clean_cols = width // segments
    shifts = []
    cleans = []
    for i in range(OUT_CHUNKS):
        if i + 1 < OUT_CHUNKS:
            forward_weights(i + 1)
        forward_w[i].wait_recv()
        begin = i * cols
        part = pl.ds(begin, cols)
        projected = jnp.dot(
            mixed,
            out_w[:, :, begin : begin + cols].reshape(PEERS * rows, cols),
            preferred_element_type=jnp.float32,
        )
        gate = mod_rows[:, 2 * width + begin : 2 * width + begin + cols]
        gated = (projected.reshape(rows // 8, 8, cols) * gate).reshape(rows, cols)
        before = kept[:, begin : begin + cols].astype(jnp.float32)
        done[:, begin : begin + cols] = (before + gated).astype(jnp.bfloat16)
        shift = remote(
            done.at[:, part],
            arrived.at[:, part],
            s_send.at[i],
            s_recv.at[i],
            (lax.rem(f + 1, segments), q),
        )
        shifts.append(shift)

        @pl.when(f < last)
        def _(shift=shift):
            shift.start()

        for to in range(begin // clean_cols, (begin + cols) // clean_cols):
            from_cols = done.at[:, pl.ds(to * clean_cols, clean_cols)]
            if to < last:
                clean_copy = remote(from_cols, clean, c_send.at[to], c_recv, (to, q))
            else:
                clean_copy = pltpu.make_async_copy(from_cols, clean, c_send.at[to])
            cleans.append(clean_copy)

            @pl.when(f == last)
            def _(clean_copy=clean_copy):
                clean_copy.start()

    for copy in mirror_x + [sibling_x] + forwards + mirror_w + [sibling_w] + forward_w + att_copies:
        copy.wait_send()
    for forth, back in halo:

        @pl.when(f < last)
        def _(forth=forth):
            forth.wait_send()

        @pl.when(f > 0)
        def _(back=back):
            back.wait_send()

    @pl.when(f == 0)
    def _():
        fresh_copy.wait()

    written = []
    for i, shift in enumerate(shifts):

        @pl.when(f > 0)
        def _(shift=shift):
            shift.wait_recv()

        part = pl.ds(i * cols, cols)
        copy = pltpu.make_async_copy(
            arrived.at[:, part], queue_next.at[:, part], out_sem.at[i]
        )
        copy.start()
        written.append(copy)
    for copy in written:
        copy.wait()
    for shift in shifts:

        @pl.when(f < last)
        def _(shift=shift):
            shift.wait_send()

    @pl.when(f == last)
    def _():
        for clean_copy in cleans[:-1]:
            clean_copy.wait_send()
        cleans[-1].wait()

    @pl.when(f < last)
    def _():
        cleans[0].wait_recv()


def hand_over(queue_in, clean_in, queue_next, clean, queue_held, clean_held, sem_in, sem_out):
    piece = queue_in.shape[0] // X_CHUNKS
    steps = []
    for i in range(X_CHUNKS):
        part = pl.ds(i * piece, piece)
        steps.append((queue_in.at[part], queue_held.at[part], queue_next.at[part]))
    steps.append((clean_in, clean_held, clean))
    reads = []
    for i, (source, held, _) in enumerate(steps):
        copy = pltpu.make_async_copy(source, held, sem_in.at[i])
        copy.start()
        reads.append(copy)
    writes = []
    for i, (_, held, target) in enumerate(steps):
        reads[i].wait()
        copy = pltpu.make_async_copy(held, target, sem_out.at[i])
        copy.start()
        writes.append(copy)
    for copy in writes:
        copy.wait()


def fused(
    mesh, queue, fresh_noise, w_mod, w_qkv, w_out, q_gain, k_gain, levels, plan, positions
):
    segments = mesh.shape["segment"]
    rows, width = queue.shape[1:]
    mod_cols = w_mod.shape[2]
    head_dim = q_gain.shape[1]
    rope, *halves = rope_rows(head_dim)
    scalars = pl.BlockSpec(memory_space=pltpu.SMEM)
    outside = pl.BlockSpec(memory_space=pl.ANY)
    bf16, f32 = jnp.bfloat16, jnp.float32
    dma = pltpu.SemaphoreType.DMA
    queue_next, clean_frame = pl.pallas_call(
        functools.partial(block_kernel, segments, tuple(halves)),
        out_shape=(
            jax.ShapeDtypeStruct((rows, width), bf16),
            jax.ShapeDtypeStruct((rows, width // segments), bf16),
        ),
        in_specs=[outside] * 7 + [scalars] * 3 + [outside] * 2,
        out_specs=(outside, outside),
        scratch_shapes=[
            pltpu.VMEM((width, mod_cols), bf16),
            pltpu.VMEM((width, 3 * head_dim), bf16),
            pltpu.VMEM((PEERS, rows, width), bf16),
            pltpu.VMEM((PEERS, rows, width), bf16),
            pltpu.VMEM((PEERS, 1, mod_cols), f32),
            pltpu.VMEM((8, 3 * width), f32),
            pltpu.VMEM((1, width // 2), f32),
            pltpu.VMEM((8, head_dim), f32),
            pltpu.VMEM((1, head_dim), f32),
            pltpu.VMEM((1, head_dim), f32),
            pltpu.VMEM((width, LANES), f32),
            pltpu.VMEM((rows, width), bf16),
            pltpu.VMEM((2 * rows, width), bf16),
            pltpu.VMEM((PEERS, rows, head_dim), f32),
            pltpu.VMEM((PEERS, rows, head_dim), f32),
            pltpu.VMEM((PEERS * rows, head_dim), bf16),
            pltpu.VMEM((3, 2, PEERS * rows, head_dim), bf16),
            pltpu.VMEM((2, PEERS * rows, head_dim), f32),
            pltpu.VMEM((PEERS * rows, head_dim), f32),
            pltpu.VMEM((PEERS, rows, head_dim), bf16),
            pltpu.VMEM((PEERS, rows, head_dim), bf16),
            pltpu.VMEM((rows, width), bf16),
            pltpu.VMEM((rows, width), bf16),
            dma((4,)),
            dma((4 + MOD_CHUNKS,)),
            dma((2 * X_CHUNKS + 1,)),
            dma((2 * X_CHUNKS + 1,)),
            dma((PEERS,)),
            dma((PEERS,)),
            dma((2, 3)),
            dma((2, 3)),
            dma((2 * OUT_CHUNKS + 1,)),
            dma((2 * OUT_CHUNKS + 1,)),
            dma((PEERS,)),
            dma((PEERS,)),
            dma((OUT_CHUNKS,)),
            dma((OUT_CHUNKS,)),
            dma((segments,)),
            dma(()),
            dma((OUT_CHUNKS,)),
        ],
        compiler_params=pltpu.CompilerParams(
            collective_id=0, has_side_effects=True, vmem_limit_bytes=56 * 1024 * 1024
        ),
        cost_estimate=pl.CostEstimate(
            flops=2 * 10**9, bytes_accessed=22 * 10**6, transcendentals=10**6
        ),
        name="relayed_block",
    )(
        queue[0],
        fresh_noise,
        w_mod[0],
        w_qkv.reshape(width, 3 * head_dim),
        w_out[0],
        q_gain,
        k_gain,
        levels,
        plan,
        positions,
        jnp.asarray(time_rates(width)),
        jnp.asarray(rope),
    )
    queue_next, clean_frame = pl.pallas_call(
        hand_over,
        out_shape=(
            jax.ShapeDtypeStruct(queue_next.shape, bf16),
            jax.ShapeDtypeStruct(clean_frame.shape, bf16),
        ),
        in_specs=[outside] * 2,
        out_specs=(outside, outside),
        scratch_shapes=[
            pltpu.VMEM(queue_next.shape, bf16),
            pltpu.VMEM(clean_frame.shape, bf16),
            dma((X_CHUNKS + 1,)),
            dma((X_CHUNKS + 1,)),
        ],
        compiler_params=pltpu.CompilerParams(vmem_limit_bytes=56 * 1024 * 1024),
        name="hand_over",
    )(queue_next, clean_frame)
    return queue_next[None], clean_frame


def solution(mesh):
    placed = (
        P("segment", "seq", None),
        P("seq", None),
        P("segment", None, "seq"),
        P("segment", None, "seq", None),
        P("segment", "seq", None),
        P("segment", None),
        P("segment", None),
        P("segment"),
        P(),
        P("segment"),
    )
    return jax.shard_map(
        functools.partial(fused, mesh) if fits(mesh) else shards,
        mesh=mesh,
        in_specs=placed,
        out_specs=(P("segment", "seq", None), P("seq", "segment")),
        check_vma=False,
    )
```

```python
import functools
import math

import jax
import jax.numpy as jnp
from jax import lax
import numpy as np
from jax.experimental import pallas as pl
from jax.experimental.pallas import tpu as pltpu
from jax.sharding import PartitionSpec as P

GRID_W = 32


EPSILON = 1e-06
ROPE_BASE = 256.0


def with_halo(cells, sides, width):
    for axis, dim in sides:
        count = lax.axis_size(axis)
        ends = count - 1
        head = lax.slice_in_dim(cells, 0, width, axis=dim)
        tail = lax.slice_in_dim(cells, cells.shape[dim] - width, cells.shape[dim], axis=dim)
        cells = jnp.concatenate(
            [
                lax.ppermute(tail, axis, [(i, (i + 1) % count) for i in range(ends)]),
                cells,
                lax.ppermute(head, axis, [((i + 1) % count, i) for i in range(ends)]),
            ],
            axis=dim,
        )
    return cells


def passed_along(value, axis, by):
    length = lax.axis_size(axis)
    pairs = [(i, i + by) for i in range(length) if 0 <= i + by < length]
    return lax.ppermute(value, axis, pairs)


def broadcast(value, axis, root):
    mine = lax.axis_index(axis) == root
    return lax.psum(jnp.where(mine, value, jnp.zeros_like(value)), axis)


def time_embedding(step_values, width):
    half_width = width // 2
    counter = jnp.arange(half_width, dtype=jnp.float32)
    frequency = jnp.exp(-jnp.log(10000.0) * counter / half_width)
    angles = step_values.astype(jnp.float32)[:, None] * frequency[None, :]
    return jnp.concatenate([jnp.cos(angles), jnp.sin(angles)], axis=-1)


def rope_angles(frame_position, row_count, head_dim, grid_width):
    time_dim = head_dim // 8
    space_dim = (head_dim - time_dim) // 2
    tokens_at = jnp.arange(row_count, dtype=jnp.int32)
    grid_row = (tokens_at // grid_width).astype(jnp.float32)
    grid_col = (tokens_at % grid_width).astype(jnp.float32)
    moment = jnp.zeros((row_count,), jnp.float32) + frame_position.astype(jnp.float32)
    sections = []
    for coords, section in ((moment, time_dim), (grid_row, space_dim), (grid_col, space_dim)):
        half_size = section // 2
        frequency = ROPE_BASE ** (-2.0 * jnp.arange(half_size, dtype=jnp.float32) / section)
        angles = coords[:, None] * frequency[None, :]
        sections.append(jnp.concatenate([angles, angles], axis=-1))
    return jnp.concatenate(sections, axis=-1)


def rotate_half(values, head_dim):
    time_dim = head_dim // 8
    space_dim = (head_dim - time_dim) // 2
    pieces_out = []
    position = 0
    for section in (time_dim, space_dim, space_dim):
        half_size = section // 2
        leading = values[..., position : position + half_size]
        second = values[..., position + half_size : position + section]
        pieces_out.append(jnp.concatenate([-second, leading], axis=-1))
        position += section
    return jnp.concatenate(pieces_out, axis=-1)


def apply_rope(values, angles, head_dim):
    return values * jnp.cos(angles) + rotate_half(values, head_dim) * jnp.sin(angles)


def rms_gain(values, gains):
    mean_square = jnp.mean(values * values, axis=-1, keepdims=True)
    return values * lax.rsqrt(mean_square + EPSILON) * gains


def layer_norm(values):
    centre = jnp.mean(values, axis=-1, keepdims=True)
    spread = jnp.mean(jnp.square(values - centre), axis=-1, keepdims=True)
    return (values - centre) * lax.rsqrt(spread + EPSILON)


def attend(query_rows, key_rows, value_rows, usable, head_dim):
    scores = jnp.dot(query_rows, key_rows.T, preferred_element_type=jnp.float32) * head_dim ** (
        -0.5
    )
    scores = jnp.where(usable[None, :], scores, -jnp.inf)
    row_max = jnp.max(scores, axis=-1, keepdims=True)
    raised = jnp.exp(scores - row_max)
    weights = (raised / jnp.sum(raised, axis=-1, keepdims=True)).astype(jnp.bfloat16)
    return jnp.dot(weights, value_rows, preferred_element_type=jnp.float32).astype(jnp.bfloat16)


def shards(queue, fresh_noise, w_mod, w_qkv, w_out, q_gain, k_gain, levels, plan, positions):
    segments = lax.axis_size("segment")
    seq_count = lax.axis_size("seq")
    segment_at = lax.axis_index("segment")
    tok_dev = queue.shape[1]
    width = queue.shape[2]
    heads_here = w_qkv.shape[2]
    head_dim = w_qkv.shape[3] // 3
    tok_frame = tok_dev * seq_count
    picked = levels[:, None] == jnp.arange(plan.shape[0], dtype=jnp.int32)[None, :]
    step_values = jnp.sum(jnp.where(picked, plan[None, :], 0), axis=1)
    embedding = jax.nn.silu(time_embedding(step_values, width)).astype(jnp.bfloat16)
    mod_part = jnp.dot(embedding, w_mod[0], preferred_element_type=jnp.float32)
    modulation = lax.all_gather(mod_part, "seq", axis=1, tiled=True)[0]
    shift_row = modulation[:width]
    scale_row = modulation[width : 2 * width]
    gate_row = modulation[2 * width :]
    resident = queue[0].astype(jnp.float32)
    modulated = (layer_norm(resident) * (1.0 + scale_row) + shift_row).astype(jnp.bfloat16)
    flat_weight = w_qkv[0].reshape(width, heads_here * 3 * head_dim)
    projected_qkv = jnp.dot(
        lax.all_gather(modulated, "seq", axis=0, tiled=True),
        flat_weight,
        preferred_element_type=jnp.float32,
    )
    projected_qkv = projected_qkv.reshape(tok_frame, heads_here, 3 * head_dim)
    angles = rope_angles(positions[0], tok_frame, head_dim, GRID_W)[:, None, :]
    queries = apply_rope(
        rms_gain(projected_qkv[..., :head_dim], q_gain[0]), angles, head_dim
    ).astype(jnp.bfloat16)
    key_rows = apply_rope(
        rms_gain(projected_qkv[..., head_dim : 2 * head_dim], k_gain[0]), angles, head_dim
    ).astype(jnp.bfloat16)
    value_rows = projected_qkv[..., 2 * head_dim :].astype(jnp.bfloat16)
    stacked = jnp.stack([key_rows, value_rows])[None]
    beside_all = with_halo(stacked, (("segment", 0),), 1)
    earlier = beside_all[0]
    following = beside_all[2]
    near_keys = jnp.concatenate([earlier[0], key_rows, following[0]], axis=0)
    near_values = jnp.concatenate([earlier[1], value_rows, following[1]], axis=0)
    filled = jnp.ones((tok_frame,), dtype=bool)
    usable = jnp.concatenate(
        [filled & (segment_at > 0), filled, filled & (segment_at < segments - 1)]
    )
    block_rows = math.gcd(tok_frame, 512)
    block_count = tok_frame // block_rows
    head_keys = near_keys[:, 0]
    head_values = near_values[:, 0]
    query_blocks = queries[:, 0].reshape(block_count, block_rows, head_dim)

    def one_block(query_rows, head_keys=head_keys, head_values=head_values):
        return attend(query_rows, head_keys, head_values, usable, head_dim)

    outputs = [lax.map(one_block, query_blocks).reshape(tok_frame, head_dim)]
    attended = jnp.stack(outputs, axis=1).reshape(tok_frame, heads_here * head_dim)
    projected = lax.psum_scatter(
        jnp.dot(attended, w_out[0], preferred_element_type=jnp.float32).astype(jnp.bfloat16),
        "seq",
        scatter_dimension=0,
        tiled=True,
    ).astype(jnp.float32)
    finished = (resident + gate_row * projected).astype(jnp.bfloat16)
    arrived = passed_along(finished, "segment", 1)
    queue_next = jnp.where(segment_at == 0, fresh_noise, arrived)[None]
    clean_whole = broadcast(finished, "segment", segments - 1)
    column_count = width // segments
    clean_frame = lax.dynamic_slice_in_dim(clean_whole, segment_at * column_count, column_count, 1)
    return (queue_next, clean_frame)


MESH = pl.DeviceIdType.MESH
PEERS = 4
MOD_CHUNKS = 6
X_CHUNKS = 4
OUT_CHUNKS = 8
LANES = 128


def fits(mesh):
    return mesh.shape["seq"] == PEERS


def rope_rows(head_dim):
    time_dim = head_dim // 8
    space_dim = (head_dim - time_dim) // 2
    rows = np.zeros((8, head_dim), np.float32)
    start = 0
    for at, section in enumerate((time_dim, space_dim, space_dim)):
        half = section // 2
        frequency = ROPE_BASE ** (-2.0 * np.arange(half) / section)
        rows[at, start : start + half] = frequency
        rows[at, start + half : start + section] = frequency
        back, forth = (3, 4) if at == 0 else (5, 6)
        rows[back, start + half : start + section] = 1.0
        rows[forth, start : start + half] = -1.0
        start += section
    return rows, time_dim // 2, space_dim // 2


def time_rates(width):
    half_width = width // 2
    return np.exp(-np.log(10000.0) * np.arange(half_width) / half_width).astype(np.float32)[None]


def block_kernel(
    segments,
    halves,
    queue,
    fresh,
    w_mod,
    w_qkv,
    w_out,
    q_gain_in,
    k_gain_in,
    levels,
    plan,
    positions,
    rates_in,
    rope_in,
    queue_next,
    clean,
    mod_w,
    qkv_w,
    out_w,
    tokens,
    mod_all,
    mod_rows,
    rates,
    rope,
    q_gain,
    k_gain,
    embedded,
    kept,
    normed,
    cosines,
    sines,
    queries,
    kv,
    ranges,
    mixes,
    own_att,
    att,
    done,
    arrived,
    small_sem,
    local_sem,
    x_send,
    x_recv,
    m_send,
    m_recv,
    h_send,
    h_recv,
    w_send,
    w_recv,
    a_send,
    a_recv,
    s_send,
    s_recv,
    c_send,
    c_recv,
    out_sem,
):
    f = lax.axis_index("segment")
    q = lax.axis_index("seq")
    last = segments - 1
    rows, width = queue.shape
    head_dim = q_gain_in.shape[1]
    mod_cols = w_mod.shape[1]
    peers = (q, q + 1 - 2 * lax.rem(q, 2), lax.rem(q + 2, 4), 3 - q)

    def remote(source, target, send, recv, device):
        return pltpu.make_async_remote_copy(
            src_ref=source,
            dst_ref=target,
            send_sem=send,
            recv_sem=recv,
            device_id=device,
            device_id_type=MESH,
        )

    barrier = pltpu.get_barrier_semaphore()
    for rel in range(1, PEERS):
        pl.semaphore_signal(barrier, inc=1, device_id=(f, peers[rel]), device_id_type=MESH)
    for step in range(1, segments):
        pl.semaphore_signal(
            barrier, inc=1, device_id=(lax.rem(f + step, segments), q), device_id_type=MESH
        )

    own_tokens = pltpu.make_async_copy(queue, kept, local_sem.at[0])
    own_tokens.start()
    small_loads = []
    for i, (source, target) in enumerate(
        ((rates_in, rates), (rope_in, rope), (q_gain_in, q_gain), (k_gain_in, k_gain))
    ):
        load = pltpu.make_async_copy(source, target, small_sem.at[i])
        load.start()
        small_loads.append(load)
    mod_depth = width // MOD_CHUNKS
    mod_loads = []
    for i in range(MOD_CHUNKS):
        part = pl.ds(i * mod_depth, mod_depth)
        load = pltpu.make_async_copy(w_mod.at[part], mod_w.at[part], local_sem.at[1 + i])
        load.start()
        mod_loads.append(load)
    qkv_load = pltpu.make_async_copy(w_qkv, qkv_w, local_sem.at[1 + MOD_CHUNKS])
    qkv_load.start()
    out_load = pltpu.make_async_copy(w_out, out_w.at[0], local_sem.at[2 + MOD_CHUNKS])
    out_load.start()

    pl.semaphore_wait(barrier, PEERS - 1 + segments - 1)

    own_tokens.wait()

    def settle_rows(i, carry):
        offset = pl.multiple_of(i * 16, 16)
        x = kept[pl.ds(offset, 16), :].astype(jnp.float32)
        x = x - jnp.mean(x, axis=1, keepdims=True)
        x = x * lax.rsqrt(jnp.mean(x * x, axis=1, keepdims=True) + EPSILON)
        tokens[0, pl.ds(offset, 16), :] = x.astype(jnp.bfloat16)
        return carry

    piece = rows // X_CHUNKS
    mirror_x = []
    for i in range(X_CHUNKS):
        lax.fori_loop(i * piece // 16, (i + 1) * piece // 16, settle_rows, 0, unroll=True)
        part = pl.ds(i * piece, piece)
        copy = remote(
            tokens.at[0, part], tokens.at[2, part], x_send.at[i], x_recv.at[i], (f, peers[2])
        )
        copy.start()
        mirror_x.append(copy)
    sibling_x = remote(
        tokens.at[0], tokens.at[1], x_send.at[X_CHUNKS], x_recv.at[X_CHUNKS], (f, peers[1])
    )
    sibling_x.start()
    fresh_copy = pltpu.make_async_copy(fresh, arrived, local_sem.at[3 + MOD_CHUNKS])

    @pl.when(f == 0)
    def _():
        fresh_copy.start()

    for load in small_loads:
        load.wait()
    step_value = plan[levels[0]].astype(jnp.float32)
    angles = rates[...] * step_value
    embedding = jnp.concatenate([jnp.cos(angles), jnp.sin(angles)], axis=1)
    embedding = embedding / (1.0 + jnp.exp(-embedding))
    embedding = embedding.astype(jnp.bfloat16).astype(jnp.float32)
    for start in range(0, width, LANES):
        entries = jnp.broadcast_to(embedding[:, start : start + LANES], (LANES, LANES))
        embedded[start : start + LANES, :] = entries.T
    tiles = mod_cols // LANES

    def add_rows(i, totals):
        offset = pl.multiple_of(i * 16, 16)
        entries = embedded[pl.ds(offset, 16), :]
        sums = []
        for tile in range(tiles):
            lanes = slice(tile * LANES, (tile + 1) * LANES)
            product = mod_w[pl.ds(offset, 16), lanes].astype(jnp.float32) * entries
            sums.append(totals[tile] + (product[:8] + product[8:]))
        return tuple(sums)

    totals = tuple(jnp.zeros((8, LANES), jnp.float32) for _ in range(tiles))
    steps = mod_depth // 16
    for i in range(MOD_CHUNKS):
        mod_loads[i].wait()
        totals = lax.fori_loop(i * steps, (i + 1) * steps, add_rows, totals, unroll=4)
    mod_all[q] = jnp.concatenate(
        [jnp.sum(total, axis=0, keepdims=True) for total in totals], axis=1
    )
    mod_copies = []
    for rel in range(1, PEERS):
        copy = remote(
            mod_all.at[q], mod_all.at[q], m_send.at[rel], m_recv.at[rel], (f, peers[rel])
        )
        copy.start()
        mod_copies.append(copy)

    position = positions[0].astype(jnp.float32)
    grid_col = lax.broadcasted_iota(jnp.int32, (GRID_W, head_dim), 0).astype(jnp.float32)
    col_turn = grid_col * rope[2:3]
    col_cos = jnp.cos(col_turn)
    col_sin = jnp.sin(col_turn)
    by_col = lax.broadcasted_iota(jnp.int32, (GRID_W, head_dim), 1) >= head_dim - 2 * halves[1]
    rows_here = rows // GRID_W
    for rel in range(PEERS):
        grid_row = lax.broadcasted_iota(jnp.int32, (8, head_dim), 0) + peers[rel] * rows_here
        row_turn = position * rope[0:1] + grid_row.astype(jnp.float32) * rope[1:2]
        row_cos = jnp.cos(row_turn)
        row_sin = jnp.sin(row_turn)
        for r in range(rows_here):
            part = slice(r * GRID_W, (r + 1) * GRID_W)
            cosines[rel, part, :] = jnp.where(by_col, col_cos, row_cos[r : r + 1])
            sines[rel, part, :] = jnp.where(by_col, col_sin, row_sin[r : r + 1])

    forwards = []

    def forward_tokens(i):
        mirror_x[i].wait_recv()
        part = pl.ds(i * piece, piece)
        copy = remote(
            tokens.at[2, part],
            tokens.at[3, part],
            x_send.at[X_CHUNKS + 1 + i],
            x_recv.at[X_CHUNKS + 1 + i],
            (f, peers[1]),
        )
        copy.start()
        forwards.append(copy)

    forward_tokens(0)
    sibling_x.wait_recv()
    forward_tokens(1)
    qkv_load.wait()
    out_load.wait()
    for copy in mod_copies:
        copy.wait()
    for peer in range(PEERS):
        mod_rows[:, peer * mod_cols : (peer + 1) * mod_cols] = jnp.broadcast_to(
            mod_all[peer], (8, mod_cols)
        )
    mod_rows[:, width : 2 * width] = 1.0 + mod_rows[:, width : 2 * width]

    def norm_piece(rel, start, size, at):
        def norm_rows(i, carry):
            offset = pl.multiple_of(i * 16, 16)
            x = tokens[rel, pl.ds(start + offset, 16), :].astype(jnp.float32)
            x = x.reshape(2, 8, width) * mod_rows[:, width : 2 * width] + mod_rows[:, :width]
            normed[pl.ds(at + offset, 16), :] = x.reshape(16, width).astype(jnp.bfloat16)
            return carry

        lax.fori_loop(0, size // 16, norm_rows, 0, unroll=2)

    norm_piece(0, 0, rows, 0)
    norm_piece(1, 0, rows, rows)
    score_scale = head_dim ** (-0.5) * math.log2(math.e)
    halo = []

    def project(pieces, task):
        at = sum(size for _, _, size in pieces)
        base = (0, 2 * rows, 3 * rows)[task]
        joined = jnp.dot(normed[:at, :], qkv_w[...], preferred_element_type=jnp.float32)
        at = 0
        for rel, start, size in pieces:
            cos = cosines[rel, start : start + size, :]
            sin = sines[rel, start : start + size, :]

            def turned(x, gain):
                x = x * lax.rsqrt(jnp.mean(x * x, axis=1, keepdims=True) + EPSILON) * gain
                swapped = (
                    pltpu.roll(x, halves[0], 1) * rope[3:4]
                    + pltpu.roll(x, head_dim - halves[0], 1) * rope[4:5]
                    + pltpu.roll(x, halves[1], 1) * rope[5:6]
                    + pltpu.roll(x, head_dim - halves[1], 1) * rope[6:7]
                )
                return (x * cos + swapped * sin).astype(jnp.bfloat16)

            own = joined[at : at + size]
            queries[base + at : base + at + size, :] = turned(
                own[:, :head_dim], q_gain[...] * score_scale
            )
            kv[1, 0, base + at : base + at + size, :] = turned(
                own[:, head_dim : 2 * head_dim], k_gain[...]
            )
            kv[1, 1, base + at : base + at + size, :] = own[:, 2 * head_dim :].astype(
                jnp.bfloat16
            )
            at += size
        part = pl.ds(base, at)
        forth = remote(
            kv.at[1, :, part],
            kv.at[0, :, part],
            h_send.at[0, task],
            h_recv.at[0, task],
            (lax.rem(f + 1, segments), q),
        )
        back = remote(
            kv.at[1, :, part],
            kv.at[2, :, part],
            h_send.at[1, task],
            h_recv.at[1, task],
            (lax.rem(f + segments - 1, segments), q),
        )

        @pl.when(f < last)
        def _():
            forth.start()

        @pl.when(f > 0)
        def _():
            back.start()

        halo.append((forth, back))

    cols = width // OUT_CHUNKS
    mirror_w = []

    def send_weights(i):
        part = pl.ds(i * cols, cols)
        copy = remote(
            out_w.at[0, :, part],
            out_w.at[2, :, part],
            w_send.at[i],
            w_recv.at[i],
            (f, peers[2]),
        )
        copy.start()
        mirror_w.append(copy)

    sibling_w = remote(
        out_w.at[0], out_w.at[1], w_send.at[OUT_CHUNKS], w_recv.at[OUT_CHUNKS], (f, peers[1])
    )
    counted = (
        jnp.where(f > 0, 1.0, 0.0).astype(jnp.float32),
        jnp.float32(1.0),
        jnp.where(f < last, 1.0, 0.0).astype(jnp.float32),
    )

    def wait_halo(task):
        forth, back = halo[task]
        begin = (0, 2 * rows, 3 * rows)[task]
        size = (2 * rows, rows, rows)[task]
        part = slice(begin, begin + size)

        @pl.when(f > 0)
        def _():
            forth.wait_recv()

        @pl.when(f < last)
        def _():
            back.wait_recv()

        for edge, side in ((0, 0), (last, 2)):

            @pl.when(f == edge)
            def _(side=side):
                kv[side, 0, part, :] = kv[1, 0, part, :]
                kv[side, 1, part, :] = jnp.zeros((size, head_dim), jnp.bfloat16)

    def attend_to(block, begin, size):
        own = queries[block * rows : (block + 1) * rows, :]
        scores = [
            lax.dot_general(
                own,
                kv[side, 0, begin : begin + size, :],
                (((1,), (1,)), ((), ())),
                preferred_element_type=jnp.float32,
            )
            for side in range(3)
        ]
        top = jnp.max(
            jnp.maximum(jnp.maximum(scores[0], scores[2]), scores[1]), axis=1, keepdims=True
        )
        return scores, top

    def mix(scores, top, begin, size):
        weight = jnp.zeros((rows, 1), jnp.float32)
        mixed = jnp.zeros((rows, head_dim), jnp.float32)
        for side in range(3):
            raised = jnp.exp2(scores[side] - top)
            weight = weight + counted[side] * jnp.sum(raised, axis=1, keepdims=True)
            mixed = mixed + jnp.dot(
                raised.astype(jnp.bfloat16),
                kv[side, 1, begin : begin + size, :],
                preferred_element_type=jnp.float32,
            )
        return weight, mixed

    early = 3 * rows

    def attend_early(block):
        part = slice(block * rows, (block + 1) * rows)
        scores, top = attend_to(block, 0, early)
        weight, mixed = mix(scores, top, 0, early)
        ranges[0, part, :] = jnp.broadcast_to(top, (rows, head_dim))
        ranges[1, part, :] = jnp.broadcast_to(weight, (rows, head_dim))
        mixes[part, :] = mixed

    def attend_late(block):
        part = slice(block * rows, (block + 1) * rows)
        scores, late_top = attend_to(block, early, rows)
        early_top = ranges[0, part, :]
        top = jnp.maximum(early_top, late_top)
        weight, mixed = mix(scores, top[:, :1], early, rows)
        keep = jnp.exp2(early_top - top)
        weight = weight + ranges[1, part, :] * keep
        return ((mixed + mixes[part, :] * keep) / weight).astype(jnp.bfloat16)

    project([(0, 0, rows), (1, 0, rows)], 0)
    half = rows // 2
    forward_tokens(2)
    send_weights(0)
    for i in range(2):
        forwards[i].wait_recv()
        norm_piece(2, i * piece, piece, i * piece)
        norm_piece(3, i * piece, piece, half + i * piece)
    project([(2, 0, half), (3, 0, half)], 1)
    send_weights(1)
    send_weights(2)
    norm_piece(2, half, piece, 0)
    forwards[2].wait_recv()
    norm_piece(3, half, piece, half)
    forward_tokens(3)
    send_weights(3)
    norm_piece(2, half + piece, piece, piece)
    forwards[3].wait_recv()
    norm_piece(3, half + piece, piece, half + piece)
    project([(2, half, half), (3, half, half)], 2)
    send_weights(4)
    sibling_w.start()
    wait_halo(0)
    wait_halo(1)
    for block in range(PEERS):
        attend_early(block)
    send_weights(5)
    wait_halo(2)
    att_copies = []
    both = [attend_late(2), attend_late(3)]
    for rel in (3, 2, 1):
        if rel == 1:
            own_att[1] = attend_late(1)
        else:
            part = slice((rel - 2) * half, (rel - 1) * half)
            own_att[rel, :half, :] = both[0][part]
            own_att[rel, half:, :] = both[1][part]
        copy = remote(own_att.at[rel], att.at[rel], a_send.at[rel], a_recv.at[rel], (f, peers[rel]))
        copy.start()
        att_copies.append(copy)
    for i in range(6, OUT_CHUNKS):
        send_weights(i)
    att[0] = attend_late(0)

    forward_w = []

    def forward_weights(i):
        mirror_w[i].wait_recv()
        part = pl.ds(i * cols, cols)
        copy = remote(
            out_w.at[2, :, part],
            out_w.at[3, :, part],
            w_send.at[OUT_CHUNKS + 1 + i],
            w_recv.at[OUT_CHUNKS + 1 + i],
            (f, peers[1]),
        )
        copy.start()
        forward_w.append(copy)

    forward_weights(0)
    sibling_w.wait_recv()
    for copy in att_copies:
        copy.wait_recv()
    mixed = jnp.concatenate([att[rel] for rel in range(PEERS)], axis=1)

    clean_cols = width // segments
    shifts = []
    cleans = []
    for i in range(OUT_CHUNKS):
        if i + 1 < OUT_CHUNKS:
            forward_weights(i + 1)
        forward_w[i].wait_recv()
        begin = i * cols
        part = pl.ds(begin, cols)
        projected = jnp.dot(
            mixed,
            out_w[:, :, begin : begin + cols].reshape(PEERS * rows, cols),
            preferred_element_type=jnp.float32,
        )
        gate = mod_rows[:, 2 * width + begin : 2 * width + begin + cols]
        gated = (projected.reshape(rows // 8, 8, cols) * gate).reshape(rows, cols)
        before = kept[:, begin : begin + cols].astype(jnp.float32)
        done[:, begin : begin + cols] = (before + gated).astype(jnp.bfloat16)
        shift = remote(
            done.at[:, part],
            arrived.at[:, part],
            s_send.at[i],
            s_recv.at[i],
            (lax.rem(f + 1, segments), q),
        )
        shifts.append(shift)

        @pl.when(f < last)
        def _(shift=shift):
            shift.start()

        for to in range(begin // clean_cols, (begin + cols) // clean_cols):
            from_cols = done.at[:, pl.ds(to * clean_cols, clean_cols)]
            if to < last:
                clean_copy = remote(from_cols, clean, c_send.at[to], c_recv, (to, q))
            else:
                clean_copy = pltpu.make_async_copy(from_cols, clean, c_send.at[to])
            cleans.append(clean_copy)

            @pl.when(f == last)
            def _(clean_copy=clean_copy):
                clean_copy.start()

    for copy in mirror_x + [sibling_x] + forwards + mirror_w + [sibling_w] + forward_w + att_copies:
        copy.wait_send()
    for forth, back in halo:

        @pl.when(f < last)
        def _(forth=forth):
            forth.wait_send()

        @pl.when(f > 0)
        def _(back=back):
            back.wait_send()

    @pl.when(f == 0)
    def _():
        fresh_copy.wait()

    written = []
    for i, shift in enumerate(shifts):

        @pl.when(f > 0)
        def _(shift=shift):
            shift.wait_recv()

        part = pl.ds(i * cols, cols)
        copy = pltpu.make_async_copy(
            arrived.at[:, part], queue_next.at[:, part], out_sem.at[i]
        )
        copy.start()
        written.append(copy)
    for copy in written:
        copy.wait()
    for shift in shifts:

        @pl.when(f < last)
        def _(shift=shift):
            shift.wait_send()

    @pl.when(f == last)
    def _():
        for clean_copy in cleans[:-1]:
            clean_copy.wait_send()
        cleans[-1].wait()

    @pl.when(f < last)
    def _():
        cleans[0].wait_recv()


def hand_over(queue_in, clean_in, queue_next, clean, queue_held, clean_held, sem_in, sem_out):
    piece = queue_in.shape[0] // X_CHUNKS
    steps = []
    for i in range(X_CHUNKS):
        part = pl.ds(i * piece, piece)
        steps.append((queue_in.at[part], queue_held.at[part], queue_next.at[part]))
    steps.append((clean_in, clean_held, clean))
    reads = []
    for i, (source, held, _) in enumerate(steps):
        copy = pltpu.make_async_copy(source, held, sem_in.at[i])
        copy.start()
        reads.append(copy)
    writes = []
    for i, (_, held, target) in enumerate(steps):
        reads[i].wait()
        copy = pltpu.make_async_copy(held, target, sem_out.at[i])
        copy.start()
        writes.append(copy)
    for copy in writes:
        copy.wait()


def fused(
    mesh, queue, fresh_noise, w_mod, w_qkv, w_out, q_gain, k_gain, levels, plan, positions
):
    segments = mesh.shape["segment"]
    rows, width = queue.shape[1:]
    mod_cols = w_mod.shape[2]
    head_dim = q_gain.shape[1]
    rope, *halves = rope_rows(head_dim)
    scalars = pl.BlockSpec(memory_space=pltpu.SMEM)
    outside = pl.BlockSpec(memory_space=pl.ANY)
    bf16, f32 = jnp.bfloat16, jnp.float32
    dma = pltpu.SemaphoreType.DMA
    queue_next, clean_frame = pl.pallas_call(
        functools.partial(block_kernel, segments, tuple(halves)),
        out_shape=(
            jax.ShapeDtypeStruct((rows, width), bf16),
            jax.ShapeDtypeStruct((rows, width // segments), bf16),
        ),
        in_specs=[outside] * 7 + [scalars] * 3 + [outside] * 2,
        out_specs=(outside, outside),
        scratch_shapes=[
            pltpu.VMEM((width, mod_cols), bf16),
            pltpu.VMEM((width, 3 * head_dim), bf16),
            pltpu.VMEM((PEERS, rows, width), bf16),
            pltpu.VMEM((PEERS, rows, width), bf16),
            pltpu.VMEM((PEERS, 1, mod_cols), f32),
            pltpu.VMEM((8, 3 * width), f32),
            pltpu.VMEM((1, width // 2), f32),
            pltpu.VMEM((8, head_dim), f32),
            pltpu.VMEM((1, head_dim), f32),
            pltpu.VMEM((1, head_dim), f32),
            pltpu.VMEM((width, LANES), f32),
            pltpu.VMEM((rows, width), bf16),
            pltpu.VMEM((2 * rows, width), bf16),
            pltpu.VMEM((PEERS, rows, head_dim), f32),
            pltpu.VMEM((PEERS, rows, head_dim), f32),
            pltpu.VMEM((PEERS * rows, head_dim), bf16),
            pltpu.VMEM((3, 2, PEERS * rows, head_dim), bf16),
            pltpu.VMEM((2, PEERS * rows, head_dim), f32),
            pltpu.VMEM((PEERS * rows, head_dim), f32),
            pltpu.VMEM((PEERS, rows, head_dim), bf16),
            pltpu.VMEM((PEERS, rows, head_dim), bf16),
            pltpu.VMEM((rows, width), bf16),
            pltpu.VMEM((rows, width), bf16),
            dma((4,)),
            dma((4 + MOD_CHUNKS,)),
            dma((2 * X_CHUNKS + 1,)),
            dma((2 * X_CHUNKS + 1,)),
            dma((PEERS,)),
            dma((PEERS,)),
            dma((2, 3)),
            dma((2, 3)),
            dma((2 * OUT_CHUNKS + 1,)),
            dma((2 * OUT_CHUNKS + 1,)),
            dma((PEERS,)),
            dma((PEERS,)),
            dma((OUT_CHUNKS,)),
            dma((OUT_CHUNKS,)),
            dma((segments,)),
            dma(()),
            dma((OUT_CHUNKS,)),
        ],
        compiler_params=pltpu.CompilerParams(
            collective_id=0, has_side_effects=True, vmem_limit_bytes=56 * 1024 * 1024
        ),
        cost_estimate=pl.CostEstimate(
            flops=2 * 10**9, bytes_accessed=22 * 10**6, transcendentals=10**6
        ),
        name="relayed_block",
    )(
        queue[0],
        fresh_noise,
        w_mod[0],
        w_qkv.reshape(width, 3 * head_dim),
        w_out[0],
        q_gain,
        k_gain,
        levels,
        plan,
        positions,
        jnp.asarray(time_rates(width)),
        jnp.asarray(rope),
    )
    queue_next, clean_frame = pl.pallas_call(
        hand_over,
        out_shape=(
            jax.ShapeDtypeStruct(queue_next.shape, bf16),
            jax.ShapeDtypeStruct(clean_frame.shape, bf16),
        ),
        in_specs=[outside] * 2,
        out_specs=(outside, outside),
        scratch_shapes=[
            pltpu.VMEM(queue_next.shape, bf16),
            pltpu.VMEM(clean_frame.shape, bf16),
            dma((X_CHUNKS + 1,)),
            dma((X_CHUNKS + 1,)),
        ],
        compiler_params=pltpu.CompilerParams(vmem_limit_bytes=56 * 1024 * 1024),
        name="hand_over",
    )(queue_next, clean_frame)
    return queue_next[None], clean_frame


def solution(mesh):
    placed = (
        P("segment", "seq", None),
        P("seq", None),
        P("segment", None, "seq"),
        P("segment", None, "seq", None),
        P("segment", "seq", None),
        P("segment", None),
        P("segment", None),
        P("segment"),
        P(),
        P("segment"),
    )
    return jax.shard_map(
        functools.partial(fused, mesh) if fits(mesh) else shards,
        mesh=mesh,
        in_specs=placed,
        out_specs=(P("segment", "seq", None), P("seq", "segment")),
        check_vma=False,
    )
```

```python
import functools
import math

import jax
import jax.numpy as jnp
from jax import lax
import numpy as np
from jax.experimental import pallas as pl
from jax.experimental.pallas import tpu as pltpu
from jax.sharding import PartitionSpec as P

GRID_W = 32


EPSILON = 1e-06
ROPE_BASE = 256.0


def with_halo(cells, sides, width):
    for axis, dim in sides:
        count = lax.axis_size(axis)
        ends = count - 1
        head = lax.slice_in_dim(cells, 0, width, axis=dim)
        tail = lax.slice_in_dim(cells, cells.shape[dim] - width, cells.shape[dim], axis=dim)
        cells = jnp.concatenate(
            [
                lax.ppermute(tail, axis, [(i, (i + 1) % count) for i in range(ends)]),
                cells,
                lax.ppermute(head, axis, [((i + 1) % count, i) for i in range(ends)]),
            ],
            axis=dim,
        )
    return cells


def passed_along(value, axis, by):
    length = lax.axis_size(axis)
    pairs = [(i, i + by) for i in range(length) if 0 <= i + by < length]
    return lax.ppermute(value, axis, pairs)


def broadcast(value, axis, root):
    mine = lax.axis_index(axis) == root
    return lax.psum(jnp.where(mine, value, jnp.zeros_like(value)), axis)


def time_embedding(step_values, width):
    half_width = width // 2
    counter = jnp.arange(half_width, dtype=jnp.float32)
    frequency = jnp.exp(-jnp.log(10000.0) * counter / half_width)
    angles = step_values.astype(jnp.float32)[:, None] * frequency[None, :]
    return jnp.concatenate([jnp.cos(angles), jnp.sin(angles)], axis=-1)


def rope_angles(frame_position, row_count, head_dim, grid_width):
    time_dim = head_dim // 8
    space_dim = (head_dim - time_dim) // 2
    tokens_at = jnp.arange(row_count, dtype=jnp.int32)
    grid_row = (tokens_at // grid_width).astype(jnp.float32)
    grid_col = (tokens_at % grid_width).astype(jnp.float32)
    moment = jnp.zeros((row_count,), jnp.float32) + frame_position.astype(jnp.float32)
    sections = []
    for coords, section in ((moment, time_dim), (grid_row, space_dim), (grid_col, space_dim)):
        half_size = section // 2
        frequency = ROPE_BASE ** (-2.0 * jnp.arange(half_size, dtype=jnp.float32) / section)
        angles = coords[:, None] * frequency[None, :]
        sections.append(jnp.concatenate([angles, angles], axis=-1))
    return jnp.concatenate(sections, axis=-1)


def rotate_half(values, head_dim):
    time_dim = head_dim // 8
    space_dim = (head_dim - time_dim) // 2
    pieces_out = []
    position = 0
    for section in (time_dim, space_dim, space_dim):
        half_size = section // 2
        leading = values[..., position : position + half_size]
        second = values[..., position + half_size : position + section]
        pieces_out.append(jnp.concatenate([-second, leading], axis=-1))
        position += section
    return jnp.concatenate(pieces_out, axis=-1)


def apply_rope(values, angles, head_dim):
    return values * jnp.cos(angles) + rotate_half(values, head_dim) * jnp.sin(angles)


def rms_gain(values, gains):
    mean_square = jnp.mean(values * values, axis=-1, keepdims=True)
    return values * lax.rsqrt(mean_square + EPSILON) * gains


def layer_norm(values):
    centre = jnp.mean(values, axis=-1, keepdims=True)
    spread = jnp.mean(jnp.square(values - centre), axis=-1, keepdims=True)
    return (values - centre) * lax.rsqrt(spread + EPSILON)


def attend(query_rows, key_rows, value_rows, usable, head_dim):
    scores = jnp.dot(query_rows, key_rows.T, preferred_element_type=jnp.float32) * head_dim ** (
        -0.5
    )
    scores = jnp.where(usable[None, :], scores, -jnp.inf)
    row_max = jnp.max(scores, axis=-1, keepdims=True)
    raised = jnp.exp(scores - row_max)
    weights = (raised / jnp.sum(raised, axis=-1, keepdims=True)).astype(jnp.bfloat16)
    return jnp.dot(weights, value_rows, preferred_element_type=jnp.float32).astype(jnp.bfloat16)


def shards(queue, fresh_noise, w_mod, w_qkv, w_out, q_gain, k_gain, levels, plan, positions):
    segments = lax.axis_size("segment")
    seq_count = lax.axis_size("seq")
    segment_at = lax.axis_index("segment")
    tok_dev = queue.shape[1]
    width = queue.shape[2]
    heads_here = w_qkv.shape[2]
    head_dim = w_qkv.shape[3] // 3
    tok_frame = tok_dev * seq_count
    picked = levels[:, None] == jnp.arange(plan.shape[0], dtype=jnp.int32)[None, :]
    step_values = jnp.sum(jnp.where(picked, plan[None, :], 0), axis=1)
    embedding = jax.nn.silu(time_embedding(step_values, width)).astype(jnp.bfloat16)
    mod_part = jnp.dot(embedding, w_mod[0], preferred_element_type=jnp.float32)
    modulation = lax.all_gather(mod_part, "seq", axis=1, tiled=True)[0]
    shift_row = modulation[:width]
    scale_row = modulation[width : 2 * width]
    gate_row = modulation[2 * width :]
    resident = queue[0].astype(jnp.float32)
    modulated = (layer_norm(resident) * (1.0 + scale_row) + shift_row).astype(jnp.bfloat16)
    flat_weight = w_qkv[0].reshape(width, heads_here * 3 * head_dim)
    projected_qkv = jnp.dot(
        lax.all_gather(modulated, "seq", axis=0, tiled=True),
        flat_weight,
        preferred_element_type=jnp.float32,
    )
    projected_qkv = projected_qkv.reshape(tok_frame, heads_here, 3 * head_dim)
    angles = rope_angles(positions[0], tok_frame, head_dim, GRID_W)[:, None, :]
    queries = apply_rope(
        rms_gain(projected_qkv[..., :head_dim], q_gain[0]), angles, head_dim
    ).astype(jnp.bfloat16)
    key_rows = apply_rope(
        rms_gain(projected_qkv[..., head_dim : 2 * head_dim], k_gain[0]), angles, head_dim
    ).astype(jnp.bfloat16)
    value_rows = projected_qkv[..., 2 * head_dim :].astype(jnp.bfloat16)
    stacked = jnp.stack([key_rows, value_rows])[None]
    beside_all = with_halo(stacked, (("segment", 0),), 1)
    earlier = beside_all[0]
    following = beside_all[2]
    near_keys = jnp.concatenate([earlier[0], key_rows, following[0]], axis=0)
    near_values = jnp.concatenate([earlier[1], value_rows, following[1]], axis=0)
    filled = jnp.ones((tok_frame,), dtype=bool)
    usable = jnp.concatenate(
        [filled & (segment_at > 0), filled, filled & (segment_at < segments - 1)]
    )
    block_rows = math.gcd(tok_frame, 512)
    block_count = tok_frame // block_rows
    head_keys = near_keys[:, 0]
    head_values = near_values[:, 0]
    query_blocks = queries[:, 0].reshape(block_count, block_rows, head_dim)

    def one_block(query_rows, head_keys=head_keys, head_values=head_values):
        return attend(query_rows, head_keys, head_values, usable, head_dim)

    outputs = [lax.map(one_block, query_blocks).reshape(tok_frame, head_dim)]
    attended = jnp.stack(outputs, axis=1).reshape(tok_frame, heads_here * head_dim)
    projected = lax.psum_scatter(
        jnp.dot(attended, w_out[0], preferred_element_type=jnp.float32).astype(jnp.bfloat16),
        "seq",
        scatter_dimension=0,
        tiled=True,
    ).astype(jnp.float32)
    finished = (resident + gate_row * projected).astype(jnp.bfloat16)
    arrived = passed_along(finished, "segment", 1)
    queue_next = jnp.where(segment_at == 0, fresh_noise, arrived)[None]
    clean_whole = broadcast(finished, "segment", segments - 1)
    column_count = width // segments
    clean_frame = lax.dynamic_slice_in_dim(clean_whole, segment_at * column_count, column_count, 1)
    return (queue_next, clean_frame)


MESH = pl.DeviceIdType.MESH
PEERS = 4
MOD_CHUNKS = 6
X_CHUNKS = 4
OUT_CHUNKS = 8
LANES = 128


def fits(mesh):
    return mesh.shape["seq"] == PEERS


def rope_rows(head_dim):
    time_dim = head_dim // 8
    space_dim = (head_dim - time_dim) // 2
    rows = np.zeros((8, head_dim), np.float32)
    start = 0
    for at, section in enumerate((time_dim, space_dim, space_dim)):
        half = section // 2
        frequency = ROPE_BASE ** (-2.0 * np.arange(half) / section)
        rows[at, start : start + half] = frequency
        rows[at, start + half : start + section] = frequency
        back, forth = (3, 4) if at == 0 else (5, 6)
        rows[back, start + half : start + section] = 1.0
        rows[forth, start : start + half] = -1.0
        start += section
    return rows, time_dim // 2, space_dim // 2


def time_rates(width):
    half_width = width // 2
    return np.exp(-np.log(10000.0) * np.arange(half_width) / half_width).astype(np.float32)[None]


def block_kernel(
    segments,
    halves,
    queue,
    fresh,
    w_mod,
    w_qkv,
    w_out,
    q_gain_in,
    k_gain_in,
    levels,
    plan,
    positions,
    rates_in,
    rope_in,
    queue_next,
    clean,
    mod_w,
    qkv_w,
    out_w,
    tokens,
    mod_all,
    mod_rows,
    rates,
    rope,
    q_gain,
    k_gain,
    embedded,
    kept,
    normed,
    cosines,
    sines,
    queries,
    kv,
    ranges,
    mixes,
    own_att,
    att,
    done,
    arrived,
    small_sem,
    local_sem,
    x_send,
    x_recv,
    m_send,
    m_recv,
    h_send,
    h_recv,
    w_send,
    w_recv,
    a_send,
    a_recv,
    s_send,
    s_recv,
    c_send,
    c_recv,
    out_sem,
):
    f = lax.axis_index("segment")
    q = lax.axis_index("seq")
    last = segments - 1
    rows, width = queue.shape
    head_dim = q_gain_in.shape[1]
    mod_cols = w_mod.shape[1]
    peers = (q, q + 1 - 2 * lax.rem(q, 2), lax.rem(q + 2, 4), 3 - q)

    def remote(source, target, send, recv, device):
        return pltpu.make_async_remote_copy(
            src_ref=source,
            dst_ref=target,
            send_sem=send,
            recv_sem=recv,
            device_id=device,
            device_id_type=MESH,
        )

    barrier = pltpu.get_barrier_semaphore()
    for rel in range(1, PEERS):
        pl.semaphore_signal(barrier, inc=1, device_id=(f, peers[rel]), device_id_type=MESH)
    for step in range(1, segments):
        pl.semaphore_signal(
            barrier, inc=1, device_id=(lax.rem(f + step, segments), q), device_id_type=MESH
        )

    own_tokens = pltpu.make_async_copy(queue, kept, local_sem.at[0])
    own_tokens.start()
    small_loads = []
    for i, (source, target) in enumerate(
        ((rates_in, rates), (rope_in, rope), (q_gain_in, q_gain), (k_gain_in, k_gain))
    ):
        load = pltpu.make_async_copy(source, target, small_sem.at[i])
        load.start()
        small_loads.append(load)
    mod_depth = width // MOD_CHUNKS
    mod_loads = []
    for i in range(MOD_CHUNKS):
        part = pl.ds(i * mod_depth, mod_depth)
        load = pltpu.make_async_copy(w_mod.at[part], mod_w.at[part], local_sem.at[1 + i])
        load.start()
        mod_loads.append(load)
    qkv_load = pltpu.make_async_copy(w_qkv, qkv_w, local_sem.at[1 + MOD_CHUNKS])
    qkv_load.start()
    out_load = pltpu.make_async_copy(w_out, out_w.at[0], local_sem.at[2 + MOD_CHUNKS])
    out_load.start()

    pl.semaphore_wait(barrier, PEERS - 1 + segments - 1)

    own_tokens.wait()

    def settle_rows(i, carry):
        offset = pl.multiple_of(i * 16, 16)
        x = kept[pl.ds(offset, 16), :].astype(jnp.float32)
        x = x - jnp.mean(x, axis=1, keepdims=True)
        x = x * lax.rsqrt(jnp.mean(x * x, axis=1, keepdims=True) + EPSILON)
        tokens[0, pl.ds(offset, 16), :] = x.astype(jnp.bfloat16)
        return carry

    piece = rows // X_CHUNKS
    mirror_x = []
    for i in range(X_CHUNKS):
        lax.fori_loop(i * piece // 16, (i + 1) * piece // 16, settle_rows, 0, unroll=True)
        part = pl.ds(i * piece, piece)
        copy = remote(
            tokens.at[0, part], tokens.at[2, part], x_send.at[i], x_recv.at[i], (f, peers[2])
        )
        copy.start()
        mirror_x.append(copy)
    sibling_x = remote(
        tokens.at[0], tokens.at[1], x_send.at[X_CHUNKS], x_recv.at[X_CHUNKS], (f, peers[1])
    )
    sibling_x.start()
    fresh_copy = pltpu.make_async_copy(fresh, arrived, local_sem.at[3 + MOD_CHUNKS])

    @pl.when(f == 0)
    def _():
        fresh_copy.start()

    for load in small_loads:
        load.wait()
    step_value = plan[levels[0]].astype(jnp.float32)
    angles = rates[...] * step_value
    embedding = jnp.concatenate([jnp.cos(angles), jnp.sin(angles)], axis=1)
    embedding = embedding / (1.0 + jnp.exp(-embedding))
    embedding = embedding.astype(jnp.bfloat16).astype(jnp.float32)
    for start in range(0, width, LANES):
        entries = jnp.broadcast_to(embedding[:, start : start + LANES], (LANES, LANES))
        embedded[start : start + LANES, :] = entries.T
    tiles = mod_cols // LANES

    def add_rows(i, totals):
        offset = pl.multiple_of(i * 16, 16)
        entries = embedded[pl.ds(offset, 16), :]
        sums = []
        for tile in range(tiles):
            lanes = slice(tile * LANES, (tile + 1) * LANES)
            product = mod_w[pl.ds(offset, 16), lanes].astype(jnp.float32) * entries
            sums.append(totals[tile] + (product[:8] + product[8:]))
        return tuple(sums)

    totals = tuple(jnp.zeros((8, LANES), jnp.float32) for _ in range(tiles))
    steps = mod_depth // 16
    for i in range(MOD_CHUNKS):
        mod_loads[i].wait()
        totals = lax.fori_loop(i * steps, (i + 1) * steps, add_rows, totals, unroll=4)
    mod_all[q] = jnp.concatenate(
        [jnp.sum(total, axis=0, keepdims=True) for total in totals], axis=1
    )
    mod_copies = []
    for rel in range(1, PEERS):
        copy = remote(
            mod_all.at[q], mod_all.at[q], m_send.at[rel], m_recv.at[rel], (f, peers[rel])
        )
        copy.start()
        mod_copies.append(copy)

    position = positions[0].astype(jnp.float32)
    grid_col = lax.broadcasted_iota(jnp.int32, (GRID_W, head_dim), 0).astype(jnp.float32)
    col_turn = grid_col * rope[2:3]
    col_cos = jnp.cos(col_turn)
    col_sin = jnp.sin(col_turn)
    by_col = lax.broadcasted_iota(jnp.int32, (GRID_W, head_dim), 1) >= head_dim - 2 * halves[1]
    rows_here = rows // GRID_W
    for rel in range(PEERS):
        grid_row = lax.broadcasted_iota(jnp.int32, (8, head_dim), 0) + peers[rel] * rows_here
        row_turn = position * rope[0:1] + grid_row.astype(jnp.float32) * rope[1:2]
        row_cos = jnp.cos(row_turn)
        row_sin = jnp.sin(row_turn)
        for r in range(rows_here):
            part = slice(r * GRID_W, (r + 1) * GRID_W)
            cosines[rel, part, :] = jnp.where(by_col, col_cos, row_cos[r : r + 1])
            sines[rel, part, :] = jnp.where(by_col, col_sin, row_sin[r : r + 1])

    forwards = []

    def forward_tokens(i):
        mirror_x[i].wait_recv()
        part = pl.ds(i * piece, piece)
        copy = remote(
            tokens.at[2, part],
            tokens.at[3, part],
            x_send.at[X_CHUNKS + 1 + i],
            x_recv.at[X_CHUNKS + 1 + i],
            (f, peers[1]),
        )
        copy.start()
        forwards.append(copy)

    forward_tokens(0)
    sibling_x.wait_recv()
    forward_tokens(1)
    qkv_load.wait()
    out_load.wait()
    for copy in mod_copies:
        copy.wait()
    for peer in range(PEERS):
        mod_rows[:, peer * mod_cols : (peer + 1) * mod_cols] = jnp.broadcast_to(
            mod_all[peer], (8, mod_cols)
        )
    mod_rows[:, width : 2 * width] = 1.0 + mod_rows[:, width : 2 * width]

    def norm_piece(rel, start, size, at):
        def norm_rows(i, carry):
            offset = pl.multiple_of(i * 16, 16)
            x = tokens[rel, pl.ds(start + offset, 16), :].astype(jnp.float32)
            x = x.reshape(2, 8, width) * mod_rows[:, width : 2 * width] + mod_rows[:, :width]
            normed[pl.ds(at + offset, 16), :] = x.reshape(16, width).astype(jnp.bfloat16)
            return carry

        lax.fori_loop(0, size // 16, norm_rows, 0, unroll=2)

    norm_piece(0, 0, rows, 0)
    norm_piece(1, 0, rows, rows)
    score_scale = head_dim ** (-0.5) * math.log2(math.e)
    halo = []

    def project(pieces, task):
        at = sum(size for _, _, size in pieces)
        base = (0, 2 * rows, 3 * rows)[task]
        joined = jnp.dot(normed[:at, :], qkv_w[...], preferred_element_type=jnp.float32)
        at = 0
        for rel, start, size in pieces:
            cos = cosines[rel, start : start + size, :]
            sin = sines[rel, start : start + size, :]

            def turned(x, gain):
                x = x * lax.rsqrt(jnp.mean(x * x, axis=1, keepdims=True) + EPSILON) * gain
                swapped = (
                    pltpu.roll(x, halves[0], 1) * rope[3:4]
                    + pltpu.roll(x, head_dim - halves[0], 1) * rope[4:5]
                    + pltpu.roll(x, halves[1], 1) * rope[5:6]
                    + pltpu.roll(x, head_dim - halves[1], 1) * rope[6:7]
                )
                return (x * cos + swapped * sin).astype(jnp.bfloat16)

            own = joined[at : at + size]
            queries[base + at : base + at + size, :] = turned(
                own[:, :head_dim], q_gain[...] * score_scale
            )
            kv[1, 0, base + at : base + at + size, :] = turned(
                own[:, head_dim : 2 * head_dim], k_gain[...]
            )
            kv[1, 1, base + at : base + at + size, :] = own[:, 2 * head_dim :].astype(
                jnp.bfloat16
            )
            at += size
        part = pl.ds(base, at)
        forth = remote(
            kv.at[1, :, part],
            kv.at[0, :, part],
            h_send.at[0, task],
            h_recv.at[0, task],
            (lax.rem(f + 1, segments), q),
        )
        back = remote(
            kv.at[1, :, part],
            kv.at[2, :, part],
            h_send.at[1, task],
            h_recv.at[1, task],
            (lax.rem(f + segments - 1, segments), q),
        )

        @pl.when(f < last)
        def _():
            forth.start()

        @pl.when(f > 0)
        def _():
            back.start()

        halo.append((forth, back))

    cols = width // OUT_CHUNKS
    mirror_w = []

    def send_weights(i):
        part = pl.ds(i * cols, cols)
        copy = remote(
            out_w.at[0, :, part],
            out_w.at[2, :, part],
            w_send.at[i],
            w_recv.at[i],
            (f, peers[2]),
        )
        copy.start()
        mirror_w.append(copy)

    sibling_w = remote(
        out_w.at[0], out_w.at[1], w_send.at[OUT_CHUNKS], w_recv.at[OUT_CHUNKS], (f, peers[1])
    )
    counted = (
        jnp.where(f > 0, 1.0, 0.0).astype(jnp.float32),
        jnp.float32(1.0),
        jnp.where(f < last, 1.0, 0.0).astype(jnp.float32),
    )

    def wait_halo(task):
        forth, back = halo[task]
        begin = (0, 2 * rows, 3 * rows)[task]
        size = (2 * rows, rows, rows)[task]
        part = slice(begin, begin + size)

        @pl.when(f > 0)
        def _():
            forth.wait_recv()

        @pl.when(f < last)
        def _():
            back.wait_recv()

        for edge, side in ((0, 0), (last, 2)):

            @pl.when(f == edge)
            def _(side=side):
                kv[side, 0, part, :] = kv[1, 0, part, :]
                kv[side, 1, part, :] = jnp.zeros((size, head_dim), jnp.bfloat16)

    def attend_to(block, begin, size):
        own = queries[block * rows : (block + 1) * rows, :]
        scores = [
            lax.dot_general(
                own,
                kv[side, 0, begin : begin + size, :],
                (((1,), (1,)), ((), ())),
                preferred_element_type=jnp.float32,
            )
            for side in range(3)
        ]
        top = jnp.max(
            jnp.maximum(jnp.maximum(scores[0], scores[2]), scores[1]), axis=1, keepdims=True
        )
        return scores, top

    def mix(scores, top, begin, size):
        weight = jnp.zeros((rows, 1), jnp.float32)
        mixed = jnp.zeros((rows, head_dim), jnp.float32)
        for side in range(3):
            raised = jnp.exp2(scores[side] - top)
            weight = weight + counted[side] * jnp.sum(raised, axis=1, keepdims=True)
            mixed = mixed + jnp.dot(
                raised.astype(jnp.bfloat16),
                kv[side, 1, begin : begin + size, :],
                preferred_element_type=jnp.float32,
            )
        return weight, mixed

    early = 3 * rows

    def attend_early(block):
        part = slice(block * rows, (block + 1) * rows)
        scores, top = attend_to(block, 0, early)
        weight, mixed = mix(scores, top, 0, early)
        ranges[0, part, :] = jnp.broadcast_to(top, (rows, head_dim))
        ranges[1, part, :] = jnp.broadcast_to(weight, (rows, head_dim))
        mixes[part, :] = mixed

    def attend_late(block):
        part = slice(block * rows, (block + 1) * rows)
        scores, late_top = attend_to(block, early, rows)
        early_top = ranges[0, part, :]
        top = jnp.maximum(early_top, late_top)
        weight, mixed = mix(scores, top[:, :1], early, rows)
        keep = jnp.exp2(early_top - top)
        weight = weight + ranges[1, part, :] * keep
        return ((mixed + mixes[part, :] * keep) / weight).astype(jnp.bfloat16)

    project([(0, 0, rows), (1, 0, rows)], 0)
    half = rows // 2
    forward_tokens(2)
    for i in range(2):
        forwards[i].wait_recv()
        norm_piece(2, i * piece, piece, i * piece)
        norm_piece(3, i * piece, piece, half + i * piece)
    project([(2, 0, half), (3, 0, half)], 1)
    norm_piece(2, half, piece, 0)
    forwards[2].wait_recv()
    norm_piece(3, half, piece, half)
    forward_tokens(3)
    for i in range(4):
        send_weights(i)
    norm_piece(2, half + piece, piece, piece)
    forwards[3].wait_recv()
    norm_piece(3, half + piece, piece, half + piece)
    project([(2, half, half), (3, half, half)], 2)
    send_weights(4)
    sibling_w.start()
    wait_halo(0)
    wait_halo(1)
    for block in range(PEERS):
        attend_early(block)
    send_weights(5)
    wait_halo(2)
    att_copies = []
    both = [attend_late(2), attend_late(3)]
    for rel in (3, 2, 1):
        if rel == 1:
            own_att[1] = attend_late(1)
        else:
            part = slice((rel - 2) * half, (rel - 1) * half)
            own_att[rel, :half, :] = both[0][part]
            own_att[rel, half:, :] = both[1][part]
        copy = remote(own_att.at[rel], att.at[rel], a_send.at[rel], a_recv.at[rel], (f, peers[rel]))
        copy.start()
        att_copies.append(copy)
    for i in range(6, OUT_CHUNKS):
        send_weights(i)
    att[0] = attend_late(0)

    forward_w = []

    def forward_weights(i):
        mirror_w[i].wait_recv()
        part = pl.ds(i * cols, cols)
        copy = remote(
            out_w.at[2, :, part],
            out_w.at[3, :, part],
            w_send.at[OUT_CHUNKS + 1 + i],
            w_recv.at[OUT_CHUNKS + 1 + i],
            (f, peers[1]),
        )
        copy.start()
        forward_w.append(copy)

    forward_weights(0)
    sibling_w.wait_recv()
    for copy in att_copies:
        copy.wait_recv()
    mixed = jnp.concatenate([att[rel] for rel in range(PEERS)], axis=1)

    clean_cols = width // segments
    shifts = []
    cleans = []
    for i in range(OUT_CHUNKS):
        if i + 1 < OUT_CHUNKS:
            forward_weights(i + 1)
        forward_w[i].wait_recv()
        begin = i * cols
        part = pl.ds(begin, cols)
        projected = jnp.dot(
            mixed,
            out_w[:, :, begin : begin + cols].reshape(PEERS * rows, cols),
            preferred_element_type=jnp.float32,
        )
        gate = mod_rows[:, 2 * width + begin : 2 * width + begin + cols]
        gated = (projected.reshape(rows // 8, 8, cols) * gate).reshape(rows, cols)
        before = kept[:, begin : begin + cols].astype(jnp.float32)
        done[:, begin : begin + cols] = (before + gated).astype(jnp.bfloat16)
        shift = remote(
            done.at[:, part],
            arrived.at[:, part],
            s_send.at[i],
            s_recv.at[i],
            (lax.rem(f + 1, segments), q),
        )
        shifts.append(shift)

        @pl.when(f < last)
        def _(shift=shift):
            shift.start()

        for to in range(begin // clean_cols, (begin + cols) // clean_cols):
            from_cols = done.at[:, pl.ds(to * clean_cols, clean_cols)]
            if to < last:
                clean_copy = remote(from_cols, clean, c_send.at[to], c_recv, (to, q))
            else:
                clean_copy = pltpu.make_async_copy(from_cols, clean, c_send.at[to])
            cleans.append(clean_copy)

            @pl.when(f == last)
            def _(clean_copy=clean_copy):
                clean_copy.start()

    for copy in mirror_x + [sibling_x] + forwards + mirror_w + [sibling_w] + forward_w + att_copies:
        copy.wait_send()
    for forth, back in halo:

        @pl.when(f < last)
        def _(forth=forth):
            forth.wait_send()

        @pl.when(f > 0)
        def _(back=back):
            back.wait_send()

    @pl.when(f == 0)
    def _():
        fresh_copy.wait()

    written = []
    for i, shift in enumerate(shifts):

        @pl.when(f > 0)
        def _(shift=shift):
            shift.wait_recv()

        part = pl.ds(i * cols, cols)
        copy = pltpu.make_async_copy(
            arrived.at[:, part], queue_next.at[:, part], out_sem.at[i]
        )
        copy.start()
        written.append(copy)
    for copy in written:
        copy.wait()
    for shift in shifts:

        @pl.when(f < last)
        def _(shift=shift):
            shift.wait_send()

    @pl.when(f == last)
    def _():
        for clean_copy in cleans[:-1]:
            clean_copy.wait_send()
        cleans[-1].wait()

    @pl.when(f < last)
    def _():
        cleans[0].wait_recv()


def hand_over(queue_in, clean_in, queue_next, clean, queue_held, clean_held, sem_in, sem_out):
    piece = queue_in.shape[0] // X_CHUNKS
    steps = []
    for i in range(X_CHUNKS):
        part = pl.ds(i * piece, piece)
        steps.append((queue_in.at[part], queue_held.at[part], queue_next.at[part]))
    steps.append((clean_in, clean_held, clean))
    reads = []
    for i, (source, held, _) in enumerate(steps):
        copy = pltpu.make_async_copy(source, held, sem_in.at[i])
        copy.start()
        reads.append(copy)
    writes = []
    for i, (_, held, target) in enumerate(steps):
        reads[i].wait()
        copy = pltpu.make_async_copy(held, target, sem_out.at[i])
        copy.start()
        writes.append(copy)
    for copy in writes:
        copy.wait()


def fused(
    mesh, queue, fresh_noise, w_mod, w_qkv, w_out, q_gain, k_gain, levels, plan, positions
):
    segments = mesh.shape["segment"]
    rows, width = queue.shape[1:]
    mod_cols = w_mod.shape[2]
    head_dim = q_gain.shape[1]
    rope, *halves = rope_rows(head_dim)
    scalars = pl.BlockSpec(memory_space=pltpu.SMEM)
    outside = pl.BlockSpec(memory_space=pl.ANY)
    bf16, f32 = jnp.bfloat16, jnp.float32
    dma = pltpu.SemaphoreType.DMA
    queue_next, clean_frame = pl.pallas_call(
        functools.partial(block_kernel, segments, tuple(halves)),
        out_shape=(
            jax.ShapeDtypeStruct((rows, width), bf16),
            jax.ShapeDtypeStruct((rows, width // segments), bf16),
        ),
        in_specs=[outside] * 7 + [scalars] * 3 + [outside] * 2,
        out_specs=(outside, outside),
        scratch_shapes=[
            pltpu.VMEM((width, mod_cols), bf16),
            pltpu.VMEM((width, 3 * head_dim), bf16),
            pltpu.VMEM((PEERS, rows, width), bf16),
            pltpu.VMEM((PEERS, rows, width), bf16),
            pltpu.VMEM((PEERS, 1, mod_cols), f32),
            pltpu.VMEM((8, 3 * width), f32),
            pltpu.VMEM((1, width // 2), f32),
            pltpu.VMEM((8, head_dim), f32),
            pltpu.VMEM((1, head_dim), f32),
            pltpu.VMEM((1, head_dim), f32),
            pltpu.VMEM((width, LANES), f32),
            pltpu.VMEM((rows, width), bf16),
            pltpu.VMEM((2 * rows, width), bf16),
            pltpu.VMEM((PEERS, rows, head_dim), f32),
            pltpu.VMEM((PEERS, rows, head_dim), f32),
            pltpu.VMEM((PEERS * rows, head_dim), bf16),
            pltpu.VMEM((3, 2, PEERS * rows, head_dim), bf16),
            pltpu.VMEM((2, PEERS * rows, head_dim), f32),
            pltpu.VMEM((PEERS * rows, head_dim), f32),
            pltpu.VMEM((PEERS, rows, head_dim), bf16),
            pltpu.VMEM((PEERS, rows, head_dim), bf16),
            pltpu.VMEM((rows, width), bf16),
            pltpu.VMEM((rows, width), bf16),
            dma((4,)),
            dma((4 + MOD_CHUNKS,)),
            dma((2 * X_CHUNKS + 1,)),
            dma((2 * X_CHUNKS + 1,)),
            dma((PEERS,)),
            dma((PEERS,)),
            dma((2, 3)),
            dma((2, 3)),
            dma((2 * OUT_CHUNKS + 1,)),
            dma((2 * OUT_CHUNKS + 1,)),
            dma((PEERS,)),
            dma((PEERS,)),
            dma((OUT_CHUNKS,)),
            dma((OUT_CHUNKS,)),
            dma((segments,)),
            dma(()),
            dma((OUT_CHUNKS,)),
        ],
        compiler_params=pltpu.CompilerParams(
            collective_id=0, has_side_effects=True, vmem_limit_bytes=56 * 1024 * 1024
        ),
        cost_estimate=pl.CostEstimate(
            flops=2 * 10**9, bytes_accessed=22 * 10**6, transcendentals=10**6
        ),
        name="relayed_block",
    )(
        queue[0],
        fresh_noise,
        w_mod[0],
        w_qkv.reshape(width, 3 * head_dim),
        w_out[0],
        q_gain,
        k_gain,
        levels,
        plan,
        positions,
        jnp.asarray(time_rates(width)),
        jnp.asarray(rope),
    )
    queue_next, clean_frame = pl.pallas_call(
        hand_over,
        out_shape=(
            jax.ShapeDtypeStruct(queue_next.shape, bf16),
            jax.ShapeDtypeStruct(clean_frame.shape, bf16),
        ),
        in_specs=[outside] * 2,
        out_specs=(outside, outside),
        scratch_shapes=[
            pltpu.VMEM(queue_next.shape, bf16),
            pltpu.VMEM(clean_frame.shape, bf16),
            dma((X_CHUNKS + 1,)),
            dma((X_CHUNKS + 1,)),
        ],
        compiler_params=pltpu.CompilerParams(vmem_limit_bytes=56 * 1024 * 1024),
        name="hand_over",
    )(queue_next, clean_frame)
    return queue_next[None], clean_frame


def solution(mesh):
    placed = (
        P("segment", "seq", None),
        P("seq", None),
        P("segment", None, "seq"),
        P("segment", None, "seq", None),
        P("segment", "seq", None),
        P("segment", None),
        P("segment", None),
        P("segment"),
        P(),
        P("segment"),
    )
    return jax.shard_map(
        functools.partial(fused, mesh) if fits(mesh) else shards,
        mesh=mesh,
        in_specs=placed,
        out_specs=(P("segment", "seq", None), P("seq", "segment")),
        check_vma=False,
    )
```
